32 devices in a mesh: blk: 16 (over z, y, x), tp: 2 (over core).
Axes of the slice: x: 2, y: 2, z: 4, core: 2. Of those that a mesh axis runs over, the one named last changes fastest.
Arguments:
- q_tokens: int32 [64, 64], P('blk'), may hold values from 0 to 30521
- p_tokens: int32 [128, 256], P('blk'), may hold values from 0 to 30521
- q_lengths: int32 [64], P('blk'), may hold values from 8 to 64, as said below
- p_lengths: int32 [128], P('blk'), may hold values from 64 to 256, as said below
- positive: int32 [64], P('blk'), may hold values from -1 to 127, as said below
- table: float32 [31104, 768], P('blk', 'tp'), may hold values from -6 to 6
- table_moment: float32 [31104, 768], P('blk', 'tp')
- table_second: float32 [31104, 768], P('blk', 'tp'), as said below
- blocks: float32 [2, 192, 192, 192], P('tp', 'blk')
- left_stats: float32 [2, 192, 192, 192], P('tp', 'blk'), as said below
- right_stats: float32 [2, 192, 192, 192], P('tp', 'blk'), as said below
- left_roots: float32 [2, 192, 192, 192], P('tp', 'blk'), as said below
- right_roots: float32 [2, 192, 192, 192], P('tp', 'blk'), as said below
- vectors: float32 [2, 2, 2304], P('tp', None, 'blk'), may hold values from -1.8 to 1.8
- vector_moment: float32 [2, 2, 2304], P('tp', None, 'blk')
- vector_second: float32 [2, 2, 2304], P('tp', None, 'blk'), as said below
- shared: float32 [14, 768], P(None, 'blk')
- shared_moment: float32 [14, 768], P(None, 'blk')
- shared_second: float32 [14, 768], P(None, 'blk'), as said below
Outputs:
- loss_sum: float32 [], replicated
- positives_count: float32 [], replicated
- grad_norm: float32 [], replicated
- block_grads: float32 [2, 192, 192, 192], P('tp', 'blk')
- left_new: float32 [2, 192, 192, 192], P('tp', 'blk')
- right_new: float32 [2, 192, 192, 192], P('tp', 'blk')
- blocks_new: float32 [2, 192, 192, 192], P('tp', 'blk')
- table_moment_new: float32 [31104, 768], P('blk', 'tp')
- table_second_new: float32 [31104, 768], P('blk', 'tp')
- table_new: float32 [31104, 768], P('blk', 'tp')
- vector_moment_new: float32 [2, 2, 2304], P('tp', None, 'blk')
- vector_second_new: float32 [2, 2, 2304], P('tp', None, 'blk')
- vectors_new: float32 [2, 2, 2304], P('tp', None, 'blk')
- shared_moment_new: float32 [14, 768], P(None, 'blk')
- shared_second_new: float32 [14, 768], P(None, 'blk')
- shared_new: float32 [14, 768], P(None, 'blk')
The draws below stay inside these ranges and needn't reach their ends.
Inputs may be any that keep to these rules, and one draw needn't show every extreme that they name: `q_lengths`: one question in every draw has length 64. `p_lengths`: one passage in every draw has length 256. -1 means that the question has no positive; the last question of every aligned 4 has one. `left_stats`: symmetric. `right_stats`: symmetric. `left_roots`: symmetric. `right_roots`: symmetric. `table_second`: positive. `vector_second`: positive. `shared_second`: positive.
All inputs are finite; a program needn't handle non-finite values.
Results may differ from the reference program's by a relative error of at most 0.017.
The reference program's roundings to bfloat16 on the way count: a program that leaves them out, or rounds other values in their place, can miss the bound.
Values may be sent and summed in bfloat16 or wider, within the bound.
No kernel may reach another device: no remote copies, remote signals or barrier semaphores. Data moves between devices by JAX's collectives and lax.ppermute only.
A program may use at most 320 MiB of HBM per device.

```python
import math
import jax
import jax.numpy as jnp
import numpy as np
from jax import lax

MODEL_WIDTH = 768
HD = 64
FF = 3072
VOCAB = 30522
TABLE_ROWS = 31104
LQ = 64
LP = 256
LAYERS = 2
STEP = 10
QDEV = 4
BLOCK = 192
NBLK = 192
NQ = 64
NP = 128


CLIP = 0.05


BETA_ONE = 0.9


BETA_TWO = 0.999


STAT_DECAY = 0.95


TABLE_SCALE = 0.1


def grad_size():
    params = TABLE_ROWS * MODEL_WIDTH + 2 * NBLK * BLOCK * BLOCK + 2 * LAYERS * (MODEL_WIDTH + FF // 2) + 14 * MODEL_WIDTH
    return CLIP / params ** 0.5


def ragged(key, count, length, shortest):
    first, second = jax.random.split(key)
    values = jax.random.randint(first, (count,), shortest, length + 1)
    chosen = jax.random.randint(second, (), 0, count)
    return jnp.where(jnp.arange(count) == chosen, length, values).astype(jnp.int32)


def draw_q_lengths(key, part):
    key = jax.random.fold_in(key, 1)
    return ragged(key, NQ, LQ, max(LQ // 8, 1))


def draw_p_lengths(key, part):
    key = jax.random.fold_in(key, 2)
    return ragged(key, NP, LP, LP // 4)


def draw_positive(key, part):
    key = jax.random.fold_in(key, 3)
    first, second = jax.random.split(key)
    index = jnp.arange(NQ)
    groups = max(NQ // QDEV - 1, 1)
    chance = 300 + 600 * (index // QDEV) // groups
    keep = (jax.random.randint(first, (NQ,), 0, 1000) < chance) | (index % QDEV == QDEV - 1)
    target = jax.random.randint(second, (NQ,), 0, NP)
    return jnp.where(keep, target, -1).astype(jnp.int32)


def draw_blocks(key, part):
    key = jax.random.fold_in(key, 4)
    per_layer = NBLK // LAYERS
    index = jnp.arange(NBLK) % per_layer
    model_rows = MODEL_WIDTH // BLOCK
    first = model_rows * (3 * MODEL_WIDTH // (2 * BLOCK))
    second = first + MODEL_WIDTH // (2 * BLOCK) * model_rows
    third = second + model_rows * (FF // (2 * BLOCK))
    scales = jnp.where(index < first, MODEL_WIDTH ** (-0.5), jnp.where(index < second, 4.0 * MODEL_WIDTH ** (-0.5), jnp.where(index < third, MODEL_WIDTH ** (-0.5), 1.5 * FF ** (-0.5))))
    return jax.random.normal(key, (2, NBLK, BLOCK, BLOCK), jnp.float32) * scales[None, :, None, None]


def symmetric(key, diagonal_scale, noise_scale):
    first, second = jax.random.split(key)
    noise = jax.random.normal(second, (2, NBLK, BLOCK, BLOCK), jnp.float32)
    noise = (noise + jnp.swapaxes(noise, -1, -2)) * noise_scale
    identity = (jnp.arange(BLOCK)[:, None] == jnp.arange(BLOCK)[None, :]).astype(jnp.float32)
    return diagonal_scale(first)[..., None] * identity + noise * (1.0 - identity)


def statistics(key):
    size = (1.0 - STAT_DECAY) / STAT_DECAY * BLOCK * grad_size() ** 2

    def diagonal(inner):
        return jax.random.uniform(inner, (2, NBLK, BLOCK), jnp.float32, 1.0, 4.0) * size
    return symmetric(key, diagonal, 0.05 * size * BLOCK ** (-0.5))


def roots(key):
    base = (BLOCK * grad_size() ** 2) ** (-0.25)

    def diagonal(inner):
        return jnp.exp(jax.random.uniform(inner, (2, NBLK, BLOCK), jnp.float32, -0.6931, 0.6931)) * base
    return symmetric(key, diagonal, 0.35 * base * BLOCK ** (-0.5))


def draw_left_stats(key, part):
    key = jax.random.fold_in(key, 5)
    return statistics(key)


def draw_right_stats(key, part):
    key = jax.random.fold_in(key, 6)
    return statistics(key)


def draw_left_roots(key, part):
    key = jax.random.fold_in(key, 7)
    return roots(key)


def draw_right_roots(key, part):
    key = jax.random.fold_in(key, 8)
    return roots(key)


def draw_shared(key, part):
    key = jax.random.fold_in(key, 9)
    first, second = jax.random.split(key)
    rows = jnp.arange(14)
    gain_row = (rows == 0) | (rows >= 2) & (((rows - 2) % 6 == 1) | ((rows - 2) % 6 == 4))
    rising = 0.5 + jnp.arange(MODEL_WIDTH).astype(jnp.float32) / MODEL_WIDTH
    gains = rising[None, :] * jax.random.uniform(first, (14, MODEL_WIDTH), jnp.float32, 0.8, 1.25)
    shifts = jax.random.normal(second, (14, MODEL_WIDTH), jnp.float32) * 0.3
    return jnp.where(gain_row[:, None], gains, shifts)


def first_moment(key, shape, size):
    return jax.random.normal(key, shape, jnp.float32) * ((1.0 - BETA_ONE) / BETA_ONE * size)


def second_moment(key, shape, size):
    return jax.random.uniform(key, shape, jnp.float32, 1.0, 4.0) * ((1.0 - BETA_TWO) / BETA_TWO * size * size)


def draw_table_moment(key, part):
    key = jax.random.fold_in(key, 10)
    return first_moment(key, (TABLE_ROWS, MODEL_WIDTH), TABLE_SCALE * grad_size())


def draw_table_second(key, part):
    key = jax.random.fold_in(key, 11)
    return second_moment(key, (TABLE_ROWS, MODEL_WIDTH), TABLE_SCALE * grad_size())


def draw_vector_moment(key, part):
    key = jax.random.fold_in(key, 12)
    return first_moment(key, (2, LAYERS, MODEL_WIDTH + FF // 2), 4.0 * grad_size())


def draw_vector_second(key, part):
    key = jax.random.fold_in(key, 13)
    return second_moment(key, (2, LAYERS, MODEL_WIDTH + FF // 2), 4.0 * grad_size())


def draw_shared_moment(key, part):
    key = jax.random.fold_in(key, 14)
    return first_moment(key, (14, MODEL_WIDTH), 4.0 * grad_size())


def draw_shared_second(key, part):
    key = jax.random.fold_in(key, 15)
    return second_moment(key, (14, MODEL_WIDTH), 4.0 * grad_size())


def touch_ends(array, own_key, low, top_value):
    dims = array.shape
    place = [jax.random.randint(jax.random.fold_in(own_key, axis), (), 0, dims[axis]) for axis in range(len(dims))]
    array = array.at[tuple(place)].set(low)
    longest = dims.index(max(dims))
    place[longest] = (place[longest] + 1) % dims[longest]
    return array.at[tuple(place)].set(top_value)


def level_of(own_key, shape, cuts, least, top_value):
    def one(axis_at, blocks):
        heights = jax.random.uniform(jax.random.fold_in(jax.random.fold_in(own_key, 6), axis_at), (blocks,), jnp.float32, least / len(cuts), top_value / len(cuts))
        return jnp.repeat(jnp.exp(heights), shape[axis_at] // blocks).reshape((-1,) + (1,) * (len(shape) - axis_at - 1))

    factor_of = one(*cuts[0])
    for cut in cuts[1:]:
        factor_of = factor_of * one(*cut)
    return factor_of


def rank_table(count, slope):
    weights = [(1 << 20) // math.isqrt(rank ** slope) + 1 for rank in range(1, count + 1)]
    scale = 1 + sum(weights) // (1 << 30)
    return np.cumsum(np.array([max(1, weight // scale) for weight in weights]))


def ranked(key, dims, amount, lean):
    table = rank_table(amount, lean)
    ticket = jax.random.randint(jax.random.fold_in(key, 1), dims, 0, int(table[amount - 1]))
    grade = jnp.searchsorted(jnp.asarray(table, jnp.int32), ticket, side="right")
    return jax.random.permutation(jax.random.fold_in(key, 2), amount)[grade].astype(jnp.int32)


def gaussian(rng, shape, deviation, bound, cuts=(), held_as=jnp.bfloat16):
    result = deviation * jax.random.normal(rng, shape, jnp.float32)
    if cuts:
        result = result * level_of(rng, shape, cuts, -0.22, 0.18)
    return jnp.clip(result, -bound, bound).astype(held_as)


def setup_inputs(seed: int = 0) -> dict:
    streams_of = jax.random.split(jax.random.key(seed), 20)
    return {
        "q_tokens": touch_ends(ranked(streams_of[0], (NQ, LQ), VOCAB, 2), jax.random.fold_in(streams_of[0], 3), 0, VOCAB - 1).astype(jnp.int32),
        "p_tokens": touch_ends(ranked(streams_of[1], (NP, LP), VOCAB, 2), jax.random.fold_in(streams_of[1], 3), 0, VOCAB - 1).astype(jnp.int32),
        "q_lengths": draw_q_lengths(jax.random.fold_in(streams_of[19], 71), 0),
        "p_lengths": draw_p_lengths(jax.random.fold_in(streams_of[19], 71), 0),
        "positive": draw_positive(jax.random.fold_in(streams_of[19], 71), 0),
        "table": gaussian(streams_of[5], (TABLE_ROWS, MODEL_WIDTH), 1.0, 6.0, ((0, 16), (1, 2)), jnp.float32),
        "table_moment": draw_table_moment(jax.random.fold_in(streams_of[19], 71), 0),
        "table_second": draw_table_second(jax.random.fold_in(streams_of[19], 71), 0),
        "blocks": draw_blocks(jax.random.fold_in(streams_of[19], 71), 0),
        "left_stats": draw_left_stats(jax.random.fold_in(streams_of[19], 71), 0),
        "right_stats": draw_right_stats(jax.random.fold_in(streams_of[19], 71), 0),
        "left_roots": draw_left_roots(jax.random.fold_in(streams_of[19], 71), 0),
        "right_roots": draw_right_roots(jax.random.fold_in(streams_of[19], 71), 0),
        "vectors": gaussian(streams_of[13], (2, LAYERS, MODEL_WIDTH + FF // 2), 0.3, 1.8, ((0, 2), (2, 16)), jnp.float32),
        "vector_moment": draw_vector_moment(jax.random.fold_in(streams_of[19], 71), 0),
        "vector_second": draw_vector_second(jax.random.fold_in(streams_of[19], 71), 0),
        "shared": draw_shared(jax.random.fold_in(streams_of[19], 71), 0),
        "shared_moment": draw_shared_moment(jax.random.fold_in(streams_of[19], 71), 0),
        "shared_second": draw_shared_second(jax.random.fold_in(streams_of[19], 71), 0),
    }


CLIP = 0.05
BETA_ONE = 0.9
BETA_TWO = 0.999
STAT_DECAY = 0.95
ADAM_RATE = 0.5
SHAMPOO_RATE = 0.5
WEIGHT_DECAY = 0.01
ADAM_EPS = 1e-08
NORM_EPS = 1e-06
PRECISION_MAX = lax.Precision.HIGHEST

@jax.custom_vjp
def lower_rows(v):
    return lax.optimization_barrier(v.astype(jnp.bfloat16)).astype(jnp.float32)

@jax.custom_vjp
def lower_rows_restored(v):
    return v

def low_keep(v):
    return (lower_rows(v), None)

def low_pass(kept, grad):
    return (grad,)

def back_keep(v):
    return (v, None)

def back_low(kept, grad):
    return (lower_rows(grad),)
lower_rows.defvjp(low_keep, low_pass)
lower_rows_restored.defvjp(back_keep, back_low)

def grid(blocks, rows, columns):
    side = blocks.shape[-1]
    return blocks.reshape(rows, columns, side, side).transpose(0, 2, 1, 3).reshape(rows * side, columns * side)

def block_counts(side):
    return (MODEL_WIDTH // side, MODEL_WIDTH // (2 * side), 3 * MODEL_WIDTH // (2 * side), FF // (2 * side))

def layer_mats(half_width):
    model_rows, half_rows, joint_columns, inner_columns = block_counts(half_width.shape[-1])
    first = model_rows * joint_columns
    second = first + half_rows * model_rows
    third = second + model_rows * inner_columns
    fourth = third + inner_columns * model_rows
    return (grid(half_width[:first], model_rows, joint_columns), grid(half_width[first:second], half_rows, model_rows), grid(half_width[second:third], model_rows, inner_columns), grid(half_width[third:fourth], inner_columns, model_rows))

def layer_norm(value, gain, shift):
    centred = value - lax.optimization_barrier(jnp.mean(value, axis=-1, keepdims=True))
    spread = lax.optimization_barrier(jnp.mean(centred * centred, axis=-1, keepdims=True))
    return centred * lax.rsqrt(spread + NORM_EPS) * gain + shift

def encode(tokens, lengths, table, halves, vectors, shared, layer_params):
    count, length = tokens.shape
    places = jnp.arange(length)
    state = layer_norm(table[tokens] + table[VOCAB + places][None], shared[0], shared[1])
    params = shared[2 + 6 * layer_params:8 + 6 * layer_params]
    live = places[None, :] < lengths[:, None]
    width = MODEL_WIDTH // 2
    layer_input_rows = lower_rows(state)
    attention_output = jnp.zeros_like(state)
    for half_width in range(2):
        joint_weight, output_weight, up_weight, down_weight = halves[half_width]
        bias = vectors[half_width, layer_params]
        joint_projection = jnp.einsum('ypz,za->ypa', layer_input_rows, joint_weight, precision=PRECISION_MAX)
        shifts = jnp.concatenate([bias[:width], jnp.zeros((width,), jnp.float32), bias[width:2 * width]])
        joint_projection = lower_rows(lower_rows_restored(joint_projection + shifts))
        query = joint_projection[..., :width].reshape(count, length, -1, HD)
        key = joint_projection[..., width:2 * width].reshape(count, length, -1, HD)
        value = joint_projection[..., 2 * width:].reshape(count, length, -1, HD)
        scores = lower_rows_restored(jnp.einsum('sqhd,skhd->shqk', query, key, precision=PRECISION_MAX) * HD ** (-0.5))
        weights = lower_rows(jax.nn.softmax(jnp.where(live[:, None, None, :], scores, -1e+30), axis=-1))
        context_vectors = jnp.einsum('shqk,skhd->sqhd', weights, value, precision=PRECISION_MAX).reshape(count, length, width)
        attention_output = attention_output + jnp.einsum('guc,ch->guh', lower_rows(lower_rows_restored(context_vectors)), output_weight, precision=PRECISION_MAX)
    hidden = layer_norm(state + lower_rows_restored(attention_output) + params[0], params[1], params[2])
    upper_rows = lower_rows(hidden)
    projected_down = jnp.zeros_like(state)
    for half_width in range(2):
        joint_weight, output_weight, up_weight, down_weight = halves[half_width]
        projected_up = lower_rows_restored(jnp.einsum('xqj,jb->xqb', upper_rows, up_weight, precision=PRECISION_MAX) + vectors[half_width, layer_params, MODEL_WIDTH:])
        activated_hidden = lower_rows(jax.nn.gelu(projected_up, approximate=False))
        projected_down = projected_down + jnp.einsum('meo,oq->meq', activated_hidden, down_weight, precision=PRECISION_MAX)
    output = layer_norm(hidden + lower_rows_restored(projected_down) + params[3], params[4], params[5])
    live_rows = live.astype(jnp.float32)
    return lax.optimization_barrier(jnp.sum(output * live_rows[..., None], axis=1)) / lengths[:, None].astype(jnp.float32)

def loss_terms(dense, binary, positive):
    columns = jnp.arange(dense.shape[1])
    hit = (columns[None, :] == positive[:, None]).astype(jnp.float32)
    valid = (positive >= 0).astype(jnp.float32)
    cross = jax.nn.logsumexp(dense, axis=1) - lax.optimization_barrier(jnp.sum(hit * dense, axis=1))
    anchor = lax.optimization_barrier(jnp.sum(hit * binary, axis=1))
    ranking = lax.optimization_barrier(jnp.sum((1.0 - hit) * jax.nn.softplus(1.0 - anchor[:, None] + binary), axis=1)) / (dense.shape[1] - 1)
    return (jnp.sum(valid * (cross + ranking)), jnp.sum(valid))

def adamw(weight, moment, second, grad):
    moment = BETA_ONE * moment + (1.0 - BETA_ONE) * grad
    second = BETA_TWO * second + (1.0 - BETA_TWO) * grad * grad
    update = moment / (1.0 - BETA_ONE ** STEP) / (jnp.sqrt(second / (1.0 - BETA_TWO ** STEP)) + ADAM_EPS)
    return (moment, second, weight - ADAM_RATE * (update + WEIGHT_DECAY * weight))

def reference(q_tokens, p_tokens, q_lengths, p_lengths, positive, table, table_moment, table_second, blocks, left_stats, right_stats, left_roots, right_roots, vectors, vector_moment, vector_second, shared, shared_moment, shared_second):

    def forward(table_w, blocks_w, vectors_w, shared_w):
        table_b = lower_rows(table_w)
        blocks_b = lower_rows(blocks_w)
        vectors_b = lower_rows(vectors_w)
        shared_b = lower_rows(shared_w)
        per_layer = blocks_b.shape[1] // LAYERS
        halves = [[layer_mats(blocks_b[half_width, layer_params * per_layer:(layer_params + 1) * per_layer]) for half_width in range(2)] for layer_params in range(LAYERS)]
        asked = encode(q_tokens, q_lengths, table_b, halves[0], vectors_b, shared_b, 0)
        passages = encode(p_tokens, p_lengths, table_b, halves[1], vectors_b, shared_b, 1)
        codes = lower_rows(jnp.tanh(passages))
        scale = 2.0 * MODEL_WIDTH ** (-0.5)
        dense = jnp.dot(asked, codes.T, precision=PRECISION_MAX) * scale
        binary = jnp.dot(jnp.tanh(asked), codes.T, precision=PRECISION_MAX) * scale
        return loss_terms(dense, binary, positive)[0]
    loss_sum, pull = jax.vjp(forward, table, blocks, vectors, shared)
    grads = pull(jnp.ones((), jnp.float32))
    count = jnp.sum((positive >= 0).astype(jnp.float32))
    grads = [item / count for item in grads]
    grad_norm = jnp.sqrt(sum((jnp.sum(item * item) for item in grads)))
    factor = jnp.minimum(1.0, CLIP / grad_norm)
    table_grad, block_grads, vector_grad, shared_grad = [factor * item for item in grads]
    left_new = STAT_DECAY * left_stats + (1.0 - STAT_DECAY) * jnp.einsum('tnij,tnkj->tnik', block_grads, block_grads, precision=PRECISION_MAX)
    right_new = STAT_DECAY * right_stats + (1.0 - STAT_DECAY) * jnp.einsum('tnji,tnjk->tnik', block_grads, block_grads, precision=PRECISION_MAX)
    turned = jnp.einsum('tnij,tnjk->tnik', left_roots, jnp.einsum('tnij,tnjk->tnik', block_grads, right_roots, precision=PRECISION_MAX), precision=PRECISION_MAX)
    blocks_new = blocks - SHAMPOO_RATE * (turned + WEIGHT_DECAY * blocks)
    table_moment_new, table_second_new, table_new = adamw(table, table_moment, table_second, table_grad)
    vector_moment_new, vector_second_new, vectors_new = adamw(vectors, vector_moment, vector_second, vector_grad)
    shared_moment_new, shared_second_new, shared_new = adamw(shared, shared_moment, shared_second, shared_grad)
    return (loss_sum, count, grad_norm, block_grads, left_new, right_new, blocks_new, table_moment_new, table_second_new, table_new, vector_moment_new, vector_second_new, vectors_new, shared_moment_new, shared_second_new, shared_new)
```

```python
from functools import partial

import jax
import jax.numpy as jnp
from jax import lax
from jax.sharding import PartitionSpec as P

MODEL_WIDTH = 768
HD = 64
FF = 3072
VOCAB = 30522
LAYERS = 2
STEP = 10


CLIP = 0.05
BETA_ONE = 0.9
BETA_TWO = 0.999
STAT_DECAY = 0.95
ADAM_RATE = 0.5
SHAMPOO_RATE = 0.5
WEIGHT_DECAY = 0.01
ADAM_EPS = 1e-08
NORM_EPS = 1e-06
PRECISION_MAX = lax.Precision.HIGHEST


GROUP = 2
SLOTS = 96
LANES = 128


def pair_blocks(blocks):
    count, side = blocks.shape[0], blocks.shape[-1]
    return (
        blocks.reshape(count // GROUP, GROUP, side, side)
        .transpose(0, 2, 1, 3)
        .reshape(count // GROUP, side, GROUP * side)
    )


def split_pairs(groups):
    count, side = groups.shape[0], groups.shape[1]
    return (
        groups.reshape(count, side, GROUP, side)
        .transpose(0, 2, 1, 3)
        .reshape(count * GROUP, side, side)
    )


def grid(groups, rows, columns):
    side, wide = groups.shape[1:]
    return (
        groups.reshape(rows, columns, side, wide)
        .transpose(0, 2, 1, 3)
        .reshape(rows * side, columns * wide)
    )


def ungrid(matrix, side, wide):
    rows, columns = matrix.shape[0] // side, matrix.shape[1] // wide
    return (
        matrix.reshape(rows, side, columns, wide)
        .transpose(0, 2, 1, 3)
        .reshape(rows * columns, side, wide)
    )


def group_counts(side):
    wide = GROUP * side
    half = MODEL_WIDTH // 2
    return (
        (MODEL_WIDTH // side, 3 * half // wide),
        (half // side, MODEL_WIDTH // wide),
        (MODEL_WIDTH // side, FF // 2 // wide),
        (FF // 2 // side, MODEL_WIDTH // wide),
    )


def layer_mats(groups):
    mats, start = [], 0
    for rows, columns in group_counts(groups.shape[1]):
        mats.append(grid(groups[start : start + rows * columns], rows, columns))
        start += rows * columns
    return mats


def layer_groups(mats, side):
    return jnp.concatenate([ungrid(mat, side, GROUP * side) for mat in mats], axis=0)


def other_core(value):
    return lax.ppermute(value, "tp", [(0, 1), (1, 0)])


def pair_sum(value):
    return value.astype(jnp.float32) + other_core(value).astype(jnp.float32)


def to_all(value, count):
    return lax.all_to_all(jnp.broadcast_to(value[None], (count,) + value.shape), "blk", 0, 0)


def slot_map(present):
    low = jnp.triu(jnp.ones((LANES, LANES), jnp.bfloat16))
    inner = jnp.einsum(
        "ohl,lm->ohm", present.astype(jnp.bfloat16), low, preferred_element_type=jnp.float32
    )
    totals = inner[..., -1]
    before = jnp.cumsum(totals, axis=1) - totals
    ranks = jnp.where(present, inner + before[..., None] - 1.0, -1.0)
    return ranks, jnp.sum(totals, axis=1)


def pick(slots, start):
    places = jnp.arange(SLOTS, dtype=jnp.float32) + start
    flat = slots.reshape(slots.shape[0], 1, -1)
    return (flat == places[None, :, None]).astype(jnp.bfloat16)


def layer_norm(value, gain, shift):
    centred = value - jnp.mean(value, axis=-1, keepdims=True)
    spread = jnp.mean(centred * centred, axis=-1, keepdims=True)
    return centred * lax.rsqrt(spread + NORM_EPS) * gain + shift


def residual_norm(state, branch, shift, gain, offset):
    return layer_norm(state + branch + shift, gain, offset)


def pool(output, lengths):
    live = (jnp.arange(output.shape[1])[None, :] < lengths[:, None]).astype(jnp.float32)
    return jnp.sum(output * live[..., None], axis=1) / lengths[:, None].astype(jnp.float32)


def loss_terms(dense, binary, positive):
    columns = jnp.arange(dense.shape[1])
    hit = (columns[None, :] == positive[:, None]).astype(jnp.float32)
    valid = (positive >= 0).astype(jnp.float32)
    cross = jax.nn.logsumexp(dense, axis=1) - jnp.sum(hit * dense, axis=1)
    anchor = jnp.sum(hit * binary, axis=1)
    ranking = jnp.sum((1.0 - hit) * jax.nn.softplus(1.0 - anchor[:, None] + binary), axis=1) / (
        dense.shape[1] - 1
    )
    return (jnp.sum(valid * (cross + ranking)), jnp.sum(valid))


def split_heads(joint_projection, width):
    count, length = (joint_projection.shape[0], joint_projection.shape[1])
    return [
        joint_projection[..., part * width : (part + 1) * width].reshape(count, length, -1, HD)
        for part in range(3)
    ]


def masked_scores(query, key, live):
    scores = jnp.einsum("sqhd,skhd->shqk", query, key, preferred_element_type=jnp.float32) * HD ** (
        -0.5
    )
    return jnp.where(live[:, None, None, :], scores, -1e30)


def layer_forward(state, lengths, mats, bias, params):
    joint_weight, output_weight, up_weight, down_weight = mats
    count, length = (state.shape[0], state.shape[1])
    width = output_weight.shape[0]
    live = jnp.arange(length)[None, :] < lengths[:, None]
    layer_input_rows = state.astype(jnp.bfloat16)
    joint_projection = jnp.einsum(
        "ypz,za->ypa", layer_input_rows, joint_weight, preferred_element_type=jnp.float32
    )
    shifts = jnp.concatenate(
        [bias[:width], jnp.zeros((width,), jnp.float32), bias[width : 2 * width]]
    )
    joint_projection = (joint_projection + shifts).astype(jnp.bfloat16)
    query, key, value = split_heads(joint_projection, width)
    scores = masked_scores(query, key, live)
    top = jnp.max(scores, axis=-1, keepdims=True)
    expo = jnp.exp(scores - top)
    total = jnp.sum(expo, axis=-1, keepdims=True)
    logsum = top + jnp.log(total)
    weights = (expo / total).astype(jnp.bfloat16)
    context_vectors = jnp.einsum(
        "shqk,skhd->sqhd", weights, value, preferred_element_type=jnp.float32
    )
    context_vectors = context_vectors.reshape(count, length, width).astype(jnp.bfloat16)
    attention_output = pair_sum(
        jnp.einsum(
            "guc,ch->guh", context_vectors, output_weight, preferred_element_type=jnp.float32
        ).astype(jnp.bfloat16)
    )
    hidden = residual_norm(state, attention_output, params[0], params[1], params[2])
    upper_rows = hidden.astype(jnp.bfloat16)
    projected_up = (
        jnp.einsum("xqj,jb->xqb", upper_rows, up_weight, preferred_element_type=jnp.float32)
        + bias[2 * width :]
    )
    activated_hidden = jax.nn.gelu(projected_up, approximate=False).astype(jnp.bfloat16)
    projected_down = pair_sum(
        jnp.einsum(
            "meo,oq->meq", activated_hidden, down_weight, preferred_element_type=jnp.float32
        ).astype(jnp.bfloat16)
    )
    output = residual_norm(hidden, projected_down, params[3], params[4], params[5])
    return (
        output,
        (
            layer_input_rows,
            joint_projection,
            logsum,
            context_vectors,
            attention_output,
            hidden,
            upper_rows,
            projected_up,
            activated_hidden,
            projected_down,
        ),
    )


def layer_backward(d_output, state, lengths, mats, params, kept):
    joint_weight, output_weight, up_weight, down_weight = mats
    (
        layer_input_rows,
        joint_projection,
        logsum,
        context_vectors,
        attention_output,
        hidden,
        upper_rows,
        projected_up,
        activated_hidden,
        projected_down,
    ) = kept
    count, length = (state.shape[0], state.shape[1])
    width = output_weight.shape[0]
    live = jnp.arange(length)[None, :] < lengths[:, None]
    tail_pull = jax.vjp(residual_norm, hidden, projected_down, params[3], params[4], params[5])[1]
    d_hidden, projected_down_gradient, d_shift_two, d_gain_two, d_offset_two = tail_pull(d_output)
    projected_down_gradient = projected_down_gradient.astype(jnp.bfloat16)
    down_weight_gradient = jnp.einsum(
        "nmq,nmb->qb", activated_hidden, projected_down_gradient, preferred_element_type=jnp.float32
    )
    activated_gradient = jnp.einsum(
        "jyx,vx->jyv", projected_down_gradient, down_weight, preferred_element_type=jnp.float32
    )
    gelu_pull = jax.vjp(partial(jax.nn.gelu, approximate=False), projected_up)[1]
    projected_up_gradient = gelu_pull(activated_gradient)[0].astype(jnp.bfloat16)
    up_weight_gradient = jnp.einsum(
        "iyv,iyg->vg", upper_rows, projected_up_gradient, preferred_element_type=jnp.float32
    )
    d_hidden = d_hidden + pair_sum(
        jnp.einsum(
            "auq,rq->aur", projected_up_gradient, up_weight, preferred_element_type=jnp.float32
        ).astype(jnp.bfloat16)
    )
    middle_pull = jax.vjp(residual_norm, state, attention_output, params[0], params[1], params[2])[
        1
    ]
    d_state, attention_output_gradient, d_shift_one, d_gain_one, d_offset_one = middle_pull(
        d_hidden
    )
    attention_output_gradient = attention_output_gradient.astype(jnp.bfloat16)
    output_weight_gradient = jnp.einsum(
        "hri,hrk->ik",
        context_vectors,
        attention_output_gradient,
        preferred_element_type=jnp.float32,
    )
    context_gradient = jnp.einsum(
        "oaq,jq->oaj", attention_output_gradient, output_weight, preferred_element_type=jnp.float32
    )
    context_gradient = context_gradient.astype(jnp.bfloat16).reshape(count, length, -1, HD)
    query, key, value = split_heads(joint_projection, width)
    weights = jnp.exp(masked_scores(query, key, live) - logsum)
    d_weights = jnp.einsum(
        "sqhd,skhd->shqk", context_gradient, value, preferred_element_type=jnp.float32
    )
    d_value = jnp.einsum(
        "shqk,sqhd->skhd",
        weights.astype(jnp.bfloat16),
        context_gradient,
        preferred_element_type=jnp.float32,
    )
    d_scores = weights * (d_weights - jnp.sum(weights * d_weights, axis=-1, keepdims=True))
    d_scores = d_scores.astype(jnp.bfloat16)
    d_query = jnp.einsum(
        "shqk,skhd->sqhd", d_scores, key, preferred_element_type=jnp.float32
    ) * HD ** (-0.5)
    d_key = jnp.einsum(
        "shqk,sqhd->skhd", d_scores, query, preferred_element_type=jnp.float32
    ) * HD ** (-0.5)
    joint_projection_gradient = jnp.concatenate(
        [part.reshape(count, length, width) for part in (d_query, d_key, d_value)], axis=-1
    )
    joint_projection_gradient = joint_projection_gradient.astype(jnp.bfloat16)
    joint_weight_gradient = jnp.einsum(
        "tha,thv->av",
        layer_input_rows,
        joint_projection_gradient,
        preferred_element_type=jnp.float32,
    )
    d_state = d_state + pair_sum(
        jnp.einsum(
            "yvt,nt->yvn",
            joint_projection_gradient,
            joint_weight,
            preferred_element_type=jnp.float32,
        ).astype(jnp.bfloat16)
    )
    mixed_sums = jnp.sum(joint_projection_gradient.astype(jnp.float32), axis=(0, 1))
    upward_sums = jnp.sum(projected_up_gradient.astype(jnp.float32), axis=(0, 1))
    grad_bias = jnp.concatenate([mixed_sums[:width], mixed_sums[2 * width :], upward_sums])
    grad_params = jnp.stack(
        [d_shift_one, d_gain_one, d_offset_one, d_shift_two, d_gain_two, d_offset_two]
    )
    return (
        d_state,
        (joint_weight_gradient, output_weight_gradient, up_weight_gradient, down_weight_gradient),
        grad_bias,
        grad_params,
    )


def adamw(weight, moment, second, grad):
    moment = BETA_ONE * moment + (1.0 - BETA_ONE) * grad
    second = BETA_TWO * second + (1.0 - BETA_TWO) * grad * grad
    update = (
        moment / (1.0 - BETA_ONE**STEP) / (jnp.sqrt(second / (1.0 - BETA_TWO**STEP)) + ADAM_EPS)
    )
    return (moment, second, weight - ADAM_RATE * (update + WEIGHT_DECAY * weight))


def on_device(
    q_tokens,
    p_tokens,
    q_lengths,
    p_lengths,
    positive,
    table,
    table_moment,
    table_second,
    blocks,
    left_stats,
    right_stats,
    left_roots,
    right_roots,
    vectors,
    vector_moment,
    vector_second,
    shared,
    shared_moment,
    shared_second,
):
    parts = lax.axis_size("blk")
    me, core = lax.axis_index("blk"), lax.axis_index("tp")
    bf16, f32 = jnp.bfloat16, jnp.float32
    rows_here, half = table.shape
    side = blocks.shape[-1]
    per_device = blocks.shape[1]
    even = per_device % GROUP == 0
    own_blocks = blocks[0].astype(bf16)
    if even:
        groups = lax.all_gather(pair_blocks(own_blocks), "blk", axis=0, tiled=True)
    else:
        groups = pair_blocks(lax.all_gather(own_blocks, "blk", axis=0, tiled=True))

    q_live = (jnp.arange(q_tokens.shape[1])[None, :] < q_lengths[:, None]).reshape(-1)
    p_live = (jnp.arange(p_tokens.shape[1])[None, :] < p_lengths[:, None]).reshape(-1)
    tokens = jnp.concatenate([q_tokens.reshape(-1), p_tokens.reshape(-1)])
    live = jnp.concatenate([q_live, p_live])
    tall = -(-rows_here // LANES)
    owner = tokens // rows_here
    inside = tokens - owner * rows_here
    high = jnp.where(live, owner * tall + inside // LANES, -1)
    high_hot = (high[:, None] == jnp.arange(parts * tall)[None, :]).astype(bf16)
    low_hot = (inside[:, None] % LANES == jnp.arange(LANES)[None, :]).astype(bf16)
    uses = jnp.einsum("th,tl->hl", high_hot, low_hot, preferred_element_type=f32)
    present = (uses > 0).reshape(parts, tall, LANES)
    slots, wanted = slot_map(present)
    token_slot = jnp.sum(
        jnp.dot(high_hot.astype(f32), slots.reshape(-1, LANES), precision=PRECISION_MAX) * low_hot,
        axis=1,
    )
    rounds_here = jnp.ceil(jnp.max(wanted) / SLOTS)

    small = jnp.concatenate(
        [
            vectors.astype(bf16).reshape(-1),
            shared.astype(bf16).reshape(-1),
            rounds_here.astype(bf16)[None],
        ]
    )
    small_size = -(-small.shape[0] // LANES) * LANES
    small = jnp.pad(small, (0, small_size - small.shape[0])).reshape(-1, LANES)
    asks = jnp.concatenate(
        [
            present.astype(bf16),
            jnp.broadcast_to(small[None], (parts,) + small.shape),
        ],
        axis=1,
    )
    asks = lax.all_to_all(asks, "blk", 0, 0)
    asked_slots, _ = slot_map(asks[:, :tall] > 0)
    small = asks[:, tall:].reshape(parts, -1)
    vector_part, shared_part = vectors.shape[2], shared.shape[1]
    vector_size, shared_size = vectors.size, shared.size
    bias_all = (
        small[:, :vector_size]
        .reshape(parts, LAYERS, vector_part)
        .transpose(1, 0, 2)
        .reshape(LAYERS, -1)
        .astype(f32)
    )
    params_all = (
        small[:, vector_size : vector_size + shared_size]
        .reshape(parts, -1, shared_part)
        .transpose(1, 0, 2)
        .reshape(-1, parts * shared_part)
        .astype(f32)
    )
    rounds = jnp.max(small[:, vector_size + shared_size].astype(f32)).astype(jnp.int32)

    table_low = jnp.pad(table.astype(bf16), ((0, tall * LANES - rows_here), (0, 0)))
    length = p_tokens.shape[1]
    q_length = q_tokens.shape[1]
    share = length // parts
    margin = jnp.zeros((length, half), bf16)
    first_place = jnp.clip(VOCAB - me * rows_here + length, 0, rows_here + length)
    places_here = lax.dynamic_slice_in_dim(
        jnp.concatenate([margin, table_low[:rows_here], margin]), first_place, length, 0
    )

    def choose(start):
        return pick(asked_slots, start)

    def serve(chosen):
        return jnp.einsum("sjr,rc->sjc", chosen, table_low, preferred_element_type=f32).astype(bf16)

    def spread(start):
        place = token_slot - start
        fits = (high >= 0) & (place >= 0) & (place < SLOTS)
        index = jnp.where(fits, owner * SLOTS + place.astype(jnp.int32), -1)
        return (index[:, None] == jnp.arange(parts * SLOTS)[None, :]).astype(bf16)

    sent = jnp.concatenate(
        [serve(choose(0.0)), places_here.reshape(parts, share, half)], axis=1
    )
    fetched = lax.all_to_all(sent, "blk", 0, 0)
    token_rows = jnp.dot(
        spread(0.0), fetched[:, :SLOTS].reshape(-1, half), preferred_element_type=f32
    ).astype(bf16)
    place_rows = to_all(jnp.sum(fetched[:, SLOTS:].astype(f32), axis=0).astype(bf16), parts)

    def fetch_more(carry):
        done, total = carry
        start = (done * SLOTS).astype(f32)
        more = lax.all_to_all(serve(choose(start)), "blk", 0, 0).reshape(-1, half)
        return done + 1, total + jnp.dot(spread(start), more, preferred_element_type=f32).astype(bf16)

    token_rows = lax.while_loop(lambda c: c[0] < rounds, fetch_more, (jnp.int32(1), token_rows))[1]
    halves = jnp.concatenate([token_rows, place_rows.reshape(length, half)])
    others = other_core(halves)
    full = jnp.where(
        core == 0,
        jnp.concatenate([halves, others], axis=1),
        jnp.concatenate([others, halves], axis=1),
    ).astype(f32)
    q_count = q_tokens.size
    place_full = full[tokens.shape[0] :]
    q_rows = full[:q_count].reshape(q_tokens.shape + (-1,)) + place_full[:q_length]
    p_rows = full[q_count : tokens.shape[0]].reshape(p_tokens.shape + (-1,)) + place_full

    per_layer = groups.shape[0] // LAYERS
    layer_weights = [
        layer_mats(groups[layer * per_layer : (layer + 1) * per_layer]) for layer in range(LAYERS)
    ]
    encoded = []
    for layer_params, rows, lengths in ((0, q_rows, q_lengths), (1, p_rows, p_lengths)):
        state, embed_pull = jax.vjp(layer_norm, rows, params_all[0], params_all[1])
        output, kept = layer_forward(
            state,
            lengths,
            layer_weights[layer_params],
            bias_all[layer_params],
            params_all[2 + 6 * layer_params : 8 + 6 * layer_params],
        )
        pooled, pool_pull = jax.vjp(partial(pool, lengths=lengths), output)
        encoded.append((state, lengths, kept, embed_pull, pool_pull, pooled))
    asked_local = encoded[0][5]
    codes_local = jnp.tanh(encoded[1][5])
    codes_low = codes_local.astype(bf16)
    every = to_all(
        jnp.concatenate(
            [
                asked_local,
                codes_low.astype(f32),
                jnp.pad(positive.astype(f32)[None], ((0, 0), (0, MODEL_WIDTH - positive.shape[0]))),
            ]
        ),
        parts,
    )
    q_part, p_part = asked_local.shape[0], codes_local.shape[0]
    asked = every[:, :q_part].reshape(-1, MODEL_WIDTH)
    codes = every[:, q_part : q_part + p_part].reshape(-1, MODEL_WIDTH)
    positives = every[:, q_part + p_part, :q_part].reshape(-1).astype(jnp.int32)
    hashed = jnp.tanh(asked)
    scale = 2.0 * MODEL_WIDTH ** (-0.5)
    dense = jnp.dot(asked, codes.T, precision=PRECISION_MAX) * scale
    binary = jnp.dot(hashed, codes.T, precision=PRECISION_MAX) * scale
    loss_sum, loss_pull = jax.vjp(
        lambda first, second: loss_terms(first, second, positives)[0], dense, binary
    )
    positives_count = jnp.sum((positives >= 0).astype(f32))
    d_dense, d_binary = loss_pull(jnp.ones((), f32))
    own_q = lambda value: lax.dynamic_slice_in_dim(value, me * q_part, q_part, 0)
    own_p = lambda value: lax.dynamic_slice_in_dim(value, me * p_part, p_part, 1)
    d_asked = jnp.dot(own_q(d_dense), codes, precision=PRECISION_MAX) * scale
    d_hashed = jnp.dot(own_q(d_binary), codes, precision=PRECISION_MAX) * scale
    d_asked = d_asked + d_hashed * (1.0 - own_q(hashed) * own_q(hashed))
    d_codes = (
        jnp.dot(own_p(d_dense).T, asked, precision=PRECISION_MAX)
        + jnp.dot(own_p(d_binary).T, hashed, precision=PRECISION_MAX)
    ) * scale
    d_passages = d_codes * (1.0 - codes_local * codes_local)
    block_parts, bias_parts, param_parts, half_rows = ([], [], [], [])
    gain_total = jnp.zeros((MODEL_WIDTH,), jnp.float32)
    shift_total = jnp.zeros((MODEL_WIDTH,), jnp.float32)
    for layer_params, d_pooled in ((0, d_asked), (1, d_passages)):
        state, lengths, kept, embed_pull, pool_pull, pooled = encoded[layer_params]
        d_output = pool_pull(d_pooled)[0]
        d_state, grad_mats, grad_bias, grad_params = layer_backward(
            d_output,
            state,
            lengths,
            layer_weights[layer_params],
            params_all[2 + 6 * layer_params : 8 + 6 * layer_params],
            kept,
        )
        d_rows, d_gain, d_shift = embed_pull(d_state)
        gain_total = gain_total + d_gain
        shift_total = shift_total + d_shift
        block_parts.append(layer_groups(grad_mats, side).astype(bf16))
        bias_parts.append(grad_bias)
        param_parts.append(grad_params)
        half_rows.append(
            lax.dynamic_slice_in_dim(
                d_rows, core * half, half, 2
            )
        )
    q_half, p_half = half_rows
    row_values = jnp.concatenate([q_half.reshape(-1, half), p_half.reshape(-1, half)])
    value_high = row_values.astype(bf16)
    value_low = (row_values - value_high.astype(f32)).astype(bf16)

    def gather_up(start):
        hot = spread(start)
        return sum(
            jnp.einsum("tj,tc->jc", hot, part, preferred_element_type=f32)
            for part in (value_high, value_low)
        ).reshape(parts, SLOTS, half)

    def put_back(chosen, received):
        return jnp.einsum("sjr,sjc->rc", chosen, received, preferred_element_type=f32)[:rows_here]

    place_grads = jnp.sum(p_half, axis=0)
    place_grads = place_grads.at[:q_length].add(jnp.sum(q_half, axis=0))
    bias_grads = jnp.stack(bias_parts).reshape(LAYERS, parts, vector_part)
    param_grads = jnp.concatenate([jnp.stack([gain_total, shift_total])] + param_parts, axis=0)
    param_grads = param_grads.reshape(-1, parts, shared_part)
    small_grads = jnp.concatenate(
        [
            bias_grads.transpose(1, 0, 2).reshape(parts, -1),
            param_grads.transpose(1, 0, 2).reshape(parts, -1),
        ],
        axis=1,
    )
    small_count = small_grads.shape[1]
    small_rows = -(-small_count // half)
    small_grads = jnp.pad(small_grads, ((0, 0), (0, small_rows * half - small_count)))
    sent = jnp.concatenate(
        [
            gather_up(0.0),
            place_grads.reshape(parts, share, half),
            small_grads.reshape(parts, small_rows, half),
        ],
        axis=1,
    ).astype(bf16)
    got = lax.all_to_all(sent, "blk", 0, 0)
    token_grad = put_back(choose(0.0), got[:, :SLOTS])

    def send_more(carry):
        done, total = carry
        start = (done * SLOTS).astype(f32)
        more = lax.all_to_all(gather_up(start).astype(bf16), "blk", 0, 0)
        return done + 1, total + put_back(choose(start), more)

    token_grad = lax.while_loop(lambda c: c[0] < rounds, send_more, (jnp.int32(1), token_grad))[1]
    rest = jnp.sum(got[:, SLOTS:].astype(f32), axis=0)
    place_part = rest[:share]
    small_grads = rest[share:].reshape(-1)
    grad_vectors = small_grads[:vector_size].reshape(vectors.shape)
    grad_shared = small_grads[vector_size : vector_size + shared_size].reshape(shared.shape)
    all_groups = jnp.concatenate(block_parts, axis=0)
    if even:
        grad_blocks = split_pairs(
            lax.psum_scatter(all_groups, "blk", scatter_dimension=0, tiled=True).astype(f32)
        )
    else:
        grad_blocks = lax.psum_scatter(
            split_pairs(all_groups), "blk", scatter_dimension=0, tiled=True
        ).astype(f32)
    first_core = (core == 0).astype(f32)
    squares = (
        jnp.sum(grad_blocks * grad_blocks)
        + jnp.sum(grad_vectors * grad_vectors)
        + jnp.sum(token_grad * token_grad)
        + jnp.sum(place_part * place_part)
        + first_core * jnp.sum(grad_shared * grad_shared)
    )
    squares = squares + other_core(squares)
    last = to_all(
        jnp.concatenate([place_part, jnp.broadcast_to(squares, (8, half))]), parts
    )
    squares = jnp.sum(last[:, share, 0])
    place_grads = last[:, :share].reshape(length, half)
    margin = jnp.zeros((rows_here, half), f32)
    place_grads = lax.dynamic_slice_in_dim(
        jnp.concatenate([margin, place_grads, margin]),
        jnp.clip(me * rows_here - VOCAB + rows_here, 0, rows_here + length),
        rows_here,
        0,
    )
    table_grad = token_grad + place_grads
    grad_norm = jnp.sqrt(squares) / positives_count
    factor = jnp.minimum(1.0, CLIP / grad_norm) / positives_count
    block_grads = grad_blocks * factor
    left_new = STAT_DECAY * left_stats[0] + (1.0 - STAT_DECAY) * jnp.einsum(
        "nij,nkj->nik", block_grads, block_grads, precision=PRECISION_MAX
    )
    right_new = STAT_DECAY * right_stats[0] + (1.0 - STAT_DECAY) * jnp.einsum(
        "nji,njk->nik", block_grads, block_grads, precision=PRECISION_MAX
    )
    turned = jnp.einsum(
        "nij,njk->nik",
        left_roots[0],
        jnp.einsum("nij,njk->nik", block_grads, right_roots[0], precision=PRECISION_MAX),
        precision=PRECISION_MAX,
    )
    blocks_new = blocks[0] - SHAMPOO_RATE * (turned + WEIGHT_DECAY * blocks[0])
    table_moment_new, table_second_new, table_new = adamw(
        table, table_moment, table_second, table_grad * factor
    )
    vector_moment_new, vector_second_new, vectors_new = adamw(
        vectors, vector_moment, vector_second, grad_vectors * factor
    )
    shared_moment_new, shared_second_new, shared_new = adamw(
        shared, shared_moment, shared_second, grad_shared * factor
    )
    return (
        loss_sum,
        positives_count,
        grad_norm,
        block_grads[None],
        left_new[None],
        right_new[None],
        blocks_new[None],
        table_moment_new,
        table_second_new,
        table_new,
        vector_moment_new,
        vector_second_new,
        vectors_new,
        shared_moment_new,
        shared_second_new,
        shared_new,
    )


def solution(mesh):
    return jax.shard_map(
        on_device,
        mesh=mesh,
        in_specs=(
            P("blk", None),
            P("blk", None),
            P("blk"),
            P("blk"),
            P("blk"),
            P("blk", "tp"),
            P("blk", "tp"),
            P("blk", "tp"),
            P("tp", "blk", None, None),
            P("tp", "blk", None, None),
            P("tp", "blk", None, None),
            P("tp", "blk", None, None),
            P("tp", "blk", None, None),
            P("tp", None, "blk"),
            P("tp", None, "blk"),
            P("tp", None, "blk"),
            P(None, "blk"),
            P(None, "blk"),
            P(None, "blk"),
        ),
        out_specs=(
            P(),
            P(),
            P(),
            P("tp", "blk", None, None),
            P("tp", "blk", None, None),
            P("tp", "blk", None, None),
            P("tp", "blk", None, None),
            P("blk", "tp"),
            P("blk", "tp"),
            P("blk", "tp"),
            P("tp", None, "blk"),
            P("tp", None, "blk"),
            P("tp", None, "blk"),
            P(None, "blk"),
            P(None, "blk"),
            P(None, "blk"),
        ),
        check_vma=False,
    )
```

```python
from functools import partial

import jax
import jax.numpy as jnp
from jax import lax
from jax.experimental import pallas as pl
from jax.experimental.pallas import tpu as pltpu
from jax.sharding import PartitionSpec as P

bf16, f32 = jnp.bfloat16, jnp.float32
MODEL_WIDTH = 768
HALF = MODEL_WIDTH // 2
HD = 64
FF = 3072
UNITS = FF // 2
NORM_EPS = 1e-06
VMEM_LIMIT = 60 * 1024 * 1024
LAYERS = 2
STEP = 10
VOCAB = 30522
CLIP = 0.05
BETA_ONE = 0.9
BETA_TWO = 0.999
STAT_DECAY = 0.95
ADAM_RATE = 0.5
SHAMPOO_RATE = 0.5
WEIGHT_DECAY = 0.01
ADAM_EPS = 1e-08
PRECISION_MAX = lax.Precision.HIGHEST
GROUP = 2
SLOTS = 96
LANES = 128

TAIL = (
    0.16918798443114483,
    0.17071555704933744,
    0.14833696008811015,
    0.2149342153930891,
    -0.09466890560267835,
    0.5477451349382827,
    -0.5122991151213244,
    0.4855729957946344,
    -0.12952484655737367,
)


def gelu_parts(u):
    t = 1.0 / (1.0 + (0.3 * 0.5**0.5) * jnp.abs(u))
    poly = jnp.full_like(t, TAIL[-1])
    for term in TAIL[-2::-1]:
        poly = poly * t + term
    bell = jnp.exp(u * u * -0.5)
    tail = (0.5 * t) * poly * bell
    below = jnp.where(u >= 0, 1.0 - tail, tail)
    return u * below, below + u * (bell * 0.3989422804014327)


def dot(a, b, contract=((1,), (0,))):
    return lax.dot_general(a, b, (contract, ((), ())), preferred_element_type=f32)


NT = ((1,), (1,))
TN = ((0,), (0,))


def unit(value):
    centred = value - jnp.mean(value, axis=-1, keepdims=True)
    rate = lax.rsqrt(jnp.mean(centred * centred, axis=-1, keepdims=True) + NORM_EPS)
    return centred * rate, rate


def unit_back(grad, hat, rate):
    return rate * (
        grad
        - jnp.mean(grad, axis=-1, keepdims=True)
        - hat * jnp.mean(grad * hat, axis=-1, keepdims=True)
    )


def total(value):
    return jnp.sum(value, axis=0, keepdims=True)


def row_lengths(lengths, rows, axis, seg, shape):
    index = lax.broadcasted_iota(jnp.int32, shape, axis)
    if seg == rows:
        return index, None, lengths[pl.program_id(0)]
    which = index // seg
    length = jnp.zeros(shape, jnp.int32)
    for place in range(rows // seg):
        length = jnp.where(which == place, lengths[place], length)
    return index - which * seg, which, length


def row_live(lengths, rows, seg):
    place, _, length = row_lengths(lengths, rows, 0, seg, (rows, 1))
    return (place < length).astype(f32), length


def key_mask(lengths, rows, seg):
    if seg == rows:
        place, _, length = row_lengths(lengths, rows, 1, seg, (1, rows))
        return place < length
    place, which, length = row_lengths(lengths, rows, 1, seg, (rows, rows))
    mine = lax.broadcasted_iota(jnp.int32, (rows, rows), 0) // seg
    return (which == mine) & (place < length)


def load_grid(groups, first, rows, columns, out):
    side, wide = groups.shape[1:]
    for row in range(rows):
        for column in range(columns):
            out[row * side : (row + 1) * side, column * wide : (column + 1) * wide] = groups[
                first + row * columns + column
            ]


def store_grid(matrix, out, first, rows, columns):
    side, wide = out.shape[1:]
    for row in range(rows):
        for column in range(columns):
            out[first + row * columns + column] = matrix[
                row * side : (row + 1) * side, column * wide : (column + 1) * wide
            ].astype(out.dtype)


def head_lanes(rows):
    return lax.broadcasted_iota(jnp.int32, (rows, 2 * HD), 1) < HD


def attention_forward_body(
    seg, lengths, left, right, place_left, place_right, groups, bias, params, state, qkv, context,
    logs, out, joint, output_weight,
):
    rows = left.shape[0]
    side, wide = groups.shape[1:]
    counts = (MODEL_WIDTH // side, 3 * HALF // wide)

    @pl.when(pl.program_id(0) == 0)
    def _():
        load_grid(groups, 0, counts[0], counts[1], joint)
        load_grid(groups, counts[0] * counts[1], HALF // side, MODEL_WIDTH // wide, output_weight)

    def places(ref):
        return jnp.concatenate([ref[:seg].astype(f32)] * (rows // seg), axis=0)

    tokens = jnp.concatenate(
        [left[...].astype(f32) + places(place_left), right[...].astype(f32) + places(place_right)],
        axis=1,
    )
    hat, _ = unit(tokens)
    value = hat * params[0:1] + params[1:2]
    state[...] = value
    projected = dot(value.astype(bf16), joint[...])
    shift = jnp.concatenate(
        [bias[:, :HALF], jnp.zeros((1, HALF), f32), bias[:, HALF : 2 * HALF]], axis=1
    )
    projected = (projected + shift).astype(bf16)
    qkv[...] = projected
    mask = key_mask(lengths, rows, seg)
    first = head_lanes(rows)
    contexts = []
    for pair in range(HALF // (2 * HD)):
        lanes = slice(pair * 2 * HD, (pair + 1) * 2 * HD)
        query = projected[:, :HALF][:, lanes] * jnp.asarray(HD**-0.5, bf16)
        key = projected[:, HALF : 2 * HALF][:, lanes]
        what = projected[:, 2 * HALF :][:, lanes]
        sides = []
        for head in range(2):
            only = jnp.where(first if head == 0 else ~first, query, jnp.zeros_like(query))
            scores = jnp.where(mask, dot(only, key, NT), -1e30)
            top = jnp.max(scores, axis=-1, keepdims=True)
            expo = jnp.exp(scores - top)
            size = jnp.sum(expo, axis=-1, keepdims=True)
            logs[:, 2 * pair + head : 2 * pair + head + 1] = top + jnp.log(size)
            sides.append(dot((expo * (1.0 / size)).astype(bf16), what))
        contexts.append(jnp.where(first, sides[0], sides[1]))
    contexts = jnp.concatenate(contexts, axis=1).astype(bf16)
    context[...] = contexts
    out[...] = dot(contexts, output_weight[...]).astype(bf16)


def forward_ffn_body(
    state, own, other, ups, downs, bias, params, hidden, active, slope, out, up_weight, down_weight
):
    side, wide = ups.shape[1:]

    @pl.when(pl.program_id(0) == 0)
    def _():
        load_grid(ups, 0, MODEL_WIDTH // side, UNITS // wide, up_weight)
        load_grid(downs, 0, UNITS // side, MODEL_WIDTH // wide, down_weight)

    hat, _ = unit(state[...] + (own[...].astype(f32) + other[...].astype(f32)) + params[0:1])
    value = hat * params[1:2] + params[2:3]
    hidden[...] = value
    low = value.astype(bf16)
    step = 2 * wide if UNITS % (2 * wide) == 0 else wide
    result = jnp.zeros(out.shape, f32)
    for start in range(0, UNITS, step):
        columns = slice(start, start + step)
        up = dot(low, up_weight[:, columns]) + bias[:, 2 * HALF + start : 2 * HALF + start + step]
        act, rise = gelu_parts(up)
        act = act.astype(bf16)
        active[:, columns] = act
        slope[:, columns] = rise.astype(bf16)
        result = result + dot(act, down_weight[columns, :])
    out[...] = result.astype(bf16)


def pool_body(seg, lengths, hidden, own, other, params, out):
    rows = hidden.shape[0]
    hat, _ = unit(hidden[...] + (own[...].astype(f32) + other[...].astype(f32)) + params[3:4])
    output = hat * params[4:5] + params[5:6]
    live, _ = row_live(lengths, rows, seg)
    output = output * live
    for place in range(rows // seg):
        index = place if seg < rows else pl.program_id(0)
        mean = total(output[place * seg : (place + 1) * seg]) / lengths[index].astype(f32)
        out[pl.ds(index, 1), :] = mean


def ffn_backward_body(
    seg, lengths, d_pooled, hidden, own, other, active, slope, ups, downs, params, base, out,
    grads, sums, d_bias, up_weight, down_weight, d_up, d_down,
):
    rows = hidden.shape[0]
    side, wide = ups.shape[1:]
    step_at, last = pl.program_id(0), pl.num_programs(0) - 1

    @pl.when(step_at == 0)
    def _():
        load_grid(ups, 0, MODEL_WIDTH // side, UNITS // wide, up_weight)
        load_grid(downs, 0, UNITS // side, MODEL_WIDTH // wide, down_weight)
        d_up[...] = jnp.zeros_like(d_up)
        d_down[...] = jnp.zeros_like(d_down)
        sums[...] = jnp.zeros_like(sums)
        d_bias[...] = jnp.zeros_like(d_bias)

    live, length = row_live(lengths, rows, seg)
    if seg == rows:
        pooled = jnp.broadcast_to(d_pooled[pl.ds(step_at, 1), :], hidden.shape)
    else:
        pooled = jnp.concatenate(
            [
                jnp.broadcast_to(d_pooled[place : place + 1, :], (seg, MODEL_WIDTH))
                for place in range(rows // seg)
            ],
            axis=0,
        )
    d_output = pooled / length.astype(f32) * live
    value = hidden[...]
    hat, rate = unit(value + (own[...].astype(f32) + other[...].astype(f32)) + params[3:4])
    d_sum = unit_back(d_output * params[4:5], hat, rate)
    base[...] = d_sum
    sums[0:1, :] += total(d_sum)
    sums[1:2, :] += total(d_output * hat)
    sums[2:3, :] += total(d_output)
    low = d_sum.astype(bf16)
    hidden_low = value.astype(bf16)
    step = 2 * wide if UNITS % (2 * wide) == 0 else wide
    result = jnp.zeros(out.shape, f32)
    for start in range(0, UNITS, step):
        columns = slice(start, start + step)
        d_down[columns, :] += dot(active[:, columns], low, TN)
        d_act = dot(low, down_weight[columns, :], NT)
        d_pre = (d_act * slope[:, columns].astype(f32)).astype(bf16)
        d_bias[:, columns] += total(d_pre.astype(f32))
        d_up[:, columns] += dot(hidden_low, d_pre, TN)
        result = result + dot(d_pre, up_weight[:, columns], NT)
    out[...] = result.astype(bf16)

    @pl.when(step_at == last)
    def _():
        count = (MODEL_WIDTH // side) * (UNITS // wide)
        store_grid(d_up, grads, 0, MODEL_WIDTH // side, UNITS // wide)
        store_grid(d_down, grads, count, UNITS // side, MODEL_WIDTH // wide)


def attention_backward_body(
    seg, lengths, carried, back_own, back_other, state, own, other, qkv, context, logs, groups,
    params, base, out, grads, sums, d_bias, joint, output_weight, d_joint, d_output_weight,
):
    rows = state.shape[0]
    side, wide = groups.shape[1:]
    counts = (MODEL_WIDTH // side, 3 * HALF // wide)
    step_at, last = pl.program_id(0), pl.num_programs(0) - 1

    @pl.when(step_at == 0)
    def _():
        load_grid(groups, 0, counts[0], counts[1], joint)
        load_grid(groups, counts[0] * counts[1], HALF // side, MODEL_WIDTH // wide, output_weight)
        d_joint[...] = jnp.zeros_like(d_joint)
        d_output_weight[...] = jnp.zeros_like(d_output_weight)
        sums[...] = jnp.zeros_like(sums)
        d_bias[...] = jnp.zeros_like(d_bias)

    d_hidden = carried[...] + (back_own[...].astype(f32) + back_other[...].astype(f32))
    value = state[...]
    hat, rate = unit(value + (own[...].astype(f32) + other[...].astype(f32)) + params[0:1])
    d_sum = unit_back(d_hidden * params[1:2], hat, rate)
    base[...] = d_sum
    sums[0:1, :] += total(d_sum)
    sums[1:2, :] += total(d_hidden * hat)
    sums[2:3, :] += total(d_hidden)
    low = d_sum.astype(bf16)
    d_output_weight[...] += dot(context[...], low, TN)
    d_context = dot(low, output_weight[...], NT).astype(bf16)
    mask = key_mask(lengths, rows, seg)
    first = head_lanes(rows)
    d_queries, d_keys, d_values = [], [], []
    for pair in range(HALF // (2 * HD)):
        lanes = slice(pair * 2 * HD, (pair + 1) * 2 * HD)
        query = qkv[:, pair * 2 * HD : (pair + 1) * 2 * HD] * jnp.asarray(HD**-0.5, bf16)
        key = qkv[:, HALF + pair * 2 * HD : HALF + (pair + 1) * 2 * HD]
        what = qkv[:, 2 * HALF + pair * 2 * HD : 2 * HALF + (pair + 1) * 2 * HD]
        d_pair = d_context[:, lanes]
        sides = []
        for head in range(2):
            mine = first if head == 0 else ~first
            only = jnp.where(mine, query, jnp.zeros_like(query))
            d_only = jnp.where(mine, d_pair, jnp.zeros_like(d_pair))
            scores = jnp.where(mask, dot(only, key, NT), -1e30)
            weights = jnp.exp(scores - logs[:, 2 * pair + head : 2 * pair + head + 1])
            d_weights = dot(d_only, what, NT)
            spread = weights * d_weights
            d_scores = spread - weights * jnp.sum(spread, axis=-1, keepdims=True)
            d_scores = d_scores.astype(bf16)
            sides.append(
                (
                    dot(d_scores, key),
                    dot(d_scores, query, TN),
                    dot(weights.astype(bf16), d_pair, TN),
                )
            )
        d_queries.append(jnp.where(first, sides[0][0], sides[1][0]) * HD**-0.5)
        d_keys.append(jnp.where(first, sides[0][1], sides[1][1]))
        d_values.append(jnp.where(first, sides[0][2], sides[1][2]))
    d_qkv = jnp.concatenate(d_queries + d_keys + d_values, axis=1).astype(bf16)
    d_bias[...] += total(d_qkv.astype(f32))
    d_joint[...] += dot(value.astype(bf16), d_qkv, TN)
    out[...] = dot(d_qkv, joint[...], NT).astype(bf16)

    @pl.when(step_at == last)
    def _():
        store_grid(d_joint, grads, 0, counts[0], counts[1])
        store_grid(
            d_output_weight, grads, counts[0] * counts[1], HALF // side, MODEL_WIDTH // wide
        )


def expand_body(slots, fetched, out):
    hot = lax.broadcasted_iota(jnp.int32, (out.shape[0], fetched.shape[0]), 1) == slots[...]
    out[...] = dot(hot.astype(bf16), fetched[...]).astype(bf16)


def embed_backward_body(
    segs, base_q, own_q, other_q, base_p, own_p, other_p, left, right, place_left, place_right,
    slots, core, params, out, d_place, sums,
):
    rows = left.shape[0]
    step_at = pl.program_id(0)

    @pl.when(step_at == 0)
    def _():
        out[...] = jnp.zeros_like(out)
        d_place[...] = jnp.zeros_like(d_place)
        sums[...] = jnp.zeros_like(sums)

    def work(seg, base, own, other):
        def places(ref):
            return jnp.concatenate([ref[:seg].astype(f32)] * (rows // seg), axis=0)

        d_state = base[...] + (own[...].astype(f32) + other[...].astype(f32))
        tokens = jnp.concatenate(
            [
                left[...].astype(f32) + places(place_left),
                right[...].astype(f32) + places(place_right),
            ],
            axis=1,
        )
        hat, rate = unit(tokens)
        d_rows = unit_back(d_state * params[0:1], hat, rate)
        sums[0:1, :] += total(d_state * hat)
        sums[1:2, :] += total(d_state)
        mine = jnp.where(core[0] == 0, d_rows[:, :HALF], d_rows[:, HALF:])
        for place in range(rows // seg):
            d_place[:seg, :] += mine[place * seg : (place + 1) * seg]
        hot = lax.broadcasted_iota(jnp.int32, (out.shape[0], rows), 0) == slots[0]
        hot = hot.astype(bf16)
        high = mine.astype(bf16)
        low = (mine - high.astype(f32)).astype(bf16)
        out[...] += dot(hot, high) + dot(hot, low)

    @pl.when(step_at == 0)
    def _():
        work(segs[0], base_q, own_q, other_q)

    @pl.when(step_at > 0)
    def _():
        work(segs[1], base_p, own_p, other_p)


def whole(shape):
    return pl.BlockSpec(shape, lambda i: (0,) * len(shape), pipeline_mode=pl.Buffered(1))


def by_rows(rows, width, offset=0):
    return pl.BlockSpec((rows, width), lambda i: (i + offset, 0))


SMEM = pl.BlockSpec(memory_space=pltpu.SMEM)


def fixed(shape):
    return pl.BlockSpec(shape, lambda i: (0,) * len(shape))


def call(body, grid, in_specs, out_specs, out_shape, scratch=(), flops=0, moved=0, name=None):
    return pl.pallas_call(
        body,
        grid=(grid,),
        in_specs=in_specs,
        out_specs=out_specs,
        out_shape=[jax.ShapeDtypeStruct(*item) for item in out_shape],
        scratch_shapes=list(scratch),
        compiler_params=pltpu.CompilerParams(vmem_limit_bytes=VMEM_LIMIT),
        cost_estimate=pl.CostEstimate(flops=flops, bytes_accessed=moved, transcendentals=0),
        name=name,
    )


def weight_spec(side, index):
    per = 16
    wide = 2 * side
    return pl.BlockSpec(
        (per, side, wide), lambda i: (index, 0, 0), pipeline_mode=pl.Buffered(1)
    )


def attention_forward(layer, seg, rows, blocks, first, lengths, left, right, groups, bias, params):
    side, wide = groups.shape[1:]
    place = left.shape[0] // rows - 1
    at_place = pl.BlockSpec((rows, HALF), lambda i: (place, 0), pipeline_mode=pl.Buffered(1))
    count = blocks * rows
    return call(
        partial(attention_forward_body, seg),
        blocks,
        [
            SMEM,
            by_rows(rows, HALF, first),
            by_rows(rows, HALF, first),
            at_place,
            at_place,
            weight_spec(side, 3 * layer),
            whole(bias.shape),
            whole(params.shape),
        ],
        [
            by_rows(rows, MODEL_WIDTH),
            by_rows(rows, 3 * HALF),
            by_rows(rows, HALF),
            by_rows(rows, 2 * HD),
            by_rows(rows, MODEL_WIDTH),
        ],
        [
            ((count, MODEL_WIDTH), f32),
            ((count, 3 * HALF), bf16),
            ((count, HALF), bf16),
            ((count, 2 * HD), f32),
            ((count, MODEL_WIDTH), bf16),
        ],
        [pltpu.VMEM((MODEL_WIDTH, 3 * HALF), bf16), pltpu.VMEM((HALF, MODEL_WIDTH), bf16)],
        flops=2 * count * MODEL_WIDTH * 2400,
        moved=count * 9000,
        name=f"attention_forward_{layer}",
    )(lengths, left, right, left, right, groups, bias, params)


def ffn_forward(layer, rows, state, own, other, groups, bias, params):
    side = groups.shape[1]
    count = state.shape[0]
    return call(
        forward_ffn_body,
        count // rows,
        [
            by_rows(rows, MODEL_WIDTH),
            by_rows(rows, MODEL_WIDTH),
            by_rows(rows, MODEL_WIDTH),
            weight_spec(side, 3 * layer + 1),
            weight_spec(side, 3 * layer + 2),
            whole(bias.shape),
            whole(params.shape),
        ],
        [
            by_rows(rows, MODEL_WIDTH),
            by_rows(rows, UNITS),
            by_rows(rows, UNITS),
            by_rows(rows, MODEL_WIDTH),
        ],
        [
            ((count, MODEL_WIDTH), f32),
            ((count, UNITS), bf16),
            ((count, UNITS), bf16),
            ((count, MODEL_WIDTH), bf16),
        ],
        [pltpu.VMEM((MODEL_WIDTH, UNITS), bf16), pltpu.VMEM((UNITS, MODEL_WIDTH), bf16)],
        flops=4 * count * MODEL_WIDTH * UNITS,
        moved=count * 17000,
        name=f"ffn_forward_{layer}",
    )(state, own, other, groups, groups, bias, params)


def pool_forward(layer, seg, rows, lengths, hidden, own, other, params):
    count = hidden.shape[0]
    return call(
        partial(pool_body, seg),
        count // rows,
        [
            SMEM,
            by_rows(rows, MODEL_WIDTH),
            by_rows(rows, MODEL_WIDTH),
            by_rows(rows, MODEL_WIDTH),
            whole(params.shape),
        ],
        [fixed((count // seg, MODEL_WIDTH))],
        [((count // seg, MODEL_WIDTH), f32)],
        flops=count * MODEL_WIDTH * 10,
        moved=count * MODEL_WIDTH * 8,
        name=f"pool_{layer}",
    )(lengths, hidden, own, other, params)[0]


def ffn_backward(
    layer, seg, rows, lengths, d_pooled, hidden, own, other, active, slope, groups, params
):
    side, wide = groups.shape[1:]
    count = hidden.shape[0]
    return call(
        partial(ffn_backward_body, seg),
        count // rows,
        [
            SMEM,
            whole(d_pooled.shape),
            by_rows(rows, MODEL_WIDTH),
            by_rows(rows, MODEL_WIDTH),
            by_rows(rows, MODEL_WIDTH),
            by_rows(rows, UNITS),
            by_rows(rows, UNITS),
            weight_spec(side, 3 * layer + 1),
            weight_spec(side, 3 * layer + 2),
            whole(params.shape),
        ],
        [
            by_rows(rows, MODEL_WIDTH),
            by_rows(rows, MODEL_WIDTH),
            fixed((32, side, wide)),
            fixed((8, MODEL_WIDTH)),
            fixed((1, UNITS)),
        ],
        [
            ((count, MODEL_WIDTH), f32),
            ((count, MODEL_WIDTH), bf16),
            ((32, side, wide), bf16),
            ((8, MODEL_WIDTH), f32),
            ((1, UNITS), f32),
        ],
        [
            pltpu.VMEM((MODEL_WIDTH, UNITS), bf16),
            pltpu.VMEM((UNITS, MODEL_WIDTH), bf16),
            pltpu.VMEM((MODEL_WIDTH, UNITS), f32),
            pltpu.VMEM((UNITS, MODEL_WIDTH), f32),
        ],
        flops=8 * count * MODEL_WIDTH * UNITS,
        moved=count * 17000,
        name=f"ffn_backward_{layer}",
    )(lengths, d_pooled, hidden, own, other, active, slope, groups, groups, params)


def attention_backward(
    layer, seg, rows, lengths, carried, back_own, back_other, state, own, other, qkv, context,
    logs, groups, params,
):
    side, wide = groups.shape[1:]
    count = state.shape[0]
    wides = by_rows(rows, MODEL_WIDTH)
    return call(
        partial(attention_backward_body, seg),
        count // rows,
        [
            SMEM,
            wides,
            wides,
            wides,
            wides,
            wides,
            wides,
            by_rows(rows, 3 * HALF),
            by_rows(rows, HALF),
            by_rows(rows, 2 * HD),
            weight_spec(side, 3 * layer),
            whole(params.shape),
        ],
        [
            wides,
            wides,
            fixed((16, side, wide)),
            fixed((8, MODEL_WIDTH)),
            fixed((1, 3 * HALF)),
        ],
        [
            ((count, MODEL_WIDTH), f32),
            ((count, MODEL_WIDTH), bf16),
            ((16, side, wide), bf16),
            ((8, MODEL_WIDTH), f32),
            ((1, 3 * HALF), f32),
        ],
        [
            pltpu.VMEM((MODEL_WIDTH, 3 * HALF), bf16),
            pltpu.VMEM((HALF, MODEL_WIDTH), bf16),
            pltpu.VMEM((MODEL_WIDTH, 3 * HALF), f32),
            pltpu.VMEM((HALF, MODEL_WIDTH), f32),
        ],
        flops=4 * count * MODEL_WIDTH * 2400,
        moved=count * 20000,
        name=f"attention_backward_{layer}",
    )(
        lengths, carried, back_own, back_other, state, own, other, qkv, context, logs, groups,
        params,
    )


def expand(rows, slots, fetched):
    count = slots.shape[0]
    return call(
        expand_body,
        count // rows,
        [by_rows(rows, 1), whole(fetched.shape)],
        [by_rows(rows, HALF)],
        [((count, HALF), bf16)],
        flops=2 * count * fetched.size,
        moved=count * HALF * 2,
        name="expand",
    )(slots, fetched)[0]


def embed_backward(segs, rows, q_parts, p_parts, left, right, slots, core, params, picked):
    place = left.shape[0] // rows - 1
    at_place = pl.BlockSpec((rows, HALF), lambda i: (place, 0), pipeline_mode=pl.Buffered(1))
    blocks = slots.shape[0]
    q_spec = pl.BlockSpec((rows, MODEL_WIDTH), lambda i: (0, 0), pipeline_mode=pl.Buffered(1))
    p_spec = pl.BlockSpec((rows, MODEL_WIDTH), lambda i: (jnp.maximum(i - 1, 0), 0))
    return call(
        partial(embed_backward_body, segs),
        blocks,
        [q_spec] * 3
        + [p_spec] * 3
        + [
            by_rows(rows, HALF),
            by_rows(rows, HALF),
            at_place,
            at_place,
            pl.BlockSpec((1, 1, rows), lambda i: (i, 0, 0)),
            SMEM,
            whole(params.shape),
        ],
        [fixed((picked, HALF)), fixed((rows, HALF)), fixed((8, MODEL_WIDTH))],
        [((picked, HALF), f32), ((rows, HALF), f32), ((8, MODEL_WIDTH), f32)],
        flops=4 * blocks * rows * picked * HALF,
        moved=blocks * rows * 8000,
        name="embed_backward",
    )(*q_parts, *p_parts, left, right, left, right, slots, core, params)


def pair_blocks(blocks):
    count, side = blocks.shape[0], blocks.shape[-1]
    return (
        blocks.reshape(count // GROUP, GROUP, side, side)
        .transpose(0, 2, 1, 3)
        .reshape(count // GROUP, side, GROUP * side)
    )


def split_pairs(groups):
    count, side = groups.shape[0], groups.shape[1]
    return (
        groups.reshape(count, side, GROUP, side)
        .transpose(0, 2, 1, 3)
        .reshape(count * GROUP, side, side)
    )


def other_core(value):
    return lax.ppermute(value, "tp", [(0, 1), (1, 0)])


def to_all(value, count):
    return lax.all_to_all(jnp.broadcast_to(value[None], (count,) + value.shape), "blk", 0, 0)


def slot_map(present):
    low = jnp.triu(jnp.ones((LANES, LANES), jnp.bfloat16))
    inner = jnp.einsum(
        "ohl,lm->ohm", present.astype(jnp.bfloat16), low, preferred_element_type=jnp.float32
    )
    totals = inner[..., -1]
    before = jnp.cumsum(totals, axis=1) - totals
    ranks = jnp.where(present, inner + before[..., None] - 1.0, -1.0)
    return ranks, jnp.sum(totals, axis=1)


def pick(slots, start):
    places = jnp.arange(SLOTS, dtype=jnp.float32) + start
    flat = slots.reshape(slots.shape[0], 1, -1)
    return (flat == places[None, :, None]).astype(jnp.bfloat16)


def loss_terms(dense, binary, positive):
    columns = jnp.arange(dense.shape[1])
    hit = (columns[None, :] == positive[:, None]).astype(jnp.float32)
    valid = (positive >= 0).astype(jnp.float32)
    cross = jax.nn.logsumexp(dense, axis=1) - jnp.sum(hit * dense, axis=1)
    anchor = jnp.sum(hit * binary, axis=1)
    ranking = jnp.sum((1.0 - hit) * jax.nn.softplus(1.0 - anchor[:, None] + binary), axis=1) / (
        dense.shape[1] - 1
    )
    return (jnp.sum(valid * (cross + ranking)), jnp.sum(valid))


def adamw(weight, moment, second, grad):
    moment = BETA_ONE * moment + (1.0 - BETA_ONE) * grad
    second = BETA_TWO * second + (1.0 - BETA_TWO) * grad * grad
    update = (
        moment / (1.0 - BETA_ONE**STEP) / (jnp.sqrt(second / (1.0 - BETA_TWO**STEP)) + ADAM_EPS)
    )
    return (moment, second, weight - ADAM_RATE * (update + WEIGHT_DECAY * weight))


def on_device(
    q_tokens,
    p_tokens,
    q_lengths,
    p_lengths,
    positive,
    table,
    table_moment,
    table_second,
    blocks,
    left_stats,
    right_stats,
    left_roots,
    right_roots,
    vectors,
    vector_moment,
    vector_second,
    shared,
    shared_moment,
    shared_second,
):
    parts = lax.axis_size("blk")
    me, core = lax.axis_index("blk"), lax.axis_index("tp")
    rows_here, half = table.shape
    side = blocks.shape[-1]
    per_device = blocks.shape[1]
    even = per_device % GROUP == 0
    own_blocks = blocks[0].astype(bf16)
    if even:
        groups = lax.all_gather(pair_blocks(own_blocks), "blk", axis=0, tiled=True)
    else:
        groups = pair_blocks(lax.all_gather(own_blocks, "blk", axis=0, tiled=True))

    q_live = (jnp.arange(q_tokens.shape[1])[None, :] < q_lengths[:, None]).reshape(-1)
    p_live = (jnp.arange(p_tokens.shape[1])[None, :] < p_lengths[:, None]).reshape(-1)
    tokens = jnp.concatenate([q_tokens.reshape(-1), p_tokens.reshape(-1)])
    live = jnp.concatenate([q_live, p_live])
    tall = -(-rows_here // LANES)
    owner = tokens // rows_here
    inside = tokens - owner * rows_here
    high = jnp.where(live, owner * tall + inside // LANES, -1)
    high_hot = (high[:, None] == jnp.arange(parts * tall)[None, :]).astype(bf16)
    low_hot = (inside[:, None] % LANES == jnp.arange(LANES)[None, :]).astype(bf16)
    uses = jnp.einsum("th,tl->hl", high_hot, low_hot, preferred_element_type=f32)
    present = (uses > 0).reshape(parts, tall, LANES)
    slots, wanted = slot_map(present)
    token_slot = jnp.sum(
        jnp.dot(high_hot.astype(f32), slots.reshape(-1, LANES), precision=PRECISION_MAX) * low_hot,
        axis=1,
    )
    rounds_here = jnp.ceil(jnp.max(wanted) / SLOTS)

    small = jnp.concatenate(
        [
            vectors.astype(bf16).reshape(-1),
            shared.astype(bf16).reshape(-1),
            rounds_here.astype(bf16)[None],
        ]
    )
    small_size = -(-small.shape[0] // LANES) * LANES
    small = jnp.pad(small, (0, small_size - small.shape[0])).reshape(-1, LANES)
    asks = jnp.concatenate(
        [
            present.astype(bf16),
            jnp.broadcast_to(small[None], (parts,) + small.shape),
        ],
        axis=1,
    )
    asks = lax.all_to_all(asks, "blk", 0, 0)
    asked_slots, _ = slot_map(asks[:, :tall] > 0)
    small = asks[:, tall:].reshape(parts, -1)
    vector_part, shared_part = vectors.shape[2], shared.shape[1]
    vector_size, shared_size = vectors.size, shared.size
    bias_all = (
        small[:, :vector_size]
        .reshape(parts, LAYERS, vector_part)
        .transpose(1, 0, 2)
        .reshape(LAYERS, -1)
        .astype(f32)
    )
    params_all = (
        small[:, vector_size : vector_size + shared_size]
        .reshape(parts, -1, shared_part)
        .transpose(1, 0, 2)
        .reshape(-1, parts * shared_part)
        .astype(f32)
    )
    rounds = jnp.max(small[:, vector_size + shared_size].astype(f32)).astype(jnp.int32)

    table_low = jnp.pad(table.astype(bf16), ((0, tall * LANES - rows_here), (0, 0)))
    length = p_tokens.shape[1]
    q_length = q_tokens.shape[1]
    share = length // parts
    margin = jnp.zeros((length, half), bf16)
    first_place = jnp.clip(VOCAB - me * rows_here + length, 0, rows_here + length)
    places_here = lax.dynamic_slice_in_dim(
        jnp.concatenate([margin, table_low[:rows_here], margin]), first_place, length, 0
    )

    def choose(start):
        return pick(asked_slots, start)

    def serve(chosen):
        return jnp.einsum("sjr,rc->sjc", chosen, table_low, preferred_element_type=f32).astype(bf16)

    def places_of(start):
        place = token_slot - start
        fits = (high >= 0) & (place >= 0) & (place < SLOTS)
        return jnp.where(fits, owner * SLOTS + place.astype(jnp.int32), -1)

    def spread(start):
        return (places_of(start)[:, None] == jnp.arange(parts * SLOTS)[None, :]).astype(bf16)

    places_first = places_of(0.0)

    sent = jnp.concatenate(
        [serve(choose(0.0)), places_here.reshape(parts, share, half)], axis=1
    )
    fetched = lax.all_to_all(sent, "blk", 0, 0)
    token_rows = expand(length, places_first[:, None], fetched[:, :SLOTS].reshape(-1, half))
    place_rows = to_all(jnp.sum(fetched[:, SLOTS:].astype(f32), axis=0).astype(bf16), parts)

    def fetch_more(carry):
        done, total = carry
        start = (done * SLOTS).astype(f32)
        more = lax.all_to_all(serve(choose(start)), "blk", 0, 0).reshape(-1, half)
        return done + 1, total + jnp.dot(spread(start), more, preferred_element_type=f32).astype(bf16)

    token_rows = lax.while_loop(lambda c: c[0] < rounds, fetch_more, (jnp.int32(1), token_rows))[1]
    halves = jnp.concatenate([token_rows, place_rows.reshape(length, half)])
    others = other_core(halves)
    left = jnp.where(core == 0, halves, others)
    right = jnp.where(core == 0, others, halves)
    encoded = []
    embed_params = params_all[:2]
    layers = (
        (0, q_length, 0, q_tokens.size // length, q_lengths),
        (1, length, q_tokens.size // length, p_tokens.size // length, p_lengths),
    )
    for layer, seg, first, count, lengths in layers:
        bias = bias_all[layer : layer + 1]
        params = params_all[2 + 6 * layer : 8 + 6 * layer]
        state, qkv, context, logs, own_one = attention_forward(
            layer, seg, length, count, first, lengths, left, right, groups, bias, embed_params
        )
        encoded.append([layer, seg, lengths, bias, params, state, qkv, context, logs, own_one])
    for kept in encoded:
        layer, seg, lengths, bias, params, state, qkv, context, logs, own_one = kept
        other_one = other_core(own_one)
        hidden, active, slope, own_two = ffn_forward(
            layer, length, state, own_one, other_one, groups, bias, params
        )
        kept += [other_one, hidden, active, slope, own_two]
    pooled = []
    for kept in encoded:
        layer, seg, lengths, _, params = kept[:5]
        hidden, _, _, own_two = kept[11:]
        other_two = other_core(own_two)
        kept.append(other_two)
        pooled.append(
            pool_forward(layer, seg, length, lengths, hidden, own_two, other_two, params)
        )
    asked_local = pooled[0]
    codes_local = jnp.tanh(pooled[1])
    codes_low = codes_local.astype(bf16)
    every = to_all(
        jnp.concatenate(
            [
                asked_local,
                codes_low.astype(f32),
                jnp.pad(positive.astype(f32)[None], ((0, 0), (0, MODEL_WIDTH - positive.shape[0]))),
            ]
        ),
        parts,
    )
    q_part, p_part = asked_local.shape[0], codes_local.shape[0]
    asked = every[:, :q_part].reshape(-1, MODEL_WIDTH)
    codes = every[:, q_part : q_part + p_part].reshape(-1, MODEL_WIDTH)
    positives = every[:, q_part + p_part, :q_part].reshape(-1).astype(jnp.int32)
    hashed = jnp.tanh(asked)
    scale = 2.0 * MODEL_WIDTH ** (-0.5)
    dense = jnp.dot(asked, codes.T, precision=PRECISION_MAX) * scale
    binary = jnp.dot(hashed, codes.T, precision=PRECISION_MAX) * scale
    loss_sum, loss_pull = jax.vjp(
        lambda first, second: loss_terms(first, second, positives)[0], dense, binary
    )
    positives_count = jnp.sum((positives >= 0).astype(f32))
    d_dense, d_binary = loss_pull(jnp.ones((), f32))
    own_q = lambda value: lax.dynamic_slice_in_dim(value, me * q_part, q_part, 0)
    own_p = lambda value: lax.dynamic_slice_in_dim(value, me * p_part, p_part, 1)
    d_asked = jnp.dot(own_q(d_dense), codes, precision=PRECISION_MAX) * scale
    d_hashed = jnp.dot(own_q(d_binary), codes, precision=PRECISION_MAX) * scale
    d_asked = d_asked + d_hashed * (1.0 - own_q(hashed) * own_q(hashed))
    d_codes = (
        jnp.dot(own_p(d_dense).T, asked, precision=PRECISION_MAX)
        + jnp.dot(own_p(d_binary).T, hashed, precision=PRECISION_MAX)
    ) * scale
    d_passages = d_codes * (1.0 - codes_local * codes_local)
    back = []
    for kept, d_pooled in zip(encoded, (d_asked, d_passages)):
        (layer, seg, lengths, bias, params, state, qkv, context, logs, own_one, other_one, hidden,
         active, slope, own_two, other_two) = kept
        base, back_own, ffn_grads, ffn_sums, up_bias = ffn_backward(
            layer, seg, length, lengths, d_pooled, hidden, own_two, other_two, active, slope,
            groups, params,
        )
        back.append((base, back_own, ffn_grads, ffn_sums, up_bias))
    block_parts, bias_parts, param_parts, state_parts = [], [], [], []
    for kept, (base, back_own, ffn_grads, ffn_sums, up_bias) in zip(encoded, back):
        (layer, seg, lengths, bias, params, state, qkv, context, logs, own_one, other_one) = kept[:11]
        state_base, state_own, attention_grads, attention_sums, qkv_bias = attention_backward(
            layer, seg, length, lengths, base, back_own, other_core(back_own), state, own_one,
            other_one, qkv, context, logs, groups, params,
        )
        block_parts += [attention_grads, ffn_grads]
        bias_parts.append(
            jnp.concatenate([qkv_bias[0, :HALF], qkv_bias[0, 2 * HALF :], up_bias[0]])
        )
        param_parts += [attention_sums[:3], ffn_sums[:3]]
        state_parts.append((state_base, state_own))
    state_parts = [(base, own, other_core(own)) for base, own in state_parts]
    picked, place_grads, embed_sums = embed_backward(
        (q_length, length), length, state_parts[0], state_parts[1], left, right,
        places_first.reshape(-1, 1, length), core[None], embed_params, parts * SLOTS,
    )
    def gather_up(start):
        return embed_backward(
            (q_length, length), length, state_parts[0], state_parts[1], left, right,
            places_of(start).reshape(-1, 1, length), core[None], embed_params, parts * SLOTS,
        )[0].reshape(parts, SLOTS, half)

    def put_back(chosen, received):
        return jnp.einsum("sjr,sjc->rc", chosen, received, preferred_element_type=f32)[:rows_here]

    bias_grads = jnp.stack(bias_parts).reshape(LAYERS, parts, vector_part)
    param_grads = jnp.concatenate([embed_sums[:2]] + param_parts, axis=0)
    param_grads = param_grads.reshape(-1, parts, shared_part)
    small_grads = jnp.concatenate(
        [
            bias_grads.transpose(1, 0, 2).reshape(parts, -1),
            param_grads.transpose(1, 0, 2).reshape(parts, -1),
        ],
        axis=1,
    )
    small_count = small_grads.shape[1]
    small_rows = -(-small_count // half)
    small_grads = jnp.pad(small_grads, ((0, 0), (0, small_rows * half - small_count)))
    sent = jnp.concatenate(
        [
            picked.reshape(parts, SLOTS, half),
            place_grads.reshape(parts, share, half),
            small_grads.reshape(parts, small_rows, half),
        ],
        axis=1,
    ).astype(bf16)
    got = lax.all_to_all(sent, "blk", 0, 0)
    token_grad = put_back(choose(0.0), got[:, :SLOTS])

    def send_more(carry):
        done, total = carry
        start = (done * SLOTS).astype(f32)
        more = lax.all_to_all(gather_up(start).astype(bf16), "blk", 0, 0)
        return done + 1, total + put_back(choose(start), more)

    token_grad = lax.while_loop(lambda c: c[0] < rounds, send_more, (jnp.int32(1), token_grad))[1]
    rest = jnp.sum(got[:, SLOTS:].astype(f32), axis=0)
    place_part = rest[:share]
    small_grads = rest[share:].reshape(-1)
    grad_vectors = small_grads[:vector_size].reshape(vectors.shape)
    grad_shared = small_grads[vector_size : vector_size + shared_size].reshape(shared.shape)
    all_groups = jnp.concatenate(block_parts, axis=0)
    if even:
        grad_blocks = split_pairs(
            lax.psum_scatter(all_groups, "blk", scatter_dimension=0, tiled=True).astype(f32)
        )
    else:
        grad_blocks = lax.psum_scatter(
            split_pairs(all_groups), "blk", scatter_dimension=0, tiled=True
        ).astype(f32)
    first_core = (core == 0).astype(f32)
    squares = (
        jnp.sum(grad_blocks * grad_blocks)
        + jnp.sum(grad_vectors * grad_vectors)
        + jnp.sum(token_grad * token_grad)
        + jnp.sum(place_part * place_part)
        + first_core * jnp.sum(grad_shared * grad_shared)
    )
    squares = squares + other_core(squares)
    last = to_all(
        jnp.concatenate([place_part, jnp.broadcast_to(squares, (8, half))]), parts
    )
    squares = jnp.sum(last[:, share, 0])
    place_grads = last[:, :share].reshape(length, half)
    margin = jnp.zeros((rows_here, half), f32)
    place_grads = lax.dynamic_slice_in_dim(
        jnp.concatenate([margin, place_grads, margin]),
        jnp.clip(me * rows_here - VOCAB + rows_here, 0, rows_here + length),
        rows_here,
        0,
    )
    table_grad = token_grad + place_grads
    grad_norm = jnp.sqrt(squares) / positives_count
    factor = jnp.minimum(1.0, CLIP / grad_norm) / positives_count
    block_grads = grad_blocks * factor
    left_new = STAT_DECAY * left_stats[0] + (1.0 - STAT_DECAY) * jnp.einsum(
        "nij,nkj->nik", block_grads, block_grads, precision=PRECISION_MAX
    )
    right_new = STAT_DECAY * right_stats[0] + (1.0 - STAT_DECAY) * jnp.einsum(
        "nji,njk->nik", block_grads, block_grads, precision=PRECISION_MAX
    )
    turned = jnp.einsum(
        "nij,njk->nik",
        left_roots[0],
        jnp.einsum("nij,njk->nik", block_grads, right_roots[0], precision=PRECISION_MAX),
        precision=PRECISION_MAX,
    )
    blocks_new = blocks[0] - SHAMPOO_RATE * (turned + WEIGHT_DECAY * blocks[0])
    table_moment_new, table_second_new, table_new = adamw(
        table, table_moment, table_second, table_grad * factor
    )
    vector_moment_new, vector_second_new, vectors_new = adamw(
        vectors, vector_moment, vector_second, grad_vectors * factor
    )
    shared_moment_new, shared_second_new, shared_new = adamw(
        shared, shared_moment, shared_second, grad_shared * factor
    )
    return (
        loss_sum,
        positives_count,
        grad_norm,
        block_grads[None],
        left_new[None],
        right_new[None],
        blocks_new[None],
        table_moment_new,
        table_second_new,
        table_new,
        vector_moment_new,
        vector_second_new,
        vectors_new,
        shared_moment_new,
        shared_second_new,
        shared_new,
    )


def solution(mesh):
    return jax.shard_map(
        on_device,
        mesh=mesh,
        in_specs=(
            P("blk", None),
            P("blk", None),
            P("blk"),
            P("blk"),
            P("blk"),
            P("blk", "tp"),
            P("blk", "tp"),
            P("blk", "tp"),
            P("tp", "blk", None, None),
            P("tp", "blk", None, None),
            P("tp", "blk", None, None),
            P("tp", "blk", None, None),
            P("tp", "blk", None, None),
            P("tp", None, "blk"),
            P("tp", None, "blk"),
            P("tp", None, "blk"),
            P(None, "blk"),
            P(None, "blk"),
            P(None, "blk"),
        ),
        out_specs=(
            P(),
            P(),
            P(),
            P("tp", "blk", None, None),
            P("tp", "blk", None, None),
            P("tp", "blk", None, None),
            P("tp", "blk", None, None),
            P("blk", "tp"),
            P("blk", "tp"),
            P("blk", "tp"),
            P("tp", None, "blk"),
            P("tp", None, "blk"),
            P("tp", None, "blk"),
            P(None, "blk"),
            P(None, "blk"),
            P(None, "blk"),
        ),
        check_vma=False,
    )
```

```python
from functools import partial

import jax
import jax.numpy as jnp
from jax import lax
from jax.experimental import pallas as pl
from jax.experimental.pallas import tpu as pltpu
from jax.sharding import PartitionSpec as P

bf16, f32 = jnp.bfloat16, jnp.float32
MODEL_WIDTH = 768
HALF = MODEL_WIDTH // 2
HD = 64
FF = 3072
UNITS = FF // 2
NORM_EPS = 1e-06
VMEM_LIMIT = 60 * 1024 * 1024
LAYERS = 2
STEP = 10
VOCAB = 30522
CLIP = 0.05
BETA_ONE = 0.9
BETA_TWO = 0.999
STAT_DECAY = 0.95
ADAM_RATE = 0.5
SHAMPOO_RATE = 0.5
WEIGHT_DECAY = 0.01
ADAM_EPS = 1e-08
PRECISION_MAX = lax.Precision.HIGHEST
GROUP = 2
SLOTS = 96
LANES = 128

TAIL = (
    0.16918798443114483,
    0.17071555704933744,
    0.14833696008811015,
    0.2149342153930891,
    -0.09466890560267835,
    0.5477451349382827,
    -0.5122991151213244,
    0.4855729957946344,
    -0.12952484655737367,
)


def gelu_parts(u):
    t = 1.0 / (1.0 + (0.3 * 0.5**0.5) * jnp.abs(u))
    poly = jnp.full_like(t, TAIL[-1])
    for term in TAIL[-2::-1]:
        poly = poly * t + term
    bell = jnp.exp(u * u * -0.5)
    tail = (0.5 * t) * poly * bell
    below = jnp.where(u >= 0, 1.0 - tail, tail)
    return u * below, below + u * (bell * 0.3989422804014327)


def dot(a, b, contract=((1,), (0,))):
    return lax.dot_general(a, b, (contract, ((), ())), preferred_element_type=f32)


NT = ((1,), (1,))
TN = ((0,), (0,))


def unit(value):
    centred = value - jnp.mean(value, axis=-1, keepdims=True)
    rate = lax.rsqrt(jnp.mean(centred * centred, axis=-1, keepdims=True) + NORM_EPS)
    return centred * rate, rate


def unit_back(grad, hat, rate):
    return rate * (
        grad
        - jnp.mean(grad, axis=-1, keepdims=True)
        - hat * jnp.mean(grad * hat, axis=-1, keepdims=True)
    )


def total(value):
    return jnp.sum(value, axis=0, keepdims=True)


def row_lengths(lengths, rows, axis, seg, shape):
    index = lax.broadcasted_iota(jnp.int32, shape, axis)
    if seg == rows:
        return index, None, lengths[pl.program_id(0)]
    which = index // seg
    length = jnp.zeros(shape, jnp.int32)
    for place in range(rows // seg):
        length = jnp.where(which == place, lengths[place], length)
    return index - which * seg, which, length


def row_live(lengths, rows, seg):
    place, _, length = row_lengths(lengths, rows, 0, seg, (rows, 1))
    return (place < length).astype(f32), length


def key_mask(lengths, rows, seg):
    if seg == rows:
        place, _, length = row_lengths(lengths, rows, 1, seg, (1, rows))
        return place < length
    place, which, length = row_lengths(lengths, rows, 1, seg, (rows, rows))
    mine = lax.broadcasted_iota(jnp.int32, (rows, rows), 0) // seg
    return (which == mine) & (place < length)


def load_weights(groups, order, mats, sem):
    side, wide = groups.shape[1:]
    copies, at = [], 0
    for mat in mats:
        for row in range(mat.shape[0] // side):
            for column in range(mat.shape[1] // wide):
                copies.append(
                    pltpu.make_async_copy(
                        groups.at[order[at]],
                        mat.at[
                            row * side : (row + 1) * side, column * wide : (column + 1) * wide
                        ],
                        sem.at[at],
                    )
                )
                at += 1
    for copy in copies:
        copy.start()
    for copy in copies:
        copy.wait()


def store_groups(mats, lows, grads, sem):
    side, wide = grads.shape[1:]
    copies, at = [], 0
    for mat, low in zip(mats, lows):
        low[...] = mat[...].astype(bf16)
        for row in range(mat.shape[0] // side):
            for column in range(mat.shape[1] // wide):
                part = low.at[row * side : (row + 1) * side, column * wide : (column + 1) * wide]
                copies.append(pltpu.make_async_copy(part, grads.at[at], sem.at[at]))
                at += 1
    for copy in copies:
        copy.start()
    for copy in copies:
        copy.wait()


def store_planes(first, mats, lows, spot, sets, sem):
    side, wide = sets[0][1].shape[-2:]
    count = sets[0][1].shape[2]
    copies, at = [], 0
    for mat, low in zip(mats, lows):
        low[...] = mat[...].astype(bf16)
        for row in range(mat.shape[0] // side):
            for column in range(mat.shape[1] // wide):
                owner, place = divmod(first + at, 2 * count)
                plane, own_y, own_x = owner // 4, owner // 2 % 2, owner % 2
                planes, *refs = next(item for item in sets if plane in item[0])
                plane = planes.index(plane)
                by_y = place < count
                mine = spot[1] == own_y if by_y else spot[0] == own_x
                index = (plane, own_x if by_y else own_y, place % count)
                send, keep = (refs[0], refs[2]) if by_y else (refs[1], refs[3])
                region = (
                    slice(row * side, (row + 1) * side),
                    slice(column * wide, (column + 1) * wide),
                )
                copies.append(
                    (mine, pltpu.make_async_copy(mat.at[region], keep.at[index], sem.at[at]))
                )
                copies.append(
                    (
                        jnp.logical_not(mine),
                        pltpu.make_async_copy(low.at[region], send.at[index], sem.at[at]),
                    )
                )
                at += 1
    for where, copy in copies:
        pl.when(where)(copy.start)
    for where, copy in copies:
        pl.when(where)(copy.wait)


def head_lanes(rows):
    return lax.broadcasted_iota(jnp.int32, (rows, 2 * HD), 1) < HD


def attention_forward_body(
    seg, order, lengths, left, right, place_left, place_right, groups, bias, params, state, qkv, context,
    logs, out, joint, output_weight, sem,
):
    rows = left.shape[0]

    @pl.when(pl.program_id(0) == 0)
    def _():
        load_weights(groups, order, (joint, output_weight), sem)

    def places(ref):
        return jnp.concatenate([ref[:seg].astype(f32)] * (rows // seg), axis=0)

    tokens = jnp.concatenate(
        [left[...].astype(f32) + places(place_left), right[...].astype(f32) + places(place_right)],
        axis=1,
    )
    hat, _ = unit(tokens)
    value = hat * params[0:1] + params[1:2]
    state[...] = value
    projected = dot(value.astype(bf16), joint[...])
    shift = jnp.concatenate(
        [bias[:, :HALF], jnp.zeros((1, HALF), f32), bias[:, HALF : 2 * HALF]], axis=1
    )
    projected = (projected + shift).astype(bf16)
    qkv[...] = projected
    mask = key_mask(lengths, rows, seg)
    first = head_lanes(rows)
    contexts = []
    for pair in range(HALF // (2 * HD)):
        lanes = slice(pair * 2 * HD, (pair + 1) * 2 * HD)
        query = projected[:, :HALF][:, lanes] * jnp.asarray(HD**-0.5, bf16)
        key = projected[:, HALF : 2 * HALF][:, lanes]
        what = projected[:, 2 * HALF :][:, lanes]
        sides = []
        for head in range(2):
            only = jnp.where(first if head == 0 else ~first, query, jnp.zeros_like(query))
            scores = jnp.where(mask, dot(only, key, NT), -1e30)
            top = jnp.max(scores, axis=-1, keepdims=True)
            expo = jnp.exp(scores - top)
            size = jnp.sum(expo, axis=-1, keepdims=True)
            logs[:, 2 * pair + head : 2 * pair + head + 1] = top + jnp.log(size)
            sides.append(dot((expo * (1.0 / size)).astype(bf16), what))
        contexts.append(jnp.where(first, sides[0], sides[1]))
    contexts = jnp.concatenate(contexts, axis=1).astype(bf16)
    context[...] = contexts
    out[...] = dot(contexts, output_weight[...]).astype(bf16)


def forward_ffn_body(
    order, state, own, other, groups, bias, params, hidden, active, slope, out, up_weight,
    down_weight, sem,
):
    wide = groups.shape[2]

    @pl.when(pl.program_id(0) == 0)
    def _():
        load_weights(groups, order, (up_weight, down_weight), sem)

    hat, _ = unit(state[...] + (own[...].astype(f32) + other[...].astype(f32)) + params[0:1])
    value = hat * params[1:2] + params[2:3]
    hidden[...] = value
    low = value.astype(bf16)
    step = 2 * wide if UNITS % (2 * wide) == 0 else wide
    result = jnp.zeros(out.shape, f32)
    for start in range(0, UNITS, step):
        columns = slice(start, start + step)
        up = dot(low, up_weight[:, columns]) + bias[:, 2 * HALF + start : 2 * HALF + start + step]
        act, rise = gelu_parts(up)
        act = act.astype(bf16)
        active[:, columns] = act
        slope[:, columns] = rise.astype(bf16)
        result = result + dot(act, down_weight[columns, :])
    out[...] = result.astype(bf16)


def pool_body(seg, lengths, hidden, own, other, params, out):
    rows = hidden.shape[0]
    hat, _ = unit(hidden[...] + (own[...].astype(f32) + other[...].astype(f32)) + params[3:4])
    output = hat * params[4:5] + params[5:6]
    live, _ = row_live(lengths, rows, seg)
    output = output * live
    for place in range(rows // seg):
        index = place if seg < rows else pl.program_id(0)
        mean = total(output[place * seg : (place + 1) * seg]) / lengths[index].astype(f32)
        out[pl.ds(index, 1), :] = mean


def ffn_backward_body(
    seg, order, sets, lengths, spot, d_pooled, hidden, own, other, active, slope, groups, params,
    base, out, sums, d_bias, *rest,
):
    grads, (up_weight, down_weight, d_up, d_down, sem) = rest[:-5], rest[-5:]
    rows = hidden.shape[0]
    wide = groups.shape[2]
    step_at, last = pl.program_id(0), pl.num_programs(0) - 1

    @pl.when(step_at == 0)
    def _():
        load_weights(groups, order, (up_weight, down_weight), sem)
        d_up[...] = jnp.zeros_like(d_up)
        d_down[...] = jnp.zeros_like(d_down)
        sums[...] = jnp.zeros_like(sums)
        d_bias[...] = jnp.zeros_like(d_bias)

    live, length = row_live(lengths, rows, seg)
    if seg == rows:
        pooled = jnp.broadcast_to(d_pooled[pl.ds(step_at, 1), :], hidden.shape)
    else:
        pooled = jnp.concatenate(
            [
                jnp.broadcast_to(d_pooled[place : place + 1, :], (seg, MODEL_WIDTH))
                for place in range(rows // seg)
            ],
            axis=0,
        )
    d_output = pooled / length.astype(f32) * live
    value = hidden[...]
    hat, rate = unit(value + (own[...].astype(f32) + other[...].astype(f32)) + params[3:4])
    d_sum = unit_back(d_output * params[4:5], hat, rate)
    base[...] = d_sum
    sums[0:1, :] += total(d_sum)
    sums[1:2, :] += total(d_output * hat)
    sums[2:3, :] += total(d_output)
    low = d_sum.astype(bf16)
    hidden_low = value.astype(bf16)
    step = 2 * wide if UNITS % (2 * wide) == 0 else wide
    result = jnp.zeros(out.shape, f32)
    for start in range(0, UNITS, step):
        columns = slice(start, start + step)
        d_down[columns, :] += dot(active[:, columns], low, TN)
        d_act = dot(low, down_weight[columns, :], NT)
        d_pre = (d_act * slope[:, columns].astype(f32)).astype(bf16)
        d_bias[:, columns] += total(d_pre.astype(f32))
        d_up[:, columns] += dot(hidden_low, d_pre, TN)
        result = result + dot(d_pre, up_weight[:, columns], NT)
    out[...] = result.astype(bf16)

    @pl.when(step_at == last)
    def _():
        mats, lows = (d_up, d_down), (up_weight, down_weight)
        if sets is None:
            store_groups(mats, lows, grads[0], sem)
        else:
            to = [(planes,) + grads[4 * at : 4 * at + 4] for at, planes in enumerate(sets)]
            store_planes(ATTENTION_GROUPS, mats, lows, spot, to, sem)


def attention_backward_body(
    seg, order, planes, carry_in, carry_out, lengths, spot, carried, back_own, back_other, state,
    own, other, qkv, context, logs, groups, params, *rest,
):
    joint, output_weight, d_joint, d_output_weight, sem = rest[-5:]
    carry, rest = (rest[:4], rest[4:-5]) if carry_in else (None, rest[:-5])
    if planes is not None and not carry_out:
        rest = rest[4:]
    base, out, sums, d_bias, *results = rest
    rows = state.shape[0]
    step_at, last = pl.program_id(0), pl.num_programs(0) - 1

    @pl.when(step_at == 0)
    def _():
        load_weights(groups, order, (joint, output_weight), sem)
        if carry is None:
            d_joint[...] = jnp.zeros_like(d_joint)
            d_output_weight[...] = jnp.zeros_like(d_output_weight)
            sums[...] = jnp.zeros_like(sums)
            d_bias[...] = jnp.zeros_like(d_bias)
        else:
            copies = [
                pltpu.make_async_copy(carry[0], d_joint, sem.at[0]),
                pltpu.make_async_copy(carry[1], d_output_weight, sem.at[1]),
            ]
            for copy in copies:
                copy.start()
            for copy in copies:
                copy.wait()
            sums[...] = carry[2][...]
            d_bias[...] = carry[3][...]

    d_hidden = carried[...] + (back_own[...].astype(f32) + back_other[...].astype(f32))
    value = state[...]
    hat, rate = unit(value + (own[...].astype(f32) + other[...].astype(f32)) + params[0:1])
    d_sum = unit_back(d_hidden * params[1:2], hat, rate)
    base[...] = d_sum
    sums[0:1, :] += total(d_sum)
    sums[1:2, :] += total(d_hidden * hat)
    sums[2:3, :] += total(d_hidden)
    low = d_sum.astype(bf16)
    d_output_weight[...] += dot(context[...], low, TN)
    d_context = dot(low, output_weight[...], NT).astype(bf16)
    mask = key_mask(lengths, rows, seg)
    first = head_lanes(rows)
    d_queries, d_keys, d_values = [], [], []
    for pair in range(HALF // (2 * HD)):
        lanes = slice(pair * 2 * HD, (pair + 1) * 2 * HD)
        query = qkv[:, pair * 2 * HD : (pair + 1) * 2 * HD] * jnp.asarray(HD**-0.5, bf16)
        key = qkv[:, HALF + pair * 2 * HD : HALF + (pair + 1) * 2 * HD]
        what = qkv[:, 2 * HALF + pair * 2 * HD : 2 * HALF + (pair + 1) * 2 * HD]
        d_pair = d_context[:, lanes]
        sides = []
        for head in range(2):
            mine = first if head == 0 else ~first
            only = jnp.where(mine, query, jnp.zeros_like(query))
            d_only = jnp.where(mine, d_pair, jnp.zeros_like(d_pair))
            scores = jnp.where(mask, dot(only, key, NT), -1e30)
            weights = jnp.exp(scores - logs[:, 2 * pair + head : 2 * pair + head + 1])
            d_weights = dot(d_only, what, NT)
            spread = weights * d_weights
            d_scores = spread - weights * jnp.sum(spread, axis=-1, keepdims=True)
            d_scores = d_scores.astype(bf16)
            sides.append(
                (
                    dot(d_scores, key),
                    dot(d_scores, query, TN),
                    dot(weights.astype(bf16), d_pair, TN),
                )
            )
        d_queries.append(jnp.where(first, sides[0][0], sides[1][0]) * HD**-0.5)
        d_keys.append(jnp.where(first, sides[0][1], sides[1][1]))
        d_values.append(jnp.where(first, sides[0][2], sides[1][2]))
    d_qkv = jnp.concatenate(d_queries + d_keys + d_values, axis=1).astype(bf16)
    d_bias[...] += total(d_qkv.astype(f32))
    d_joint[...] += dot(value.astype(bf16), d_qkv, TN)
    out[...] = dot(d_qkv, joint[...], NT).astype(bf16)

    @pl.when(step_at == last)
    def _():
        mats, lows = (d_joint, d_output_weight), (joint, output_weight)
        if carry_out:
            copies = [
                pltpu.make_async_copy(d_joint, results[0], sem.at[0]),
                pltpu.make_async_copy(d_output_weight, results[1], sem.at[1]),
            ]
            for copy in copies:
                copy.start()
            for copy in copies:
                copy.wait()
        elif planes is None:
            store_groups(mats, lows, results[0], sem)
        else:
            store_planes(0, mats, lows, spot, [(planes,) + tuple(results)], sem)


def expand_body(slots, fetched, out):
    hot = lax.broadcasted_iota(jnp.int32, (out.shape[0], fetched.shape[0]), 1) == slots[...]
    out[...] = dot(hot.astype(bf16), fetched[...]).astype(bf16)


def embed_backward_body(
    segs, starts, *refs
):
    sources = [refs[at * 3 : at * 3 + 3] for at in range(len(starts))]
    left, right, place_left, place_right, slots, core, params, out, d_place, sums = refs[-10:]
    rows = left.shape[0]
    step_at = pl.program_id(0)

    @pl.when(step_at == 0)
    def _():
        out[...] = jnp.zeros_like(out)
        d_place[...] = jnp.zeros_like(d_place)
        sums[...] = jnp.zeros_like(sums)

    def work(seg, base, own, other):
        def places(ref):
            return jnp.concatenate([ref[:seg].astype(f32)] * (rows // seg), axis=0)

        d_state = base[...] + (own[...].astype(f32) + other[...].astype(f32))
        tokens = jnp.concatenate(
            [
                left[...].astype(f32) + places(place_left),
                right[...].astype(f32) + places(place_right),
            ],
            axis=1,
        )
        hat, rate = unit(tokens)
        d_rows = unit_back(d_state * params[0:1], hat, rate)
        sums[0:1, :] += total(d_state * hat)
        sums[1:2, :] += total(d_state)
        mine = jnp.where(core[0] == 0, d_rows[:, :HALF], d_rows[:, HALF:])
        for place in range(rows // seg):
            d_place[:seg, :] += mine[place * seg : (place + 1) * seg]
        hot = lax.broadcasted_iota(jnp.int32, (out.shape[0], rows), 0) == slots[0]
        hot = hot.astype(bf16)
        high = mine.astype(bf16)
        low = (mine - high.astype(f32)).astype(bf16)
        out[...] += dot(hot, high) + dot(hot, low)

    ends = starts[1:] + (None,)
    for source, seg, start, end in zip(sources, segs, starts, ends):
        here = step_at >= start
        if end is not None:
            here = here & (step_at < end)

        @pl.when(here)
        def _():
            work(seg, *source)


def whole(shape):
    return pl.BlockSpec(shape, lambda i: (0,) * len(shape), pipeline_mode=pl.Buffered(1))


def by_rows(rows, width, offset=0):
    return pl.BlockSpec((rows, width), lambda i: (i + offset, 0))


SMEM = pl.BlockSpec(memory_space=pltpu.SMEM)


def fixed(shape):
    return pl.BlockSpec(shape, lambda i: (0,) * len(shape))


def call(body, grid, in_specs, out_specs, out_shape, scratch=(), us=1.0, name=None, alias=None):
    return pl.pallas_call(
        body,
        grid=(grid,),
        in_specs=in_specs,
        out_specs=out_specs,
        out_shape=[jax.ShapeDtypeStruct(*item) for item in out_shape],
        scratch_shapes=list(scratch),
        compiler_params=pltpu.CompilerParams(vmem_limit_bytes=VMEM_LIMIT),
        cost_estimate=pl.CostEstimate(
            flops=int(us * 1.15e8), bytes_accessed=int(us * 1e4), transcendentals=0
        ),
        input_output_aliases=alias or {},
        name=name,
    )


ANY = pl.BlockSpec(memory_space=pl.ANY)
ATTENTION_GROUPS = 16
FFN_GROUPS = 32


def attention_forward(
    layer, seg, rows, blocks, first, lengths, left, right, groups, order, bias, params
):
    place = left.shape[0] // rows - 1
    at_place = pl.BlockSpec((rows, HALF), lambda i: (place, 0), pipeline_mode=pl.Buffered(1))
    count = blocks * rows
    return call(
        partial(attention_forward_body, seg, order[:ATTENTION_GROUPS]),
        blocks,
        [
            SMEM,
            by_rows(rows, HALF, first),
            by_rows(rows, HALF, first),
            at_place,
            at_place,
            ANY,
            whole(bias.shape),
            whole(params.shape),
        ],
        [
            by_rows(rows, MODEL_WIDTH),
            by_rows(rows, 3 * HALF),
            by_rows(rows, HALF),
            by_rows(rows, 2 * HD),
            by_rows(rows, MODEL_WIDTH),
        ],
        [
            ((count, MODEL_WIDTH), f32),
            ((count, 3 * HALF), bf16),
            ((count, HALF), bf16),
            ((count, 2 * HD), f32),
            ((count, MODEL_WIDTH), bf16),
        ],
        [
            pltpu.VMEM((MODEL_WIDTH, 3 * HALF), bf16),
            pltpu.VMEM((HALF, MODEL_WIDTH), bf16),
            pltpu.SemaphoreType.DMA((ATTENTION_GROUPS,)),
        ],
        us=2.5 * blocks,
        name=f"attention_forward_{layer}",
    )(lengths, left, right, left, right, groups, bias, params)


def ffn_forward(layer, rows, state, own, other, groups, order, bias, params):
    count = state.shape[0]
    return call(
        partial(forward_ffn_body, order[ATTENTION_GROUPS:]),
        count // rows,
        [
            by_rows(rows, MODEL_WIDTH),
            by_rows(rows, MODEL_WIDTH),
            by_rows(rows, MODEL_WIDTH),
            ANY,
            whole(bias.shape),
            whole(params.shape),
        ],
        [
            by_rows(rows, MODEL_WIDTH),
            by_rows(rows, UNITS),
            by_rows(rows, UNITS),
            by_rows(rows, MODEL_WIDTH),
        ],
        [
            ((count, MODEL_WIDTH), f32),
            ((count, UNITS), bf16),
            ((count, UNITS), bf16),
            ((count, MODEL_WIDTH), bf16),
        ],
        [
            pltpu.VMEM((MODEL_WIDTH, UNITS), bf16),
            pltpu.VMEM((UNITS, MODEL_WIDTH), bf16),
            pltpu.SemaphoreType.DMA((FFN_GROUPS,)),
        ],
        us=3.8 * (count // rows),
        name=f"ffn_forward_{layer}",
    )(state, own, other, groups, bias, params)


def pool_forward(layer, seg, rows, lengths, hidden, own, other, params):
    count = hidden.shape[0]
    return call(
        partial(pool_body, seg),
        count // rows,
        [
            SMEM,
            by_rows(rows, MODEL_WIDTH),
            by_rows(rows, MODEL_WIDTH),
            by_rows(rows, MODEL_WIDTH),
            whole(params.shape),
        ],
        [fixed((count // seg, MODEL_WIDTH))],
        [((count // seg, MODEL_WIDTH), f32)],
        us=1.1 * (count // rows),
        name=f"pool_{layer}",
    )(lengths, hidden, own, other, params)[0]


def plane_shapes(planes, side, wide):
    shape = (len(planes), 2, 3, side, wide)
    return [(shape, bf16)] * 2 + [(shape, f32)] * 2


def ffn_backward(
    layer, seg, rows, lengths, spot, d_pooled, hidden, own, other, active, slope, groups, order,
    params, sets,
):
    side, wide = groups.shape[1:]
    count = hidden.shape[0]
    if sets is None:
        results = [((FFN_GROUPS, side, wide), bf16)]
    else:
        results = [item for planes in sets for item in plane_shapes(planes, side, wide)]
    return call(
        partial(ffn_backward_body, seg, order[ATTENTION_GROUPS:], sets),
        count // rows,
        [
            SMEM,
            SMEM,
            whole(d_pooled.shape),
            by_rows(rows, MODEL_WIDTH),
            by_rows(rows, MODEL_WIDTH),
            by_rows(rows, MODEL_WIDTH),
            by_rows(rows, UNITS),
            by_rows(rows, UNITS),
            ANY,
            whole(params.shape),
        ],
        [
            by_rows(rows, MODEL_WIDTH),
            by_rows(rows, MODEL_WIDTH),
            fixed((8, MODEL_WIDTH)),
            fixed((1, UNITS)),
        ]
        + [ANY] * len(results),
        [
            ((count, MODEL_WIDTH), f32),
            ((count, MODEL_WIDTH), bf16),
            ((8, MODEL_WIDTH), f32),
            ((1, UNITS), f32),
        ]
        + results,
        [
            pltpu.VMEM((MODEL_WIDTH, UNITS), bf16),
            pltpu.VMEM((UNITS, MODEL_WIDTH), bf16),
            pltpu.VMEM((MODEL_WIDTH, UNITS), f32),
            pltpu.VMEM((UNITS, MODEL_WIDTH), f32),
            pltpu.SemaphoreType.DMA((FFN_GROUPS,)),
        ],
        us=4.8 * (count // rows),
        name=f"ffn_backward_{layer}",
    )(lengths, spot, d_pooled, hidden, own, other, active, slope, groups, params)


def attention_backward(
    layer, seg, rows, first, blocks, lengths, spot, carried, back_own, back_other, state, own,
    other, qkv, context, logs, groups, order, params, planes=None, buffers=(), carry=(),
    carry_out=False,
):
    side, wide = groups.shape[1:]
    count = blocks * rows
    wides = by_rows(rows, MODEL_WIDTH, first)
    out = by_rows(rows, MODEL_WIDTH)
    mats = [((MODEL_WIDTH, 3 * HALF), f32), ((HALF, MODEL_WIDTH), f32)]
    sums = [((8, MODEL_WIDTH), f32), ((1, 3 * HALF), f32)]
    aliases = {}
    if carry_out:
        results = mats
    elif planes is None:
        results = [((ATTENTION_GROUPS, side, wide), bf16)]
    else:
        results = plane_shapes(planes, side, wide)
        aliases = {13 + len(carry) + at: 4 + at for at in range(len(results))}
    return call(
        partial(
            attention_backward_body, seg, order[:ATTENTION_GROUPS], planes, bool(carry), carry_out
        ),
        blocks,
        [
            SMEM,
            SMEM,
            wides,
            wides,
            wides,
            wides,
            wides,
            wides,
            by_rows(rows, 3 * HALF, first),
            by_rows(rows, HALF, first),
            by_rows(rows, 2 * HD, first),
            ANY,
            whole(params.shape),
        ]
        + ([ANY, ANY] + [whole(shape) for shape, _ in sums] if carry else [])
        + [ANY] * len(buffers),
        [out, out] + [fixed(shape) for shape, _ in sums] + [ANY] * len(results),
        [((count, MODEL_WIDTH), f32), ((count, MODEL_WIDTH), bf16)] + sums + results,
        [
            pltpu.VMEM((MODEL_WIDTH, 3 * HALF), bf16),
            pltpu.VMEM((HALF, MODEL_WIDTH), bf16),
            pltpu.VMEM((MODEL_WIDTH, 3 * HALF), f32),
            pltpu.VMEM((HALF, MODEL_WIDTH), f32),
            pltpu.SemaphoreType.DMA((ATTENTION_GROUPS,)),
        ],
        us=5.8 * blocks,
        name=f"attention_backward_{layer}_{first}",
        alias=aliases,
    )(
        lengths, spot, carried, back_own, back_other, state, own, other, qkv, context, logs,
        groups, params, *carry, *buffers,
    )


def expand(rows, slots, fetched):
    count = slots.shape[0]
    return call(
        expand_body,
        count // rows,
        [by_rows(rows, 1), whole(fetched.shape)],
        [by_rows(rows, HALF)],
        [((count, HALF), bf16)],
        us=10.0,
        name="expand",
    )(slots, fetched)[0]


def embed_backward(segs, rows, q_parts, p_parts, left, right, slots, core, params, picked):
    place = left.shape[0] // rows - 1
    at_place = pl.BlockSpec((rows, HALF), lambda i: (place, 0), pipeline_mode=pl.Buffered(1))
    blocks = slots.shape[0]
    sources = [q_parts] + list(zip(*p_parts))
    starts, specs, start = [], [], 0
    for source in sources:
        count = source[0].shape[0] // rows
        spec = pl.BlockSpec(
            (rows, MODEL_WIDTH),
            lambda i, start=start, count=count: (jnp.clip(i - start, 0, count - 1), 0),
        )
        specs += [spec] * 3
        starts.append(start)
        start += count
    return call(
        partial(embed_backward_body, segs[:1] + segs[1:] * len(p_parts[0]), tuple(starts)),
        blocks,
        specs
        + [
            by_rows(rows, HALF),
            by_rows(rows, HALF),
            at_place,
            at_place,
            pl.BlockSpec((1, 1, rows), lambda i: (i, 0, 0)),
            SMEM,
            whole(params.shape),
        ],
        [fixed((picked, HALF)), fixed((rows, HALF)), fixed((8, MODEL_WIDTH))],
        [((picked, HALF), f32), ((rows, HALF), f32), ((8, MODEL_WIDTH), f32)],
        us=20.0,
        name="embed_backward",
    )(
        *[part for source in sources for part in source], left, right, left, right, slots, core,
        params,
    )


def pair_blocks(blocks):
    count, side = blocks.shape[0], blocks.shape[-1]
    return (
        blocks.reshape(count // GROUP, GROUP, side, side)
        .transpose(0, 2, 1, 3)
        .reshape(count // GROUP, side, GROUP * side)
    )


def split_pairs(groups):
    count, side = groups.shape[0], groups.shape[1]
    return (
        groups.reshape(count, side, GROUP, side)
        .transpose(0, 2, 1, 3)
        .reshape(count * GROUP, side, side)
    )


def other_core(value):
    return lax.ppermute(value, "tp", [(0, 1), (1, 0)])


def to_all(value, count):
    return lax.all_to_all(jnp.broadcast_to(value[None], (count,) + value.shape), "blk", 0, 0)


def slot_map(present):
    low = jnp.triu(jnp.ones((LANES, LANES), jnp.bfloat16))
    inner = jnp.einsum(
        "ohl,lm->ohm", present.astype(jnp.bfloat16), low, preferred_element_type=jnp.float32
    )
    totals = inner[..., -1]
    before = jnp.cumsum(totals, axis=1) - totals
    ranks = jnp.where(present, inner + before[..., None] - 1.0, -1.0)
    return ranks, jnp.sum(totals, axis=1)


def pick(slots, start):
    places = jnp.arange(SLOTS, dtype=jnp.float32) + start
    flat = slots.reshape(slots.shape[0], 1, -1)
    return (flat == places[None, :, None]).astype(jnp.bfloat16)


def loss_body(asked, codes, positive, d_asked, d_codes, numbers):
    def full(a, b, contract=((1,), (0,))):
        return lax.dot_general(
            a, b, (contract, ((), ())), precision=PRECISION_MAX, preferred_element_type=f32
        )

    scale = 2.0 * MODEL_WIDTH ** (-0.5)
    asks, words = asked[...], codes[...]
    hashed = jnp.tanh(asks)
    dense = full(asks, words, NT) * scale
    binary = full(hashed, words, NT) * scale
    wanted = positive[...]
    columns = lax.broadcasted_iota(jnp.int32, dense.shape, 1)
    hit = columns == wanted
    valid = (wanted >= 0).astype(f32)
    top = jnp.max(dense, axis=1, keepdims=True)
    expo = jnp.exp(dense - top)
    size = jnp.sum(expo, axis=1, keepdims=True)
    cross = top + jnp.log(size) - jnp.sum(jnp.where(hit, dense, 0.0), axis=1, keepdims=True)
    anchor = jnp.sum(jnp.where(hit, binary, 0.0), axis=1, keepdims=True)
    margin = 1.0 - anchor + binary
    small = jnp.exp(-jnp.abs(margin))
    soft = jnp.maximum(margin, 0.0) + jnp.log1p(small)
    others = 1.0 / (dense.shape[1] - 1)
    ranking = jnp.sum(jnp.where(hit, 0.0, soft), axis=1, keepdims=True) * others
    numbers[0:1, :] = jnp.broadcast_to(total(valid * (cross + ranking)), (1, LANES))
    numbers[1:2, :] = jnp.broadcast_to(total(valid), (1, LANES))
    d_dense = valid * (expo / size - hit.astype(f32)) * scale
    rise = jnp.where(margin >= 0, 1.0, small) / (1.0 + small)
    pull = jnp.where(hit, 0.0, rise) * (valid * others)
    d_binary = (pull - jnp.where(hit, jnp.sum(pull, axis=1, keepdims=True), 0.0)) * scale
    d_asked[...] = full(d_dense, words) + full(d_binary, words) * (1.0 - hashed * hashed)
    d_codes[...] = full(d_dense, asks, TN) + full(d_binary, hashed, TN)


def loss_and_back(asked, codes, positive):
    d_asked, d_codes, numbers = call(
        loss_body,
        1,
        [fixed(asked.shape), fixed(codes.shape), fixed(positive.shape)],
        [fixed(asked.shape), fixed(codes.shape), fixed((8, LANES))],
        [(asked.shape, f32), (codes.shape, f32), ((8, LANES), f32)],
        us=5.0,
        name="loss",
    )(asked, codes, positive)
    return numbers[0, 0], numbers[1, 0], d_asked, d_codes


def halves_of(value):
    high = value.astype(bf16)
    return high, (value - high.astype(f32)).astype(bf16)


def near_full(a, b, contract=((1,), (0,))):
    return dot(a[0], b[0], contract) + (dot(a[0], b[1], contract) + dot(a[1], b[0], contract))


def block_products_body(
    paired, inverse, left, right, *rest
):
    parts, (scaled, square, turned, rows, squares) = rest[:-5], rest[-5:]

    @pl.when(pl.program_id(0) == 0)
    def _():
        squares[...] = jnp.zeros_like(squares)

    side = left.shape[-1]
    for at in range(left.shape[0]):
        grad = sum(
            (part[0][:, at * side : (at + 1) * side] if paired else part[at]).astype(f32)
            for part in parts
        )
        grad = grad * inverse[0]
        scaled[at] = grad
        grad_parts = halves_of(grad)
        square[at] = near_full(grad_parts, grad_parts, NT)
        rows[at] = near_full(grad_parts, grad_parts, TN)
        inner = near_full(grad_parts, halves_of(right[at]))
        turned[at] = near_full(halves_of(left[at]), halves_of(inner))
        squares[...] += jnp.broadcast_to(jnp.sum(grad * grad, axis=0, keepdims=True), (8, side))


def block_products(paired, parts, inverse, left, right):
    amount, side = left.shape[1], left.shape[-1]
    per = GROUP if paired else 1
    four = pl.BlockSpec((None, per, side, side), lambda i: (0, i, 0, 0))
    three = pl.BlockSpec((per, side, side), lambda i: (i, 0, 0))
    given = pl.BlockSpec((1,) + parts[0].shape[1:], lambda i: (i, 0, 0))
    return call(
        partial(block_products_body, paired),
        amount // per,
        [SMEM, four, four] + [given] * len(parts),
        [three] * 4 + [fixed((8, side))],
        [((amount, side, side), f32)] * 4 + [((8, side), f32)],
        us=10.0,
        name="block_products",
    )(inverse, left, right, *parts)


def block_update_body(
    factor, scaled, square, rows, turned, left, right, blocks, grads, left_new, right_new, new
):
    scale = factor[0]
    grads[...] = scaled[...] * scale
    left_new[...] = STAT_DECAY * left[...] + ((1.0 - STAT_DECAY) * scale * scale) * square[...]
    right_new[...] = STAT_DECAY * right[...] + ((1.0 - STAT_DECAY) * scale * scale) * rows[...]
    value = blocks[...]
    new[...] = value - SHAMPOO_RATE * (turned[...] * scale + WEIGHT_DECAY * value)


def block_update(factor, scaled, square, rows, turned, left, right, blocks):
    amount, side = left.shape[1], left.shape[-1]
    per = 3 if amount % 3 == 0 else 1
    four = pl.BlockSpec((None, per, side, side), lambda i: (0, i, 0, 0))
    three = pl.BlockSpec((per, side, side), lambda i: (i, 0, 0))
    return call(
        block_update_body,
        amount // per,
        [SMEM] + [three] * 4 + [four] * 3,
        [four] * 4,
        [(left.shape, f32)] * 4,
        us=9.0,
        name="block_update",
    )(factor, scaled, square, rows, turned, left, right, blocks)


class Slice:
    def __init__(self):
        me = lax.axis_index("blk")
        self.x, self.y, self.z = me % 2, me // 2 % 2, me // 4

    @staticmethod
    def over_x(value):
        return lax.ppermute(value, "blk", [(at, at ^ 1) for at in range(16)])

    @staticmethod
    def over_y(value):
        return lax.ppermute(value, "blk", [(at, at ^ 2) for at in range(16)])

    @staticmethod
    def over_z(value, pairs):
        return lax.ppermute(
            value, "blk", [(4 * a + at, 4 * b + at) for a, b in pairs for at in range(4)]
        )


def choose_at(value, index, axis):
    return lax.dynamic_index_in_dim(value, index, axis, keepdims=False)


def add(*values):
    return sum(value.astype(f32) for value in values)


def after(value, *others):
    return lax.optimization_barrier((value,) + others)[0]


def plane_first(links, send_one, send_two, keep_one, keep_two):
    return keep_one, links.over_y(send_one), keep_two, links.over_x(send_two)


def plane_second(links, one, got_one, two, got_two):
    def both(kept, got, index):
        return add(choose_at(kept, index, 1), choose_at(got, index, 1))

    last_one = links.over_x(both(one, got_one, 1 - links.x).astype(bf16))
    last_two = links.over_y(both(two, got_two, 1 - links.y).astype(bf16))
    one = add(both(one, got_one, links.x), last_one)
    two = add(both(two, got_two, links.y), last_two)
    return jnp.concatenate([one, two], axis=1)


def column_start(links, plane, pairs):
    return links.over_z(plane.astype(bf16), pairs)


def column_step(links, at_end, first, others, pairs):
    return links.over_z(jnp.where(at_end, first, others).astype(bf16), pairs)


def own_column(links, planes):
    z = links.z
    return jnp.where(
        z < 2, jnp.where(z == 0, planes[0], planes[1]), jnp.where(z == 2, planes[2], planes[3])
    )


def adamw(weight, moment, second, grad):
    moment = BETA_ONE * moment + (1.0 - BETA_ONE) * grad
    second = BETA_TWO * second + (1.0 - BETA_TWO) * grad * grad
    update = (
        moment / (1.0 - BETA_ONE**STEP) / (jnp.sqrt(second / (1.0 - BETA_TWO**STEP)) + ADAM_EPS)
    )
    return (moment, second, weight - ADAM_RATE * (update + WEIGHT_DECAY * weight))


def on_device(
    q_tokens,
    p_tokens,
    q_lengths,
    p_lengths,
    positive,
    table,
    table_moment,
    table_second,
    blocks,
    left_stats,
    right_stats,
    left_roots,
    right_roots,
    vectors,
    vector_moment,
    vector_second,
    shared,
    shared_moment,
    shared_second,
):
    parts = lax.axis_size("blk")
    me, core = lax.axis_index("blk"), lax.axis_index("tp")
    rows_here, half = table.shape
    side = blocks.shape[-1]
    per_device = blocks.shape[1]
    even = per_device % GROUP == 0
    own_blocks = blocks[0].astype(bf16)
    in_order = list(range(ATTENTION_GROUPS + FFN_GROUPS))
    known = parts == 16 and even
    if known:
        links = Slice()
        own_groups = pair_blocks(own_blocks)
        keep = own_groups.shape[0] // 2
        got = links.over_z(own_groups[keep:], [(0, 2), (1, 3), (2, 0), (3, 1)])
        kept_groups = own_groups[:keep]
        top_half = links.z >= 2
        later = lax.all_gather(
            jnp.where(top_half, kept_groups, got), "blk", axis=0, tiled=True
        )
        early, later = lax.optimization_barrier((jnp.where(top_half, got, kept_groups), later))
        early = lax.all_gather(early, "blk", axis=0, tiled=True)
        layer_groups = [early, later]
        per = 2 * keep
        owners = len(in_order) // per
        orders = [
            [
                keep * ((at // per) + owners * (first ^ (at % per // keep))) + at % keep
                for at in in_order
            ]
            for first in (0, 1)
        ]
    elif even:
        groups = lax.all_gather(pair_blocks(own_blocks), "blk", axis=0, tiled=True)
    else:
        groups = pair_blocks(lax.all_gather(own_blocks, "blk", axis=0, tiled=True))
    if not known:
        layer_groups = [groups[: len(in_order)], groups[len(in_order) :]]
        orders = [in_order, in_order]

    q_live = (jnp.arange(q_tokens.shape[1])[None, :] < q_lengths[:, None]).reshape(-1)
    p_live = (jnp.arange(p_tokens.shape[1])[None, :] < p_lengths[:, None]).reshape(-1)
    tokens = jnp.concatenate([q_tokens.reshape(-1), p_tokens.reshape(-1)])
    live = jnp.concatenate([q_live, p_live])
    tall = -(-rows_here // LANES)
    owner = tokens // rows_here
    inside = tokens - owner * rows_here
    high = jnp.where(live, owner * tall + inside // LANES, -1)
    high_hot = (high[:, None] == jnp.arange(parts * tall)[None, :]).astype(bf16)
    low_hot = (inside[:, None] % LANES == jnp.arange(LANES)[None, :]).astype(bf16)
    uses = jnp.einsum("th,tl->hl", high_hot, low_hot, preferred_element_type=f32)
    present = (uses > 0).reshape(parts, tall, LANES)
    slots, wanted = slot_map(present)
    token_slot = jnp.sum(
        jnp.dot(high_hot.astype(f32), slots.reshape(-1, LANES), precision=PRECISION_MAX) * low_hot,
        axis=1,
    )
    rounds_here = jnp.ceil(jnp.max(wanted) / SLOTS)

    small = jnp.concatenate(
        [
            vectors.astype(bf16).reshape(-1),
            shared.astype(bf16).reshape(-1),
            rounds_here.astype(bf16)[None],
        ]
    )
    small_size = -(-small.shape[0] // LANES) * LANES
    small = jnp.pad(small, (0, small_size - small.shape[0])).reshape(-1, LANES)
    table_low = jnp.pad(table.astype(bf16), ((0, tall * LANES - rows_here), (0, 0)))
    length = p_tokens.shape[1]
    q_length = q_tokens.shape[1]
    share = length // parts
    margin = jnp.zeros((length, half), bf16)
    first_place = jnp.clip(VOCAB - me * rows_here + length, 0, rows_here + length)
    places_here = lax.dynamic_slice_in_dim(
        jnp.concatenate([margin, table_low[:rows_here], margin]), first_place, length, 0
    )
    asks = jnp.concatenate(
        [
            present.astype(bf16),
            jnp.broadcast_to(small[None], (parts,) + small.shape),
            places_here.reshape(parts, share * half // LANES, LANES),
        ],
        axis=1,
    )
    asks = lax.all_to_all(asks, "blk", 0, 0)
    asked_slots, _ = slot_map(asks[:, :tall] > 0)
    place_share = jnp.sum(asks[:, tall + small.shape[0] :].astype(f32), axis=0).astype(bf16)
    place_share = place_share.reshape(share, half)
    small = asks[:, tall : tall + small.shape[0]].reshape(parts, -1)
    vector_part, shared_part = vectors.shape[2], shared.shape[1]
    vector_size, shared_size = vectors.size, shared.size
    bias_all = (
        small[:, :vector_size]
        .reshape(parts, LAYERS, vector_part)
        .transpose(1, 0, 2)
        .reshape(LAYERS, -1)
        .astype(f32)
    )
    params_all = (
        small[:, vector_size : vector_size + shared_size]
        .reshape(parts, -1, shared_part)
        .transpose(1, 0, 2)
        .reshape(-1, parts * shared_part)
        .astype(f32)
    )
    rounds = jnp.max(small[:, vector_size + shared_size].astype(f32)).astype(jnp.int32)

    def choose(start):
        return pick(asked_slots, start)

    def serve(chosen):
        return jnp.einsum("sjr,rc->sjc", chosen, table_low, preferred_element_type=f32).astype(bf16)

    def places_of(start):
        place = token_slot - start
        fits = (high >= 0) & (place >= 0) & (place < SLOTS)
        return jnp.where(fits, owner * SLOTS + place.astype(jnp.int32), -1)

    def spread(start):
        return (places_of(start)[:, None] == jnp.arange(parts * SLOTS)[None, :]).astype(bf16)

    places_first = places_of(0.0)

    sent = jnp.concatenate(
        [serve(choose(0.0)), jnp.broadcast_to(place_share[None], (parts, share, half))], axis=1
    )
    fetched = lax.all_to_all(sent, "blk", 0, 0)
    token_rows = expand(length, places_first[:, None], fetched[:, :SLOTS].reshape(-1, half))
    place_rows = fetched[:, SLOTS:]

    def fetch_more(carry):
        done, total = carry
        start = (done * SLOTS).astype(f32)
        more = lax.all_to_all(serve(choose(start)), "blk", 0, 0).reshape(-1, half)
        return done + 1, total + jnp.dot(spread(start), more, preferred_element_type=f32).astype(bf16)

    token_rows = lax.while_loop(lambda c: c[0] < rounds, fetch_more, (jnp.int32(1), token_rows))[1]
    halves = jnp.concatenate([token_rows, place_rows.reshape(length, half)])
    others = other_core(halves)
    left = jnp.where(core == 0, halves, others)
    right = jnp.where(core == 0, others, halves)
    left, place_rows = lax.optimization_barrier((left, places_first.reshape(-1, 1, length)))
    encoded = []
    embed_params = params_all[:2]
    layers = (
        (0, q_length, 0, q_tokens.size // length, q_lengths),
        (1, length, q_tokens.size // length, p_tokens.size // length, p_lengths),
    )
    for layer, seg, first, count, lengths in layers:
        bias = bias_all[layer : layer + 1]
        params = params_all[2 + 6 * layer : 8 + 6 * layer]
        state, qkv, context, logs, own_one = attention_forward(
            layer, seg, length, count, first, lengths, left, right,
            layer_groups[layer], orders[layer], bias, embed_params,
        )
        encoded.append([layer, seg, lengths, bias, params, state, qkv, context, logs, own_one])
    for kept in encoded:
        layer, seg, lengths, bias, params, state, qkv, context, logs, own_one = kept
        other_one = other_core(own_one)
        hidden, active, slope, own_two = ffn_forward(
            layer, length, state, own_one, other_one, layer_groups[layer], orders[layer], bias,
            params,
        )
        kept += [other_one, hidden, active, slope, own_two]
    pooled = []
    for kept in encoded:
        layer, seg, lengths, _, params = kept[:5]
        hidden, _, _, own_two = kept[11:]
        other_two = other_core(own_two)
        kept.append(other_two)
        pooled.append(
            pool_forward(layer, seg, length, lengths, hidden, own_two, other_two, params)
        )
    asked_local = pooled[0]
    codes_local = jnp.tanh(pooled[1])
    codes_low = codes_local.astype(bf16)
    every = to_all(
        jnp.concatenate(
            [
                asked_local,
                codes_low.astype(f32),
                jnp.pad(positive.astype(f32)[None], ((0, 0), (0, MODEL_WIDTH - positive.shape[0]))),
            ]
        ),
        parts,
    )
    q_part, p_part = asked_local.shape[0], codes_local.shape[0]
    asked = every[:, :q_part].reshape(-1, MODEL_WIDTH)
    codes = every[:, q_part : q_part + p_part].reshape(-1, MODEL_WIDTH)
    positives = every[:, q_part + p_part, :q_part].reshape(-1).astype(jnp.int32)
    loss_sum, positives_count, d_asked, d_codes = loss_and_back(asked, codes, positives[:, None])
    d_asked = lax.dynamic_slice_in_dim(d_asked, me * q_part, q_part, 0)
    d_codes = lax.dynamic_slice_in_dim(d_codes, me * p_part, p_part, 0)
    d_passages = d_codes * (1.0 - codes_local * codes_local)
    spot = jnp.stack([links.x, links.y]) if known else jnp.zeros((2,), jnp.int32)

    def ffn_back(kept, d_pooled, sets):
        (layer, seg, lengths, bias, params, state, qkv, context, logs, own_one, other_one, hidden,
         active, slope, own_two, other_two) = kept
        return ffn_backward(
            layer, seg, length, lengths, spot, d_pooled, hidden, own_two, other_two, active, slope,
            layer_groups[layer], orders[layer], params, sets,
        )

    def attention_back(kept, base, back_own, back_other, first, count, **more):
        (layer, seg, lengths, bias, params, state, qkv, context, logs, own_one, other_one) = kept[:11]
        return attention_backward(
            layer, seg, length, first, count, lengths[first:] if first else lengths, spot, base,
            back_own, back_other, state, own_one, other_one, qkv, context, logs,
            layer_groups[layer], orders[layer], params, **more,
        )

    q_kept, p_kept = encoded
    q_blocks, p_blocks = q_tokens.size // length, p_tokens.size // length
    q_base, q_back, q_ffn_sums, q_up_bias, *q_ffn = ffn_back(
        q_kept, d_asked, ((0, 1),) if known else None
    )
    q_state, q_state_own, q_sums, q_bias, *q_attention = attention_back(
        q_kept, q_base, q_back, other_core(q_back), 0, q_blocks,
        **(dict(planes=(0, 1), buffers=q_ffn) if known else {}),
    )
    p_base, p_back, p_ffn_sums, p_up_bias, *p_ffn = ffn_back(
        p_kept, after(d_passages, q_sums), ((0,), (1,)) if known else None
    )
    if known:
        early = p_blocks // 2
        q_first = plane_first(links, *q_attention)
        top_first = plane_first(links, *p_ffn[4:])
        p_back, *q_first = lax.optimization_barrier((p_back,) + q_first)
        p_back_other = other_core(p_back)
        q_planes = plane_second(links, *q_first)
        state_one, own_one, *carry = attention_back(
            p_kept, p_base, p_back, p_back_other, 0, early, carry_out=True
        )
        carry = carry[2:] + carry[:2]
        other_one = other_core(own_one)
        carry[2], q_planes, *top_first = lax.optimization_barrier(
            (carry[2], q_planes) + top_first
        )
        top_plane = plane_second(links, *top_first)[0]
        down = column_start(links, q_planes[0], [(3, 2)])
        state_two, own_two, p_sums, p_bias, *low = attention_back(
            p_kept, p_base, p_back, p_back_other, early, p_blocks - early, carry=carry,
            planes=(0,), buffers=p_ffn[:4],
        )
        own_two, top_plane, down = lax.optimization_barrier((own_two, top_plane, down))
        other_two = other_core(own_two)
        up = column_start(links, top_plane, [(0, 1)])
        down = column_step(
            links, links.z == 3, q_planes[1], add(q_planes[0], down), [(3, 2), (2, 1)]
        )
        low_first = plane_first(links, *low)
        state_p = ((state_one, state_two), (own_one, own_two), (other_one, other_two))
        low_first = plane_first(links, *low)
    else:
        p_back_other = other_core(p_back)
        state_one, own_one, p_sums, p_bias, *p_attention = attention_back(
            p_kept, p_base, p_back, p_back_other, 0, p_blocks
        )
        state_p = ((state_one,), (own_one,), (other_core(own_one),))
    def third(value, at):
        return value[:, at * half : (at + 1) * half]

    rows_sent = []
    for bias, up_bias in ((q_bias, q_up_bias), (p_bias, p_up_bias)):
        rows_sent += [third(bias, 0), third(bias, 2)]
        rows_sent += [third(up_bias, at) for at in range(UNITS // half)]
    vector_rows = len(rows_sent)
    state_parts = [
        (q_state, q_state_own, other_core(q_state_own)),
        state_p,
    ]
    picked, place_grads, embed_sums = embed_backward(
        (q_length, length), length, state_parts[0], state_parts[1], left, right,
        place_rows, core[None], embed_params, parts * SLOTS,
    )
    def gather_up(start):
        return embed_backward(
            (q_length, length), length, state_parts[0], state_parts[1], left, right,
            places_of(start).reshape(-1, 1, length), core[None], embed_params, parts * SLOTS,
        )[0].reshape(parts, SLOTS, half)

    def put_back(chosen, received):
        return jnp.einsum("sjr,sjc->rc", chosen, received, preferred_element_type=f32)[:rows_here]

    shared_sums = [embed_sums[:2]]
    for attention_sums, ffn_sums in ((q_sums, q_ffn_sums), (p_sums, p_ffn_sums)):
        shared_sums += [attention_sums[:3], ffn_sums[:3]]
    rows_sent += [third(value, side_at) for side_at in range(2) for value in shared_sums]
    used = sum(value.shape[0] for value in rows_sent)
    per_part = -(-used // parts)
    rows_sent.append(jnp.zeros((parts * per_part - used, half), f32))
    small_grads = jnp.concatenate(rows_sent, axis=0)
    sent = jnp.concatenate(
        [
            picked.reshape(parts, SLOTS, half),
            place_grads.reshape(parts, share, half),
            small_grads.reshape(parts, per_part, half),
        ],
        axis=1,
    ).astype(bf16)
    got = lax.all_to_all(sent, "blk", 0, 0)
    token_grad = put_back(choose(0.0), got[:, :SLOTS])

    def send_more(carry):
        done, total = carry
        start = (done * SLOTS).astype(f32)
        more = lax.all_to_all(gather_up(start).astype(bf16), "blk", 0, 0)
        return done + 1, total + put_back(choose(start), more)

    token_grad = lax.while_loop(lambda c: c[0] < rounds, send_more, (jnp.int32(1), token_grad))[1]
    rest = jnp.sum(got[:, SLOTS:].astype(f32), axis=0)
    if known:
        embed_sums, up, down, *low_first = lax.optimization_barrier(
            (embed_sums, up, down) + low_first
        )
        low_plane = plane_second(links, *low_first)[0]
        z = links.z
        planes = [q_planes[0], q_planes[1], low_plane, top_plane]
        up = column_step(links, z == 0, low_plane, add(top_plane, up), [(0, 1), (1, 2)])
        down = column_step(
            links, z == 3, low_plane, add(jnp.where(z == 2, q_planes[1], q_planes[0]), down),
            [(3, 2), (2, 1), (1, 0)],
        )
        up = column_step(
            links, z == 0, q_planes[1], add(jnp.where(z == 1, low_plane, top_plane), up),
            [(0, 1), (1, 2), (2, 3)],
        )
        grad_parts = (own_column(links, planes), up, down)
    else:
        all_groups = jnp.concatenate(q_attention + q_ffn + p_attention + p_ffn, axis=0)
        if not even:
            all_groups = split_pairs(all_groups)
        grad_parts = (lax.psum_scatter(all_groups, "blk", scatter_dimension=0, tiled=True),)
    inverse = 1.0 / positives_count
    rest = rest * inverse
    row_index = me * per_part + jnp.arange(per_part)
    counted = ((row_index < vector_rows) | (core == 0)).astype(f32)
    squares = (
        jnp.sum(rest[:share] ** 2)
        + jnp.sum(rest[share:] ** 2 * counted[:, None])
        + jnp.sum((token_grad * inverse) ** 2)
    )
    rest = to_all(rest, parts)
    place_grads = rest[:, :share].reshape(length, half)
    small_grads = rest[:, share:].reshape(-1, half)
    grad_vectors = lax.dynamic_slice_in_dim(
        small_grads[:vector_rows].reshape(LAYERS, -1), me * vector_part, vector_part, 1
    )[None]
    shared_rows = shared.shape[0]
    grad_shared = lax.dynamic_slice_in_dim(
        jnp.concatenate(
            [
                small_grads[vector_rows : vector_rows + shared_rows],
                small_grads[vector_rows + shared_rows : vector_rows + 2 * shared_rows],
            ],
            axis=1,
        ),
        me * shared_part,
        shared_part,
        1,
    )
    margin = jnp.zeros((rows_here, half), f32)
    place_grads = lax.dynamic_slice_in_dim(
        jnp.concatenate([margin, place_grads, margin]),
        jnp.clip(me * rows_here - VOCAB + rows_here, 0, rows_here + length),
        rows_here,
        0,
    )
    table_grad = token_grad * inverse + place_grads
    if known:
        (squares, table_grad, grad_vectors, grad_shared, *grad_parts) = lax.optimization_barrier(
            (squares, table_grad, grad_vectors, grad_shared) + grad_parts
        )
    scaled, square, turned, row_square, block_squares = block_products(
        even, grad_parts, inverse[None], left_roots, right_roots
    )
    squares = squares + jnp.sum(block_squares[0])
    devices = parts * 2
    squares = lax.all_to_all(
        jnp.broadcast_to(squares, (devices, 8, LANES)), ("blk", "tp"), 0, 0
    )
    squares = jnp.sum(squares[:, 0, 0])
    grad_norm = jnp.sqrt(squares)
    factor = jnp.minimum(1.0, CLIP / grad_norm)
    block_grads, left_new, right_new, blocks_new = block_update(
        factor[None], scaled, square, row_square, turned, left_stats, right_stats, blocks
    )
    table_moment_new, table_second_new, table_new = adamw(
        table, table_moment, table_second, table_grad * factor
    )
    vector_moment_new, vector_second_new, vectors_new = adamw(
        vectors, vector_moment, vector_second, grad_vectors * factor
    )
    shared_moment_new, shared_second_new, shared_new = adamw(
        shared, shared_moment, shared_second, grad_shared * factor
    )
    return (
        loss_sum,
        positives_count,
        grad_norm,
        block_grads,
        left_new,
        right_new,
        blocks_new,
        table_moment_new,
        table_second_new,
        table_new,
        vector_moment_new,
        vector_second_new,
        vectors_new,
        shared_moment_new,
        shared_second_new,
        shared_new,
    )


def solution(mesh):
    return jax.shard_map(
        on_device,
        mesh=mesh,
        in_specs=(
            P("blk", None),
            P("blk", None),
            P("blk"),
            P("blk"),
            P("blk"),
            P("blk", "tp"),
            P("blk", "tp"),
            P("blk", "tp"),
            P("tp", "blk", None, None),
            P("tp", "blk", None, None),
            P("tp", "blk", None, None),
            P("tp", "blk", None, None),
            P("tp", "blk", None, None),
            P("tp", None, "blk"),
            P("tp", None, "blk"),
            P("tp", None, "blk"),
            P(None, "blk"),
            P(None, "blk"),
            P(None, "blk"),
        ),
        out_specs=(
            P(),
            P(),
            P(),
            P("tp", "blk", None, None),
            P("tp", "blk", None, None),
            P("tp", "blk", None, None),
            P("tp", "blk", None, None),
            P("blk", "tp"),
            P("blk", "tp"),
            P("blk", "tp"),
            P("tp", None, "blk"),
            P("tp", None, "blk"),
            P("tp", None, "blk"),
            P(None, "blk"),
            P(None, "blk"),
            P(None, "blk"),
        ),
        check_vma=False,
    )
```

```python
from functools import partial

import jax
import jax.numpy as jnp
from jax import lax
from jax.experimental import pallas as pl
from jax.experimental.pallas import tpu as pltpu
from jax.sharding import PartitionSpec as P

bf16, f32 = jnp.bfloat16, jnp.float32
MODEL_WIDTH = 768
HALF = MODEL_WIDTH // 2
HD = 64
FF = 3072
UNITS = FF // 2
NORM_EPS = 1e-06
VMEM_LIMIT = 60 * 1024 * 1024
LAYERS = 2
STEP = 10
VOCAB = 30522
CLIP = 0.05
BETA_ONE = 0.9
BETA_TWO = 0.999
STAT_DECAY = 0.95
ADAM_RATE = 0.5
SHAMPOO_RATE = 0.5
WEIGHT_DECAY = 0.01
ADAM_EPS = 1e-08
PRECISION_MAX = lax.Precision.HIGHEST
GROUP = 2
SLOTS = 92
LANES = 128

TAIL = (
    0.16918798443114483,
    0.17071555704933744,
    0.14833696008811015,
    0.2149342153930891,
    -0.09466890560267835,
    0.5477451349382827,
    -0.5122991151213244,
    0.4855729957946344,
    -0.12952484655737367,
)


def gelu_parts(u):
    t = 1.0 / (1.0 + (0.3 * 0.5**0.5) * jnp.abs(u))
    poly = jnp.full_like(t, TAIL[-1])
    for term in TAIL[-2::-1]:
        poly = poly * t + term
    bell = jnp.exp(u * u * -0.5)
    tail = (0.5 * t) * poly * bell
    below = jnp.where(u >= 0, 1.0 - tail, tail)
    return u * below, below + u * (bell * 0.3989422804014327)


def dot(a, b, contract=((1,), (0,))):
    return lax.dot_general(a, b, (contract, ((), ())), preferred_element_type=f32)


NT = ((1,), (1,))
TN = ((0,), (0,))


def unit(value):
    centred = value - jnp.mean(value, axis=-1, keepdims=True)
    rate = lax.rsqrt(jnp.mean(centred * centred, axis=-1, keepdims=True) + NORM_EPS)
    return centred * rate, rate


def unit_back(grad, hat, rate):
    return rate * (
        grad
        - jnp.mean(grad, axis=-1, keepdims=True)
        - hat * jnp.mean(grad * hat, axis=-1, keepdims=True)
    )


def total(value):
    return jnp.sum(value, axis=0, keepdims=True)


def row_lengths(lengths, rows, axis, seg, shape):
    index = lax.broadcasted_iota(jnp.int32, shape, axis)
    if seg == rows:
        return index, None, lengths[pl.program_id(0)]
    which = index // seg
    length = jnp.zeros(shape, jnp.int32)
    before = pl.program_id(0) * (rows // seg)
    for place in range(rows // seg):
        length = jnp.where(which == place, lengths[before + place], length)
    return index - which * seg, which, length


def row_live(lengths, rows, seg):
    place, _, length = row_lengths(lengths, rows, 0, seg, (rows, 1))
    return (place < length).astype(f32), length


def key_mask(lengths, rows, seg):
    if seg == rows:
        place, _, length = row_lengths(lengths, rows, 1, seg, (1, rows))
        return place < length
    place, which, length = row_lengths(lengths, rows, 1, seg, (rows, rows))
    mine = lax.broadcasted_iota(jnp.int32, (rows, rows), 0) // seg
    return (which == mine) & (place < length)


def load_weights(groups, order, first, spot, mats, sem):
    side, wide = groups[0].shape[1:]
    starts, waits, at = [], [], 0
    for mat in mats:
        for row in range(mat.shape[0] // side):
            for column in range(mat.shape[1] // wide):
                to = mat.at[row * side : (row + 1) * side, column * wide : (column + 1) * wide]
                if len(groups) == 1:
                    choices = [(None, groups[0].at[order[first + at]])]
                else:
                    choices = group_choices(groups, order, first + at, spot)
                copies = [
                    (where, pltpu.make_async_copy(part, to, sem.at[at])) for where, part in choices
                ]
                starts += copies
                waits.append(copies[0][1])
                at += 1
    for where, copy in starts:
        if where is None:
            copy.start()
        else:
            pl.when(where)(copy.start)
    for copy in waits:
        copy.wait()


def group_choices(groups, layer, group, spot):
    owner, place = divmod(group, 6)
    plane, own_y, own_x = owner // 4, owner // 2 % 2, owner % 2
    is_first = spot[2 + layer] == (0 if plane == 1 - layer else 1)
    far_x, far_y = spot[0] != own_x, spot[1] != own_y
    near_x, near_y = jnp.logical_not(far_x), jnp.logical_not(far_y)
    part, rest = divmod(place, 3)
    choices = []
    for here, (own, by_x, by_y, *both) in (
        (is_first, groups[:5]),
        (jnp.logical_not(is_first), groups[5:]),
    ):
        choices += [
            (here & near_x & near_y, own.at[place]),
            (here & far_x & near_y, by_x.at[place]),
            (here & near_x & far_y, by_y.at[place]),
            (here & far_x & far_y, both[part].at[rest]),
        ]
    return choices


def gather_near(links, piece):
    return links.over_x(piece), links.over_y(piece)


def gather_far(links, by_x, by_y):
    half = by_x.shape[0] // 2
    return links.over_y(by_x[:half]), links.over_x(by_y[half:])


def store_groups(mats, lows, grads, sem):
    side, wide = grads.shape[1:]
    copies, at = [], 0
    for mat, low in zip(mats, lows):
        low[...] = mat[...].astype(bf16)
        for row in range(mat.shape[0] // side):
            for column in range(mat.shape[1] // wide):
                part = low.at[row * side : (row + 1) * side, column * wide : (column + 1) * wide]
                copies.append(pltpu.make_async_copy(part, grads.at[at], sem.at[at]))
                at += 1
    for copy in copies:
        copy.start()
    for copy in copies:
        copy.wait()


def store_planes(first, mats, lows, spot, sets, sem):
    side, wide = sets[0][1].shape[-2:]
    count = 3
    copies, at = [], 0
    for mat, low in zip(mats, lows):
        low[...] = mat[...].astype(bf16)
        for row in range(mat.shape[0] // side):
            for column in range(mat.shape[1] // wide):
                owner, place = divmod(first + at, 2 * count)
                plane, own_y, own_x = owner // 4, owner // 2 % 2, owner % 2
                planes, *refs = next(item for item in sets if plane in item[0])
                plane = planes.index(plane)
                by_y = place < count
                mine = spot[1] == own_y if by_y else spot[0] == own_x
                index = (plane * 2 + (own_x if by_y else own_y)) * count + place % count
                send, keep = (refs[0], refs[2]) if by_y else (refs[1], refs[3])
                region = (
                    slice(row * side, (row + 1) * side),
                    slice(column * wide, (column + 1) * wide),
                )
                copies.append(
                    (mine, pltpu.make_async_copy(mat.at[region], keep.at[index], sem.at[at]))
                )
                copies.append(
                    (
                        jnp.logical_not(mine),
                        pltpu.make_async_copy(low.at[region], send.at[index], sem.at[at]),
                    )
                )
                at += 1
    for where, copy in copies:
        pl.when(where)(copy.start)
    for where, copy in copies:
        pl.when(where)(copy.wait)


def head_lanes(rows):
    return lax.broadcasted_iota(jnp.int32, (rows, 2 * HD), 1) < HD


def embedded(seg, spot, mine, theirs, place_mine, place_theirs):
    rows = mine.shape[0]

    def side_of(ref, places):
        place = jnp.concatenate([places[:seg].astype(f32)] * (rows // seg), axis=0)
        return ref[...].astype(f32) + place

    own, other = side_of(mine, place_mine), side_of(theirs, place_theirs)
    first = spot[4] == 0
    return jnp.concatenate([jnp.where(first, own, other), jnp.where(first, other, own)], axis=1)


def attention_forward_body(
    seg, order, lengths, spot, mine, theirs, place_mine, place_theirs, bias, params, *rest,
):
    groups, rest = rest[:-8], rest[-8:]
    state, qkv, context, logs, out, joint, output_weight, sem = rest
    rows = mine.shape[0]

    @pl.when(pl.program_id(0) == 0)
    def _():
        load_weights(groups, order, 0, spot, (joint, output_weight), sem)

    hat, _ = unit(embedded(seg, spot, mine, theirs, place_mine, place_theirs))
    value = hat * params[0:1] + params[1:2]
    state[...] = value
    projected = dot(value.astype(bf16), joint[...])
    shift = jnp.concatenate(
        [bias[:, :HALF], jnp.zeros((1, HALF), f32), bias[:, HALF : 2 * HALF]], axis=1
    )
    projected = (projected + shift).astype(bf16)
    qkv[...] = projected
    mask = key_mask(lengths, rows, seg)
    first = head_lanes(rows)
    contexts = []
    for pair in range(HALF // (2 * HD)):
        lanes = slice(pair * 2 * HD, (pair + 1) * 2 * HD)
        query = projected[:, :HALF][:, lanes] * jnp.asarray(HD**-0.5, bf16)
        key = projected[:, HALF : 2 * HALF][:, lanes]
        what = projected[:, 2 * HALF :][:, lanes]
        sides = []
        for head in range(2):
            only = jnp.where(first if head == 0 else ~first, query, jnp.zeros_like(query))
            scores = jnp.where(mask, dot(only, key, NT), -1e30)
            top = jnp.max(scores, axis=-1, keepdims=True)
            expo = jnp.exp(scores - top)
            size = jnp.sum(expo, axis=-1, keepdims=True)
            logs[:, 2 * pair + head : 2 * pair + head + 1] = top + jnp.log(size)
            sides.append(dot((expo * (1.0 / size)).astype(bf16), what))
        contexts.append(jnp.where(first, sides[0], sides[1]))
    contexts = jnp.concatenate(contexts, axis=1).astype(bf16)
    context[...] = contexts
    out[...] = dot(contexts, output_weight[...]).astype(bf16)


def forward_ffn_body(
    order, spot, state, own, other, bias, params, *rest,
):
    groups, rest = rest[:-7], rest[-7:]
    hidden, active, slope, out, up_weight, down_weight, sem = rest
    wide = groups[0].shape[2]

    @pl.when(pl.program_id(0) == 0)
    def _():
        load_weights(groups, order, ATTENTION_GROUPS, spot, (up_weight, down_weight), sem)

    hat, _ = unit(state[...] + (own[...].astype(f32) + other[...].astype(f32)) + params[0:1])
    value = hat * params[1:2] + params[2:3]
    hidden[...] = value
    low = value.astype(bf16)
    step = 2 * wide if UNITS % (2 * wide) == 0 else wide
    result = jnp.zeros(out.shape, f32)
    for start in range(0, UNITS, step):
        columns = slice(start, start + step)
        up = dot(low, up_weight[:, columns]) + bias[:, 2 * HALF + start : 2 * HALF + start + step]
        act, rise = gelu_parts(up)
        act = act.astype(bf16)
        active[:, columns] = act
        slope[:, columns] = rise.astype(bf16)
        result = result + dot(act, down_weight[columns, :])
    out[...] = result.astype(bf16)


def pool_body(seg, lengths, hidden, own, other, params, out):
    rows = hidden.shape[0]
    hat, _ = unit(hidden[...] + (own[...].astype(f32) + other[...].astype(f32)) + params[3:4])
    output = hat * params[4:5] + params[5:6]
    live, _ = row_live(lengths, rows, seg)
    output = output * live
    for place in range(rows // seg):
        index = pl.program_id(0) * (rows // seg) + place
        mean = total(output[place * seg : (place + 1) * seg]) / lengths[index].astype(f32)
        out[pl.ds(index, 1), :] = mean


def ffn_backward_body(
    seg, order, sets, amount, lengths, spot, d_pooled, hidden, own, other, active, slope, params,
    *rest,
):
    groups, rest = rest[:amount], rest[amount:]
    base, out, sums, d_bias, *rest = rest
    grads, (up_weight, down_weight, d_up, d_down, sem) = tuple(rest[:-5]), rest[-5:]
    rows = hidden.shape[0]
    wide = groups[0].shape[2]
    step_at, last = pl.program_id(0), pl.num_programs(0) - 1

    @pl.when(step_at == 0)
    def _():
        load_weights(groups, order, ATTENTION_GROUPS, spot, (up_weight, down_weight), sem)
        d_up[...] = jnp.zeros_like(d_up)
        d_down[...] = jnp.zeros_like(d_down)
        sums[...] = jnp.zeros_like(sums)
        d_bias[...] = jnp.zeros_like(d_bias)

    live, length = row_live(lengths, rows, seg)
    pooled = jnp.concatenate(
        [
            jnp.broadcast_to(
                d_pooled[pl.ds(step_at * (rows // seg) + place, 1), :], (seg, MODEL_WIDTH)
            )
            for place in range(rows // seg)
        ],
        axis=0,
    )
    d_output = pooled / length.astype(f32) * live
    value = hidden[...]
    hat, rate = unit(value + (own[...].astype(f32) + other[...].astype(f32)) + params[3:4])
    d_sum = unit_back(d_output * params[4:5], hat, rate)
    base[...] = d_sum
    sums[0:1, :] += total(d_sum)
    sums[1:2, :] += total(d_output * hat)
    sums[2:3, :] += total(d_output)
    low = d_sum.astype(bf16)
    hidden_low = value.astype(bf16)
    step = 2 * wide if UNITS % (2 * wide) == 0 else wide
    result = jnp.zeros(out.shape, f32)
    for start in range(0, UNITS, step):
        columns = slice(start, start + step)
        d_down[columns, :] += dot(active[:, columns], low, TN)
        d_act = dot(low, down_weight[columns, :], NT)
        d_pre = (d_act * slope[:, columns].astype(f32)).astype(bf16)
        d_bias[:, columns] += total(d_pre.astype(f32))
        d_up[:, columns] += dot(hidden_low, d_pre, TN)
        result = result + dot(d_pre, up_weight[:, columns], NT)
    out[...] = result.astype(bf16)

    @pl.when(step_at == last)
    def _():
        mats, lows = (d_up, d_down), (up_weight, down_weight)
        if sets is None:
            store_groups(mats, lows, grads[0], sem)
        else:
            to = [(planes,) + grads[4 * at : 4 * at + 4] for at, planes in enumerate(sets)]
            store_planes(ATTENTION_GROUPS, mats, lows, spot, to, sem)


def attention_backward_body(
    seg, order, planes, carry_in, carry_out, amount, lengths, spot, carried, back_own, back_other,
    state, own, other, qkv, context, logs, params, *rest,
):
    groups, rest = rest[:amount], rest[amount:]
    joint, output_weight, d_joint, d_output_weight, sem = rest[-5:]
    carry, rest = (rest[:4], rest[4:-5]) if carry_in else (None, rest[:-5])
    if planes is not None and not carry_out:
        rest = rest[4:]
    base, out, sums, d_bias, *results = rest
    rows = state.shape[0]
    step_at, last = pl.program_id(0), pl.num_programs(0) - 1

    @pl.when(step_at == 0)
    def _():
        load_weights(groups, order, 0, spot, (joint, output_weight), sem)
        if carry is None:
            d_joint[...] = jnp.zeros_like(d_joint)
            d_output_weight[...] = jnp.zeros_like(d_output_weight)
            sums[...] = jnp.zeros_like(sums)
            d_bias[...] = jnp.zeros_like(d_bias)
        else:
            copies = [
                pltpu.make_async_copy(carry[0], d_joint, sem.at[0]),
                pltpu.make_async_copy(carry[1], d_output_weight, sem.at[1]),
            ]
            for copy in copies:
                copy.start()
            for copy in copies:
                copy.wait()
            sums[...] = carry[2][...]
            d_bias[...] = carry[3][...]

    d_hidden = carried[...] + (back_own[...].astype(f32) + back_other[...].astype(f32))
    value = state[...]
    hat, rate = unit(value + (own[...].astype(f32) + other[...].astype(f32)) + params[0:1])
    d_sum = unit_back(d_hidden * params[1:2], hat, rate)
    base[...] = d_sum
    sums[0:1, :] += total(d_sum)
    sums[1:2, :] += total(d_hidden * hat)
    sums[2:3, :] += total(d_hidden)
    low = d_sum.astype(bf16)
    d_output_weight[...] += dot(context[...], low, TN)
    d_context = dot(low, output_weight[...], NT).astype(bf16)
    mask = key_mask(lengths, rows, seg)
    first = head_lanes(rows)
    d_queries, d_keys, d_values = [], [], []
    for pair in range(HALF // (2 * HD)):
        lanes = slice(pair * 2 * HD, (pair + 1) * 2 * HD)
        query = qkv[:, pair * 2 * HD : (pair + 1) * 2 * HD] * jnp.asarray(HD**-0.5, bf16)
        key = qkv[:, HALF + pair * 2 * HD : HALF + (pair + 1) * 2 * HD]
        what = qkv[:, 2 * HALF + pair * 2 * HD : 2 * HALF + (pair + 1) * 2 * HD]
        d_pair = d_context[:, lanes]
        sides = []
        for head in range(2):
            mine = first if head == 0 else ~first
            only = jnp.where(mine, query, jnp.zeros_like(query))
            d_only = jnp.where(mine, d_pair, jnp.zeros_like(d_pair))
            scores = jnp.where(mask, dot(only, key, NT), -1e30)
            weights = jnp.exp(scores - logs[:, 2 * pair + head : 2 * pair + head + 1])
            d_weights = dot(d_only, what, NT)
            spread = weights * d_weights
            d_scores = spread - weights * jnp.sum(spread, axis=-1, keepdims=True)
            d_scores = d_scores.astype(bf16)
            sides.append(
                (
                    dot(d_scores, key),
                    dot(d_scores, query, TN),
                    dot(weights.astype(bf16), d_pair, TN),
                )
            )
        d_queries.append(jnp.where(first, sides[0][0], sides[1][0]) * HD**-0.5)
        d_keys.append(jnp.where(first, sides[0][1], sides[1][1]))
        d_values.append(jnp.where(first, sides[0][2], sides[1][2]))
    d_qkv = jnp.concatenate(d_queries + d_keys + d_values, axis=1).astype(bf16)
    d_bias[...] += total(d_qkv.astype(f32))
    d_joint[...] += dot(value.astype(bf16), d_qkv, TN)
    out[...] = dot(d_qkv, joint[...], NT).astype(bf16)

    @pl.when(step_at == last)
    def _():
        mats, lows = (d_joint, d_output_weight), (joint, output_weight)
        if carry_out:
            copies = [
                pltpu.make_async_copy(d_joint, results[0], sem.at[0]),
                pltpu.make_async_copy(d_output_weight, results[1], sem.at[1]),
            ]
            for copy in copies:
                copy.start()
            for copy in copies:
                copy.wait()
        elif planes is None:
            store_groups(mats, lows, results[0], sem)
        else:
            store_planes(0, mats, lows, spot, [(planes,) + tuple(results)], sem)


def expand_body(slots, fetched, out):
    hot = lax.broadcasted_iota(jnp.int32, (out.shape[0], fetched.shape[0]), 1) == slots[...]
    out[...] = dot(hot.astype(bf16), fetched[...]).astype(bf16)


def embed_backward_body(
    segs, starts, parts, *refs
):
    sources = [refs[at * 3 : at * 3 + 3] for at in range(len(starts))]
    smalls = refs[3 * len(starts) : 3 * len(starts) + 8]
    mine, theirs, place_mine, place_theirs, slots, spot, params, out, sums = refs[-11:-2]
    d_place, picked = refs[-2:]
    rows = mine.shape[0]
    step_at = pl.program_id(0)

    @pl.when(step_at == 0)
    def _():
        picked[...] = jnp.zeros_like(picked)
        d_place[...] = jnp.zeros_like(d_place)
        sums[...] = jnp.zeros_like(sums)

    def work(seg, base, own, other):
        d_state = base[...] + (own[...].astype(f32) + other[...].astype(f32))
        hat, rate = unit(embedded(seg, spot, mine, theirs, place_mine, place_theirs))
        d_rows = unit_back(d_state * params[0:1], hat, rate)
        sums[0:1, :] += total(d_state * hat)
        sums[1:2, :] += total(d_state)
        own = jnp.where(spot[4] == 0, d_rows[:, :HALF], d_rows[:, HALF:])
        for place in range(rows // seg):
            d_place[:seg, :] += own[place * seg : (place + 1) * seg]
        hot = lax.broadcasted_iota(jnp.int32, (out.shape[0], rows), 0) == slots[0]
        hot = hot.astype(bf16)
        high = own.astype(bf16)
        low = (own - high.astype(f32)).astype(bf16)
        picked[...] += dot(hot, high) + dot(hot, low)

    ends = starts[1:] + (None,)
    for source, seg, start, end in zip(sources, segs, starts, ends):
        here = step_at >= start
        if end is not None:
            here = here & (step_at < end)

        @pl.when(here)
        def _():
            work(seg, *source)

    @pl.when(step_at == pl.num_programs(0) - 1)
    def _():
        width, share = out.shape[0] // parts, rows // parts
        for part in range(parts):
            at = part * width + SLOTS
            picked[at : at + share, :] = d_place[part * share : (part + 1) * share, :]
        lines = []
        for bias, up_bias in (smalls[0:2], smalls[2:4]):
            lines += [bias[:, :HALF], bias[:, 2 * HALF :]]
            lines += [up_bias[:, at : at + HALF] for at in range(0, UNITS, HALF)]
        for at in (0, HALF):
            lines += [sums[row : row + 1, at : at + HALF] for row in range(2)]
            lines += [
                value[row : row + 1, at : at + HALF] for value in smalls[4:] for row in range(3)
            ]
        per = -(-len(lines) // parts)
        for line, value in enumerate(lines):
            at = line // per * width + SLOTS + share + line % per
            picked[at : at + 1, :] = value
        out[...] = picked[...].astype(bf16)


def whole(shape):
    return pl.BlockSpec(shape, lambda i: (0,) * len(shape), pipeline_mode=pl.Buffered(1))


def by_rows(rows, width, offset=0):
    return pl.BlockSpec((rows, width), lambda i: (i + offset, 0))


SMEM = pl.BlockSpec(memory_space=pltpu.SMEM)


def fixed(shape):
    return pl.BlockSpec(shape, lambda i: (0,) * len(shape))


def call(body, grid, in_specs, out_specs, out_shape, scratch=(), us=1.0, name=None, alias=None):
    return pl.pallas_call(
        body,
        grid=(grid,),
        in_specs=in_specs,
        out_specs=out_specs,
        out_shape=[jax.ShapeDtypeStruct(*item) for item in out_shape],
        scratch_shapes=list(scratch),
        compiler_params=pltpu.CompilerParams(vmem_limit_bytes=VMEM_LIMIT),
        cost_estimate=pl.CostEstimate(
            flops=int(us * 1.15e8), bytes_accessed=int(us * 1e4), transcendentals=0
        ),
        input_output_aliases=alias or {},
        name=name,
    )


ANY = pl.BlockSpec(memory_space=pl.ANY)
ATTENTION_GROUPS = 16
FFN_GROUPS = 32


def attention_forward(
    layer, seg, rows, blocks, first, lengths, spot, mine, theirs, groups, order, bias, params
):
    place = mine.shape[0] // rows - 1
    at_place = pl.BlockSpec((rows, HALF), lambda i: (place, 0), pipeline_mode=pl.Buffered(1))
    count = blocks * rows
    return call(
        partial(attention_forward_body, seg, order),
        blocks,
        [
            SMEM,
            SMEM,
            by_rows(rows, HALF, first),
            by_rows(rows, HALF, first),
            at_place,
            at_place,
            whole(bias.shape),
            whole(params.shape),
        ]
        + [ANY] * len(groups),
        [
            by_rows(rows, MODEL_WIDTH),
            by_rows(rows, 3 * HALF),
            by_rows(rows, HALF),
            by_rows(rows, 2 * HD),
            by_rows(rows, MODEL_WIDTH),
        ],
        [
            ((count, MODEL_WIDTH), f32),
            ((count, 3 * HALF), bf16),
            ((count, HALF), bf16),
            ((count, 2 * HD), f32),
            ((count, MODEL_WIDTH), bf16),
        ],
        [
            pltpu.VMEM((MODEL_WIDTH, 3 * HALF), bf16),
            pltpu.VMEM((HALF, MODEL_WIDTH), bf16),
            pltpu.SemaphoreType.DMA((ATTENTION_GROUPS,)),
        ],
        us=2.5 * blocks,
        name=f"attention_forward_{layer}",
    )(lengths, spot, mine, theirs, mine, theirs, bias, params, *groups)


def ffn_forward(layer, rows, spot, state, own, other, groups, order, bias, params):
    count = state.shape[0]
    return call(
        partial(forward_ffn_body, order),
        count // rows,
        [
            SMEM,
            by_rows(rows, MODEL_WIDTH),
            by_rows(rows, MODEL_WIDTH),
            by_rows(rows, MODEL_WIDTH),
            whole(bias.shape),
            whole(params.shape),
        ]
        + [ANY] * len(groups),
        [
            by_rows(rows, MODEL_WIDTH),
            by_rows(rows, UNITS),
            by_rows(rows, UNITS),
            by_rows(rows, MODEL_WIDTH),
        ],
        [
            ((count, MODEL_WIDTH), f32),
            ((count, UNITS), bf16),
            ((count, UNITS), bf16),
            ((count, MODEL_WIDTH), bf16),
        ],
        [
            pltpu.VMEM((MODEL_WIDTH, UNITS), bf16),
            pltpu.VMEM((UNITS, MODEL_WIDTH), bf16),
            pltpu.SemaphoreType.DMA((FFN_GROUPS,)),
        ],
        us=3.8 * count / 256,
        name=f"ffn_forward_{layer}",
    )(spot, state, own, other, bias, params, *groups)


def pool_forward(layer, seg, rows, lengths, hidden, own, other, params):
    count = hidden.shape[0]
    return call(
        partial(pool_body, seg),
        count // rows,
        [
            SMEM,
            by_rows(rows, MODEL_WIDTH),
            by_rows(rows, MODEL_WIDTH),
            by_rows(rows, MODEL_WIDTH),
            whole(params.shape),
        ],
        [fixed((count // seg, MODEL_WIDTH))],
        [((count // seg, MODEL_WIDTH), f32)],
        us=1.1 * (count // rows),
        name=f"pool_{layer}",
    )(lengths, hidden, own, other, params)[0]


def plane_shapes(planes, side, wide):
    shape = (len(planes) * 2 * 3, side, wide)
    return [(shape, bf16)] * 2 + [(shape, f32)] * 2


def ffn_backward(
    layer, seg, rows, lengths, spot, d_pooled, hidden, own, other, active, slope, groups, order,
    params, sets,
):
    side, wide = groups[0].shape[1:]
    count = hidden.shape[0]
    if sets is None:
        results = [((FFN_GROUPS, side, wide), bf16)]
    else:
        results = [item for planes in sets for item in plane_shapes(planes, side, wide)]
    return call(
        partial(ffn_backward_body, seg, order, sets, len(groups)),
        count // rows,
        [
            SMEM,
            SMEM,
            whole(d_pooled.shape),
            by_rows(rows, MODEL_WIDTH),
            by_rows(rows, MODEL_WIDTH),
            by_rows(rows, MODEL_WIDTH),
            by_rows(rows, UNITS),
            by_rows(rows, UNITS),
            whole(params.shape),
        ]
        + [ANY] * len(groups),
        [
            by_rows(rows, MODEL_WIDTH),
            by_rows(rows, MODEL_WIDTH),
            fixed((8, MODEL_WIDTH)),
            fixed((1, UNITS)),
        ]
        + [ANY] * len(results),
        [
            ((count, MODEL_WIDTH), f32),
            ((count, MODEL_WIDTH), bf16),
            ((8, MODEL_WIDTH), f32),
            ((1, UNITS), f32),
        ]
        + results,
        [
            pltpu.VMEM((MODEL_WIDTH, UNITS), bf16),
            pltpu.VMEM((UNITS, MODEL_WIDTH), bf16),
            pltpu.VMEM((MODEL_WIDTH, UNITS), f32),
            pltpu.VMEM((UNITS, MODEL_WIDTH), f32),
            pltpu.SemaphoreType.DMA((FFN_GROUPS,)),
        ],
        us=4.8 * count / 256,
        name=f"ffn_backward_{layer}",
    )(lengths, spot, d_pooled, hidden, own, other, active, slope, params, *groups)


def attention_backward(
    layer, seg, rows, first, blocks, lengths, spot, carried, back_own, back_other, state, own,
    other, qkv, context, logs, groups, order, params, planes=None, buffers=(), carry=(),
    carry_out=False,
):
    side, wide = groups[0].shape[1:]
    count = blocks * rows
    wides = by_rows(rows, MODEL_WIDTH, first)
    out = by_rows(rows, MODEL_WIDTH)
    mats = [((MODEL_WIDTH, 3 * HALF), f32), ((HALF, MODEL_WIDTH), f32)]
    sums = [((8, MODEL_WIDTH), f32), ((1, 3 * HALF), f32)]
    aliases = {}
    if carry_out:
        results = mats
    elif planes is None:
        results = [((ATTENTION_GROUPS, side, wide), bf16)]
    else:
        results = plane_shapes(planes, side, wide)
        before = 12 + len(groups) + len(carry)
        aliases = {before + at: 4 + at for at in range(len(results))}
    return call(
        partial(
            attention_backward_body, seg, order, planes, bool(carry), carry_out, len(groups)
        ),
        blocks,
        [
            SMEM,
            SMEM,
            wides,
            wides,
            wides,
            wides,
            wides,
            wides,
            by_rows(rows, 3 * HALF, first),
            by_rows(rows, HALF, first),
            by_rows(rows, 2 * HD, first),
            whole(params.shape),
        ]
        + [ANY] * len(groups)
        + ([ANY, ANY] + [whole(shape) for shape, _ in sums] if carry else [])
        + [ANY] * len(buffers),
        [out, out] + [fixed(shape) for shape, _ in sums] + [ANY] * len(results),
        [((count, MODEL_WIDTH), f32), ((count, MODEL_WIDTH), bf16)] + sums + results,
        [
            pltpu.VMEM((MODEL_WIDTH, 3 * HALF), bf16),
            pltpu.VMEM((HALF, MODEL_WIDTH), bf16),
            pltpu.VMEM((MODEL_WIDTH, 3 * HALF), f32),
            pltpu.VMEM((HALF, MODEL_WIDTH), f32),
            pltpu.SemaphoreType.DMA((ATTENTION_GROUPS,)),
        ],
        us=5.8 * blocks,
        name=f"attention_backward_{layer}_{first}",
        alias=aliases,
    )(
        lengths, spot, carried, back_own, back_other, state, own, other, qkv, context, logs,
        params, *groups, *carry, *buffers,
    )


def tall_rows(value):
    return 512 if value.shape[0] % 512 == 0 else 256


def expand(rows, slots, fetched):
    count = slots.shape[0]
    return call(
        expand_body,
        count // rows,
        [by_rows(rows, 1), whole(fetched.shape)],
        [by_rows(rows, HALF)],
        [((count, HALF), bf16)],
        us=10.0,
        name="expand",
    )(slots, fetched)[0]


def embed_backward(
    segs, rows, q_parts, p_parts, smalls, mine, theirs, slots, spot, params, parts, width
):
    place = mine.shape[0] // rows - 1
    at_place = pl.BlockSpec((rows, HALF), lambda i: (place, 0), pipeline_mode=pl.Buffered(1))
    blocks = slots.shape[0]
    sources = [q_parts] + list(zip(*p_parts))
    starts, specs, start = [], [], 0
    for source in sources:
        count = source[0].shape[0] // rows
        spec = pl.BlockSpec(
            (rows, MODEL_WIDTH),
            lambda i, start=start, count=count: (jnp.clip(i - start, 0, count - 1), 0),
        )
        specs += [spec] * 3
        starts.append(start)
        start += count
    return call(
        partial(embed_backward_body, segs[:1] + segs[1:] * len(p_parts[0]), tuple(starts), parts),
        blocks,
        specs
        + [whole(value.shape) for value in smalls]
        + [
            by_rows(rows, HALF),
            by_rows(rows, HALF),
            at_place,
            at_place,
            pl.BlockSpec((1, 1, rows), lambda i: (i, 0, 0)),
            SMEM,
            whole(params.shape),
        ],
        [fixed((parts * width, HALF)), fixed((8, MODEL_WIDTH))],
        [((parts * width, HALF), bf16), ((8, MODEL_WIDTH), f32)],
        [pltpu.VMEM((rows, HALF), f32), pltpu.VMEM((parts * width, HALF), f32)],
        us=20.0,
        name="embed_backward",
    )(
        *[part for source in sources for part in source], *smalls, mine, theirs, mine, theirs,
        slots, spot, params,
    )


def pair_blocks(blocks):
    count, side = blocks.shape[0], blocks.shape[-1]
    return (
        blocks.reshape(count // GROUP, GROUP, side, side)
        .transpose(0, 2, 1, 3)
        .reshape(count // GROUP, side, GROUP * side)
    )


def split_pairs(groups):
    count, side = groups.shape[0], groups.shape[1]
    return (
        groups.reshape(count, side, GROUP, side)
        .transpose(0, 2, 1, 3)
        .reshape(count * GROUP, side, side)
    )


def other_core(value):
    return lax.ppermute(value, "tp", [(0, 1), (1, 0)])


def to_all(value, count):
    return lax.all_to_all(jnp.broadcast_to(value[None], (count,) + value.shape), "blk", 0, 0)


def slot_map(present):
    low = jnp.triu(jnp.ones((LANES, LANES), jnp.bfloat16))
    inner = jnp.einsum(
        "ohl,lm->ohm", present.astype(jnp.bfloat16), low, preferred_element_type=jnp.float32
    )
    totals = inner[..., -1]
    before = jnp.cumsum(totals, axis=1) - totals
    ranks = jnp.where(present, inner + before[..., None] - 1.0, -1.0)
    return ranks, jnp.sum(totals, axis=1)


def pick(slots, start, width):
    places = jnp.arange(width, dtype=jnp.float32)
    places = jnp.where(places < SLOTS, places + start, -2.0)
    flat = slots.reshape(slots.shape[0], 1, -1)
    return (flat == places[None, :, None]).astype(jnp.bfloat16)


def pack_body(blocks, out):
    out[0] = jnp.concatenate([blocks[at] for at in range(GROUP)], axis=1).astype(bf16)


def pack(blocks):
    amount, side = blocks.shape[1], blocks.shape[-1]
    return call(
        pack_body,
        amount // GROUP,
        [pl.BlockSpec((None, GROUP, side, side), lambda i: (0, i, 0, 0))],
        [pl.BlockSpec((1, side, GROUP * side), lambda i: (i, 0, 0))],
        [((amount // GROUP, side, GROUP * side), bf16)],
        us=3.0,
        name="pack",
    )(blocks)[0]


def loss_body(asked, codes, positive, d_asked, d_codes, numbers):
    def full(a, b, contract=((1,), (0,))):
        return lax.dot_general(
            a, b, (contract, ((), ())), precision=PRECISION_MAX, preferred_element_type=f32
        )

    scale = 2.0 * MODEL_WIDTH ** (-0.5)
    asks, words = asked[...], codes[...]
    hashed = jnp.tanh(asks)
    dense = full(asks, words, NT) * scale
    binary = full(hashed, words, NT) * scale
    wanted = positive[...]
    columns = lax.broadcasted_iota(jnp.int32, dense.shape, 1)
    hit = columns == wanted
    valid = (wanted >= 0).astype(f32)
    top = jnp.max(dense, axis=1, keepdims=True)
    expo = jnp.exp(dense - top)
    size = jnp.sum(expo, axis=1, keepdims=True)
    cross = top + jnp.log(size) - jnp.sum(jnp.where(hit, dense, 0.0), axis=1, keepdims=True)
    anchor = jnp.sum(jnp.where(hit, binary, 0.0), axis=1, keepdims=True)
    margin = 1.0 - anchor + binary
    small = jnp.exp(-jnp.abs(margin))
    soft = jnp.maximum(margin, 0.0) + jnp.log1p(small)
    others = 1.0 / (dense.shape[1] - 1)
    ranking = jnp.sum(jnp.where(hit, 0.0, soft), axis=1, keepdims=True) * others
    numbers[0:1, :] = jnp.broadcast_to(total(valid * (cross + ranking)), (1, LANES))
    numbers[1:2, :] = jnp.broadcast_to(total(valid), (1, LANES))
    d_dense = valid * (expo / size - hit.astype(f32)) * scale
    rise = jnp.where(margin >= 0, 1.0, small) / (1.0 + small)
    pull = jnp.where(hit, 0.0, rise) * (valid * others)
    d_binary = (pull - jnp.where(hit, jnp.sum(pull, axis=1, keepdims=True), 0.0)) * scale
    d_asked[...] = full(d_dense, words) + full(d_binary, words) * (1.0 - hashed * hashed)
    d_codes[...] = full(d_dense, asks, TN) + full(d_binary, hashed, TN)


def loss_and_back(asked, codes, positive):
    d_asked, d_codes, numbers = call(
        loss_body,
        1,
        [fixed(asked.shape), fixed(codes.shape), fixed(positive.shape)],
        [fixed(asked.shape), fixed(codes.shape), fixed((8, LANES))],
        [(asked.shape, f32), (codes.shape, f32), ((8, LANES), f32)],
        us=5.0,
        name="loss",
    )(asked, codes, positive)
    return numbers[0, 0], numbers[1, 0], d_asked, d_codes


def halves_of(value):
    high = value.astype(bf16)
    return high, (value - high.astype(f32)).astype(bf16)


def near_full(a, b, contract=((1,), (0,))):
    return dot(a[0], b[0], contract) + (dot(a[0], b[1], contract) + dot(a[1], b[0], contract))


def block_products_body(
    paired, inverse, left, right, *rest
):
    parts, (scaled, square, turned, rows, squares) = rest[:-5], rest[-5:]

    @pl.when(pl.program_id(0) == 0)
    def _():
        squares[...] = jnp.zeros_like(squares)

    side = left.shape[-1]
    for at in range(left.shape[0]):
        grad = sum(
            (part[0][:, at * side : (at + 1) * side] if paired else part[at]).astype(f32)
            for part in parts
        )
        grad = grad * inverse[0]
        scaled[at] = grad
        grad_parts = halves_of(grad)
        square[at] = near_full(grad_parts, grad_parts, NT)
        rows[at] = near_full(grad_parts, grad_parts, TN)
        inner = near_full(grad_parts, halves_of(right[at]))
        turned[at] = near_full(halves_of(left[at]), halves_of(inner))
        squares[...] += jnp.broadcast_to(jnp.sum(grad * grad, axis=0, keepdims=True), (8, side))


def block_products(paired, parts, inverse, left, right):
    amount, side = left.shape[1], left.shape[-1]
    per = GROUP if paired else 1
    four = pl.BlockSpec((None, per, side, side), lambda i: (0, i, 0, 0))
    three = pl.BlockSpec((per, side, side), lambda i: (i, 0, 0))
    given = pl.BlockSpec((1,) + parts[0].shape[1:], lambda i: (i, 0, 0))
    return call(
        partial(block_products_body, paired),
        amount // per,
        [SMEM, four, four] + [given] * len(parts),
        [three] * 4 + [fixed((8, side))],
        [((amount, side, side), f32)] * 4 + [((8, side), f32)],
        us=10.0,
        name="block_products",
    )(inverse, left, right, *parts)


def block_update_body(
    factor, scaled, square, rows, turned, left, right, blocks, grads, left_new, right_new, new
):
    scale = factor[0]
    grads[...] = scaled[...] * scale
    left_new[...] = STAT_DECAY * left[...] + ((1.0 - STAT_DECAY) * scale * scale) * square[...]
    right_new[...] = STAT_DECAY * right[...] + ((1.0 - STAT_DECAY) * scale * scale) * rows[...]
    value = blocks[...]
    new[...] = value - SHAMPOO_RATE * (turned[...] * scale + WEIGHT_DECAY * value)


def block_update(factor, scaled, square, rows, turned, left, right, blocks):
    amount, side = left.shape[1], left.shape[-1]
    per = 3 if amount % 3 == 0 else 1
    four = pl.BlockSpec((None, per, side, side), lambda i: (0, i, 0, 0))
    three = pl.BlockSpec((per, side, side), lambda i: (i, 0, 0))
    return call(
        block_update_body,
        amount // per,
        [SMEM] + [three] * 4 + [four] * 3,
        [four] * 4,
        [(left.shape, f32)] * 4,
        us=9.0,
        name="block_update",
    )(factor, scaled, square, rows, turned, left, right, blocks)


class Slice:
    def __init__(self):
        me = lax.axis_index("blk")
        self.x, self.y, self.z = me % 2, me // 2 % 2, me // 4

    @staticmethod
    def over_x(value):
        return lax.ppermute(value, "blk", [(at, at ^ 1) for at in range(16)])

    @staticmethod
    def over_y(value):
        return lax.ppermute(value, "blk", [(at, at ^ 2) for at in range(16)])

    @staticmethod
    def over_z(value, pairs):
        return lax.ppermute(
            value, "blk", [(4 * a + at, 4 * b + at) for a, b in pairs for at in range(4)]
        )


def choose_at(value, index, axis):
    return lax.dynamic_index_in_dim(value, index, axis, keepdims=False)


def add(*values):
    return sum(value.astype(f32) for value in values)


def after(value, *others):
    return lax.optimization_barrier((value,) + others)[0]


def plane_first(links, send_one, send_two, keep_one, keep_two):
    return keep_one, links.over_y(send_one), keep_two, links.over_x(send_two)


def plane_second(links, one, got_one, two, got_two):
    def both(kept, got, index):
        shape = (-1, 2, 3) + kept.shape[1:]
        return add(*(choose_at(part.reshape(shape), index, 1) for part in (kept, got)))

    last_one = links.over_x(both(one, got_one, 1 - links.x).astype(bf16))
    last_two = links.over_y(both(two, got_two, 1 - links.y).astype(bf16))
    one = add(both(one, got_one, links.x), last_one)
    two = add(both(two, got_two, links.y), last_two)
    return jnp.concatenate([one, two], axis=1)


def column_start(links, plane, pairs):
    return links.over_z(plane.astype(bf16), pairs)


def column_step(links, at_end, first, others, pairs):
    return links.over_z(jnp.where(at_end, first, others).astype(bf16), pairs)


def own_column(links, planes):
    z = links.z
    return jnp.where(
        z < 2, jnp.where(z == 0, planes[0], planes[1]), jnp.where(z == 2, planes[2], planes[3])
    )


def adamw(weight, moment, second, grad):
    moment = BETA_ONE * moment + (1.0 - BETA_ONE) * grad
    second = BETA_TWO * second + (1.0 - BETA_TWO) * grad * grad
    update = (
        moment / (1.0 - BETA_ONE**STEP) / (jnp.sqrt(second / (1.0 - BETA_TWO**STEP)) + ADAM_EPS)
    )
    return (moment, second, weight - ADAM_RATE * (update + WEIGHT_DECAY * weight))


def on_device(
    q_tokens,
    p_tokens,
    q_lengths,
    p_lengths,
    positive,
    table,
    table_moment,
    table_second,
    blocks,
    left_stats,
    right_stats,
    left_roots,
    right_roots,
    vectors,
    vector_moment,
    vector_second,
    shared,
    shared_moment,
    shared_second,
):
    parts = lax.axis_size("blk")
    me, core = lax.axis_index("blk"), lax.axis_index("tp")
    rows_here, half = table.shape
    side = blocks.shape[-1]
    per_device = blocks.shape[1]
    even = per_device % GROUP == 0
    own_blocks = blocks[0].astype(bf16)
    in_order = list(range(ATTENTION_GROUPS + FFN_GROUPS))
    known = parts == 16 and even
    if known:
        links = Slice()
        own_groups = pack(blocks)
        at_z, over = links.z, links.over_z
        spot = jnp.stack(
            [links.x, links.y, (at_z == 0).astype(jnp.int32), (at_z == 3).astype(jnp.int32), core]
        )
        down_one, down_own = over(own_groups, [(3, 2), (2, 1)]), over(own_groups, [(2, 3)])
        up_one, up_own = over(own_groups, [(0, 1), (1, 2)]), over(own_groups, [(1, 0)])
    elif even:
        groups = lax.all_gather(pair_blocks(own_blocks), "blk", axis=0, tiled=True)
    else:
        groups = pair_blocks(lax.all_gather(own_blocks, "blk", axis=0, tiled=True))
    if not known:
        spot = jnp.zeros((5,), jnp.int32).at[4].set(core)
        layer_groups = [(groups[: len(in_order)],), (groups[len(in_order) :],)]
        orders = [in_order, in_order]

    q_live = (jnp.arange(q_tokens.shape[1])[None, :] < q_lengths[:, None]).reshape(-1)
    p_live = (jnp.arange(p_tokens.shape[1])[None, :] < p_lengths[:, None]).reshape(-1)
    tokens = jnp.concatenate([q_tokens.reshape(-1), p_tokens.reshape(-1)])
    live = jnp.concatenate([q_live, p_live])
    tall = -(-rows_here // LANES)
    owner = tokens // rows_here
    inside = tokens - owner * rows_here
    high = jnp.where(live, owner * tall + inside // LANES, -1)
    high_hot = (high[:, None] == jnp.arange(parts * tall)[None, :]).astype(bf16)
    low_hot = (inside[:, None] % LANES == jnp.arange(LANES)[None, :]).astype(bf16)
    uses = jnp.einsum("th,tl->hl", high_hot, low_hot, preferred_element_type=f32)
    present = (uses > 0).reshape(parts, tall, LANES)
    slots, wanted = slot_map(present)
    token_slot = jnp.sum(
        jnp.dot(high_hot.astype(f32), slots.reshape(-1, LANES), precision=PRECISION_MAX) * low_hot,
        axis=1,
    )
    rounds_here = jnp.ceil(jnp.max(wanted) / SLOTS)

    small = jnp.concatenate(
        [
            vectors.astype(bf16).reshape(-1),
            shared.astype(bf16).reshape(-1),
            rounds_here.astype(bf16)[None],
        ]
    )
    small_size = -(-small.shape[0] // LANES) * LANES
    small = jnp.pad(small, (0, small_size - small.shape[0])).reshape(-1, LANES)
    table_low = jnp.pad(table.astype(bf16), ((0, tall * LANES - rows_here), (0, 0)))
    length = p_tokens.shape[1]
    q_length = q_tokens.shape[1]
    share = length // parts
    margin = jnp.zeros((length, half), bf16)
    first_place = jnp.clip(VOCAB - me * rows_here + length, 0, rows_here + length)
    places_here = lax.dynamic_slice_in_dim(
        jnp.concatenate([margin, table_low[:rows_here], margin]), first_place, length, 0
    )
    asks = jnp.concatenate(
        [
            present.astype(bf16),
            jnp.broadcast_to(small[None], (parts,) + small.shape),
            places_here.reshape(parts, share * half // LANES, LANES),
        ],
        axis=1,
    )
    if known:
        asks, down_one, down_own, up_one, up_own = lax.optimization_barrier(
            (asks, down_one, down_own, up_one, up_own)
        )
        down_two, up_two = over(down_one, [(1, 0), (2, 1)]), over(up_one, [(2, 3), (1, 2)])
    asks = lax.all_to_all(asks, "blk", 0, 0)
    if known:
        asks, down_two, up_two = lax.optimization_barrier((asks, down_two, up_two))
        down_three, up_three = over(down_two, [(1, 0)]), over(up_two, [(2, 3)])
        pick_at = lambda *values: jnp.where(
            at_z < 2,
            jnp.where(at_z == 0, values[0], values[1]),
            jnp.where(at_z == 2, values[2], values[3]),
        )
        later_one = pick_at(down_two, down_one, own_groups, own_groups)
        near_one = gather_near(links, later_one)
    asked_slots, _ = slot_map(asks[:, :tall] > 0)
    place_share = jnp.sum(asks[:, tall + small.shape[0] :].astype(f32), axis=0).astype(bf16)
    place_share = place_share.reshape(share, half)
    small = asks[:, tall : tall + small.shape[0]].reshape(parts, -1)
    vector_part, shared_part = vectors.shape[2], shared.shape[1]
    vector_size, shared_size = vectors.size, shared.size
    bias_all = (
        small[:, :vector_size]
        .reshape(parts, LAYERS, vector_part)
        .transpose(1, 0, 2)
        .reshape(LAYERS, -1)
        .astype(f32)
    )
    params_all = (
        small[:, vector_size : vector_size + shared_size]
        .reshape(parts, -1, shared_part)
        .transpose(1, 0, 2)
        .reshape(-1, parts * shared_part)
        .astype(f32)
    )
    rounds = jnp.max(small[:, vector_size + shared_size].astype(f32)).astype(jnp.int32)

    per_part = -(-(LAYERS * (vectors.shape[2] * parts // half) + 2 * shared.shape[0]) // parts)
    width = -(-(SLOTS + share + per_part) // 16) * 16

    def choose(start):
        return pick(asked_slots, start, width)

    def serve(chosen):
        return jnp.einsum("sjr,rc->sjc", chosen, table_low, preferred_element_type=f32).astype(bf16)

    def places_of(start):
        place = token_slot - start
        fits = (high >= 0) & (place >= 0) & (place < SLOTS)
        return jnp.where(fits, owner * width + place.astype(jnp.int32), -1)

    def spread(start):
        return (places_of(start)[:, None] == jnp.arange(parts * width)[None, :]).astype(bf16)

    places_first = places_of(0.0)
    place_at = jnp.arange(length)
    places_first = jnp.concatenate(
        [places_first, place_at // share * width + SLOTS + place_at % share]
    )
    place_rows = places_first[: tokens.shape[0]].reshape(-1, 1, length)
    place_columns = places_first[:, None]

    sent = jnp.concatenate(
        [
            serve(choose(0.0))[:, :SLOTS],
            jnp.broadcast_to(place_share[None], (parts, share, half)),
            jnp.zeros((parts, width - SLOTS - share, half), bf16),
        ],
        axis=1,
    )
    if known:
        sent, down_three, up_three, *near_one = lax.optimization_barrier(
            (sent, down_three, up_three) + near_one
        )
        far_one = gather_far(links, *near_one)
        later_two = pick_at(down_three, down_two, down_one, down_own)
        near_two = gather_near(links, later_two)
    fetched = lax.all_to_all(sent, "blk", 0, 0)
    if known:
        place_columns, place_rows, far_two, near_two = lax.optimization_barrier(
            (place_columns, place_rows, far_one, near_two)
        )
        far_one = far_two
        far_two = gather_far(links, *near_two)
    halves = expand(length, place_columns, fetched.reshape(-1, half))

    def fetch_more(carry):
        done, total = carry
        start = (done * SLOTS).astype(f32)
        more = lax.all_to_all(serve(choose(start)), "blk", 0, 0).reshape(-1, half)
        more = jnp.dot(spread(start), more, preferred_element_type=f32).astype(bf16)
        return done + 1, total.at[: tokens.shape[0]].add(more)

    if known:
        halves, *far_two = lax.optimization_barrier((halves,) + far_two)
        layer_groups = [
            None, (later_one, *near_one, *far_one, later_two, *near_two, *far_two)
        ]
        orders = [0, 1]
        early_one = pick_at(own_groups, own_groups, up_one, up_two)
        early_two = pick_at(up_own, up_one, up_two, up_three)
    halves = lax.while_loop(lambda c: c[0] < rounds, fetch_more, (jnp.int32(1), halves))[1]
    others = other_core(halves)
    embed_params = params_all[:2]
    q_blocks, p_blocks = q_tokens.size // length, p_tokens.size // length

    def first_half(layer, seg, first, count, lengths):
        bias = bias_all[layer : layer + 1]
        params = params_all[2 + 6 * layer : 8 + 6 * layer]
        return [layer, seg, lengths, bias, params] + list(attention_forward(
            layer, seg, length, count, first, lengths, spot, halves, others,
            layer_groups[layer], orders[layer], bias, embed_params,
        ))

    def second_half(kept):
        layer, seg, lengths, bias, params, state, qkv, context, logs, own_one = kept
        other_one = other_core(own_one)
        return kept + [other_one] + list(ffn_forward(
            layer, tall_rows(state), spot, state, own_one, other_one, layer_groups[layer],
            orders[layer], bias, params,
        ))

    def pool_of(kept):
        layer, seg, lengths, _, params = kept[:5]
        hidden, _, _, own_two = kept[11:]
        other_two = other_core(own_two)
        kept.append(other_two)
        return pool_forward(layer, seg, length, lengths, hidden, own_two, other_two, params)

    if known:
        near_one = gather_near(links, early_one)
    p_kept = first_half(1, length, q_blocks, p_blocks, p_lengths)
    if known:
        p_kept[-1], *near_one = lax.optimization_barrier((p_kept[-1],) + near_one)
        far_one = gather_far(links, *near_one)
        near_two = gather_near(links, early_two)
    p_kept = second_half(p_kept)
    if known:
        p_kept[-1], *four = lax.optimization_barrier((p_kept[-1],) + far_one + near_two)
        far_one, near_two = four[:2], four[2:]
        far_two = gather_far(links, *near_two)
    p_pooled = pool_of(p_kept)
    if known:
        p_pooled, *far_two = lax.optimization_barrier((p_pooled,) + far_two)
        layer_groups[0] = (early_one, *near_one, *far_one, early_two, *near_two, *far_two)
    q_kept = second_half(first_half(0, q_length, 0, q_blocks, q_lengths))
    pooled = [pool_of(q_kept), p_pooled]
    asked_local = pooled[0]
    codes_local = jnp.tanh(pooled[1])
    codes_low = codes_local.astype(bf16)
    every = to_all(
        jnp.concatenate(
            [
                asked_local,
                codes_low.astype(f32),
                jnp.pad(positive.astype(f32)[None], ((0, 0), (0, MODEL_WIDTH - positive.shape[0]))),
            ]
        ),
        parts,
    )
    q_part, p_part = asked_local.shape[0], codes_local.shape[0]
    asked = every[:, :q_part].reshape(-1, MODEL_WIDTH)
    codes = every[:, q_part : q_part + p_part].reshape(-1, MODEL_WIDTH)
    positives = every[:, q_part + p_part, :q_part].reshape(-1).astype(jnp.int32)
    loss_sum, positives_count, d_asked, d_codes = loss_and_back(asked, codes, positives[:, None])
    d_asked = lax.dynamic_slice_in_dim(d_asked, me * q_part, q_part, 0)
    d_codes = lax.dynamic_slice_in_dim(d_codes, me * p_part, p_part, 0)
    d_passages = d_codes * (1.0 - codes_local * codes_local)
    def ffn_back(kept, d_pooled, sets):
        (layer, seg, lengths, bias, params, state, qkv, context, logs, own_one, other_one, hidden,
         active, slope, own_two, other_two) = kept
        return ffn_backward(
            layer, seg, tall_rows(hidden), lengths, spot, d_pooled, hidden, own_two, other_two, active, slope,
            layer_groups[layer], orders[layer], params, sets,
        )

    def attention_back(kept, base, back_own, back_other, first, count, **more):
        (layer, seg, lengths, bias, params, state, qkv, context, logs, own_one, other_one) = kept[:11]
        return attention_backward(
            layer, seg, length, first, count, lengths[first:] if first else lengths, spot, base,
            back_own, back_other, state, own_one, other_one, qkv, context, logs,
            layer_groups[layer], orders[layer], params, **more,
        )

    q_base, q_back, q_ffn_sums, q_up_bias, *q_ffn = ffn_back(
        q_kept, d_asked, ((0, 1),) if known else None
    )
    q_state, q_state_own, q_sums, q_bias, *q_attention = attention_back(
        q_kept, q_base, q_back, other_core(q_back), 0, q_blocks,
        **(dict(planes=(0, 1), buffers=q_ffn) if known else {}),
    )
    p_base, p_back, p_ffn_sums, p_up_bias, *p_ffn = ffn_back(
        p_kept, after(d_passages, q_sums), ((0,), (1,)) if known else None
    )
    if known:
        early = p_blocks // 2
        q_first = plane_first(links, *q_attention)
        top_first = plane_first(links, *p_ffn[4:])
        p_back, *q_first = lax.optimization_barrier((p_back,) + q_first)
        p_back_other = other_core(p_back)
        q_planes = plane_second(links, *q_first)
        state_one, own_one, *carry = attention_back(
            p_kept, p_base, p_back, p_back_other, 0, early, carry_out=True
        )
        carry = carry[2:] + carry[:2]
        other_one = other_core(own_one)
        carry[2], q_planes, *top_first = lax.optimization_barrier(
            (carry[2], q_planes) + top_first
        )
        top_plane = plane_second(links, *top_first)[0]
        down = column_start(links, q_planes[0], [(3, 2)])
        state_two, own_two, p_sums, p_bias, *low = attention_back(
            p_kept, p_base, p_back, p_back_other, early, p_blocks - early, carry=carry,
            planes=(0,), buffers=p_ffn[:4],
        )
        own_two, top_plane, down = lax.optimization_barrier((own_two, top_plane, down))
        other_two = other_core(own_two)
        up = column_start(links, top_plane, [(0, 1)])
        down = column_step(
            links, links.z == 3, q_planes[1], add(q_planes[0], down), [(3, 2), (2, 1)]
        )
        low_first = plane_first(links, *low)
        state_p = ((state_one, state_two), (own_one, own_two), (other_one, other_two))
        low_first = plane_first(links, *low)
    else:
        p_back_other = other_core(p_back)
        state_one, own_one, p_sums, p_bias, *p_attention = attention_back(
            p_kept, p_base, p_back, p_back_other, 0, p_blocks
        )
        state_p = ((state_one,), (own_one,), (other_core(own_one),))
    smalls = (
        q_bias, q_up_bias, p_bias, p_up_bias, q_sums, q_ffn_sums, p_sums, p_ffn_sums
    )
    vector_rows = LAYERS * vector_part * parts // half
    state_parts = [
        (q_state, q_state_own, other_core(q_state_own)),
        state_p,
    ]
    picked, _ = embed_backward(
        (q_length, length), length, state_parts[0], state_parts[1], smalls, halves, others, place_rows,
        spot, embed_params, parts, width,
    )
    if known:
        picked, up, down, *low_first = lax.optimization_barrier((picked, up, down) + low_first)

    def gather_up(start):
        return embed_backward(
            (q_length, length), length, state_parts[0], state_parts[1], smalls, halves, others,
            places_of(start).reshape(-1, 1, length), spot, embed_params, parts, width,
        )[0].reshape(parts, width, half)

    def put_back(chosen, received):
        return jnp.einsum("sjr,sjc->rc", chosen, received, preferred_element_type=f32)[:rows_here]

    sent = picked.reshape(parts, width, half)
    got = lax.all_to_all(sent, "blk", 0, 0)
    token_grad = put_back(choose(0.0), got)

    def send_more(carry):
        done, total = carry
        start = (done * SLOTS).astype(f32)
        more = lax.all_to_all(gather_up(start), "blk", 0, 0)
        return done + 1, total + put_back(choose(start), more)

    token_grad = lax.while_loop(lambda c: c[0] < rounds, send_more, (jnp.int32(1), token_grad))[1]
    rest = jnp.sum(got[:, SLOTS : SLOTS + share + per_part].astype(f32), axis=0)
    if known:
        low_plane = plane_second(links, *low_first)[0]
        z = links.z
        planes = [q_planes[0], q_planes[1], low_plane, top_plane]
        up = column_step(links, z == 0, low_plane, add(top_plane, up), [(0, 1), (1, 2)])
        down = column_step(
            links, z == 3, low_plane, add(jnp.where(z == 2, q_planes[1], q_planes[0]), down),
            [(3, 2), (2, 1), (1, 0)],
        )
        base = lax.optimization_barrier(
            jnp.where(z == 0, q_planes[1], jnp.where(z == 1, low_plane, top_plane))
        )
        up = links.over_z(
            (base + jnp.where(z == 0, 0.0, up.astype(f32))).astype(bf16),
            [(0, 1), (1, 2), (2, 3)],
        )
        grad_parts = (own_column(links, planes), up, down)
    else:
        all_groups = jnp.concatenate(q_attention + q_ffn + p_attention + p_ffn, axis=0)
        if not even:
            all_groups = split_pairs(all_groups)
        grad_parts = (lax.psum_scatter(all_groups, "blk", scatter_dimension=0, tiled=True),)
    inverse = 1.0 / positives_count
    rest = rest * inverse
    row_index = me * per_part + jnp.arange(per_part)
    counted = ((row_index < vector_rows) | (core == 0)).astype(f32)
    squares = (
        jnp.sum(rest[:share] ** 2)
        + jnp.sum(rest[share:] ** 2 * counted[:, None])
        + jnp.sum((token_grad * inverse) ** 2)
    )
    rest = to_all(rest, parts)
    if known:
        squares, *grad_parts = lax.optimization_barrier((squares,) + grad_parts)
    scaled, square, turned, row_square, block_squares = block_products(
        even, grad_parts, inverse[None], left_roots, right_roots
    )
    block_squares, rest = lax.optimization_barrier((block_squares, rest))
    place_grads = rest[:, :share].reshape(length, half)
    small_grads = rest[:, share:].reshape(-1, half)
    grad_vectors = lax.dynamic_slice_in_dim(
        small_grads[:vector_rows].reshape(LAYERS, -1), me * vector_part, vector_part, 1
    )[None]
    shared_rows = shared.shape[0]
    grad_shared = lax.dynamic_slice_in_dim(
        jnp.concatenate(
            [
                small_grads[vector_rows : vector_rows + shared_rows],
                small_grads[vector_rows + shared_rows : vector_rows + 2 * shared_rows],
            ],
            axis=1,
        ),
        me * shared_part,
        shared_part,
        1,
    )
    margin = jnp.zeros((rows_here, half), f32)
    place_grads = lax.dynamic_slice_in_dim(
        jnp.concatenate([margin, place_grads, margin]),
        jnp.clip(me * rows_here - VOCAB + rows_here, 0, rows_here + length),
        rows_here,
        0,
    )
    table_grad = token_grad * inverse + place_grads
    squares = squares + jnp.sum(block_squares[0])
    devices = parts * 2
    squares = lax.all_to_all(
        jnp.broadcast_to(squares, (devices, 8, LANES)), ("blk", "tp"), 0, 0
    )
    squares = jnp.sum(squares[:, 0, 0])
    grad_norm = jnp.sqrt(squares)
    factor = jnp.minimum(1.0, CLIP / grad_norm)
    block_grads, left_new, right_new, blocks_new = block_update(
        factor[None], scaled, square, row_square, turned, left_stats, right_stats, blocks
    )
    table_moment_new, table_second_new, table_new = adamw(
        table, table_moment, table_second, table_grad * factor
    )
    vector_moment_new, vector_second_new, vectors_new = adamw(
        vectors, vector_moment, vector_second, grad_vectors * factor
    )
    shared_moment_new, shared_second_new, shared_new = adamw(
        shared, shared_moment, shared_second, grad_shared * factor
    )
    return (
        loss_sum,
        positives_count,
        grad_norm,
        block_grads,
        left_new,
        right_new,
        blocks_new,
        table_moment_new,
        table_second_new,
        table_new,
        vector_moment_new,
        vector_second_new,
        vectors_new,
        shared_moment_new,
        shared_second_new,
        shared_new,
    )


def solution(mesh):
    return jax.shard_map(
        on_device,
        mesh=mesh,
        in_specs=(
            P("blk", None),
            P("blk", None),
            P("blk"),
            P("blk"),
            P("blk"),
            P("blk", "tp"),
            P("blk", "tp"),
            P("blk", "tp"),
            P("tp", "blk", None, None),
            P("tp", "blk", None, None),
            P("tp", "blk", None, None),
            P("tp", "blk", None, None),
            P("tp", "blk", None, None),
            P("tp", None, "blk"),
            P("tp", None, "blk"),
            P("tp", None, "blk"),
            P(None, "blk"),
            P(None, "blk"),
            P(None, "blk"),
        ),
        out_specs=(
            P(),
            P(),
            P(),
            P("tp", "blk", None, None),
            P("tp", "blk", None, None),
            P("tp", "blk", None, None),
            P("tp", "blk", None, None),
            P("blk", "tp"),
            P("blk", "tp"),
            P("blk", "tp"),
            P("tp", None, "blk"),
            P("tp", None, "blk"),
            P("tp", None, "blk"),
            P(None, "blk"),
            P(None, "blk"),
            P(None, "blk"),
        ),
        check_vma=False,
    )
```

```python
from functools import partial

import jax
import jax.numpy as jnp
from jax import lax
from jax.experimental import pallas as pl
from jax.experimental.pallas import tpu as pltpu
from jax.sharding import PartitionSpec as P

bf16, f32 = jnp.bfloat16, jnp.float32
MODEL_WIDTH = 768
HALF = MODEL_WIDTH // 2
HD = 64
FF = 3072
UNITS = FF // 2
NORM_EPS = 1e-06
VMEM_LIMIT = 60 * 1024 * 1024
LAYERS = 2
STEP = 10
VOCAB = 30522
CLIP = 0.05
BETA_ONE = 0.9
BETA_TWO = 0.999
STAT_DECAY = 0.95
ADAM_RATE = 0.5
SHAMPOO_RATE = 0.5
WEIGHT_DECAY = 0.01
ADAM_EPS = 1e-08
PRECISION_MAX = lax.Precision.HIGHEST
GROUP = 2
SLOTS = 92
LANES = 128

TAIL = (
    0.16918798443114483,
    0.17071555704933744,
    0.14833696008811015,
    0.2149342153930891,
    -0.09466890560267835,
    0.5477451349382827,
    -0.5122991151213244,
    0.4855729957946344,
    -0.12952484655737367,
)


def gelu_parts(u):
    t = 1.0 / (1.0 + (0.3 * 0.5**0.5) * jnp.abs(u))
    poly = jnp.full_like(t, TAIL[-1])
    for term in TAIL[-2::-1]:
        poly = poly * t + term
    bell = jnp.exp(u * u * -0.5)
    tail = (0.5 * t) * poly * bell
    below = jnp.where(u >= 0, 1.0 - tail, tail)
    return u * below, below + u * (bell * 0.3989422804014327)


def dot(a, b, contract=((1,), (0,))):
    return lax.dot_general(a, b, (contract, ((), ())), preferred_element_type=f32)


NT = ((1,), (1,))
TN = ((0,), (0,))


def unit(value):
    centred = value - jnp.mean(value, axis=-1, keepdims=True)
    rate = lax.rsqrt(jnp.mean(centred * centred, axis=-1, keepdims=True) + NORM_EPS)
    return centred * rate, rate


def unit_back(grad, hat, rate):
    return rate * (
        grad
        - jnp.mean(grad, axis=-1, keepdims=True)
        - hat * jnp.mean(grad * hat, axis=-1, keepdims=True)
    )


def total(value):
    return jnp.sum(value, axis=0, keepdims=True)


def row_lengths(lengths, rows, axis, seg, shape):
    index = lax.broadcasted_iota(jnp.int32, shape, axis)
    if seg == rows:
        return index, None, lengths[pl.program_id(0)]
    which = index // seg
    length = jnp.zeros(shape, jnp.int32)
    before = pl.program_id(0) * (rows // seg)
    for place in range(rows // seg):
        length = jnp.where(which == place, lengths[before + place], length)
    return index - which * seg, which, length


def row_live(lengths, rows, seg):
    place, _, length = row_lengths(lengths, rows, 0, seg, (rows, 1))
    return (place < length).astype(f32), length


def key_mask(lengths, rows, seg):
    if seg == rows:
        place, _, length = row_lengths(lengths, rows, 1, seg, (1, rows))
        return place < length
    place, which, length = row_lengths(lengths, rows, 1, seg, (rows, rows))
    mine = lax.broadcasted_iota(jnp.int32, (rows, rows), 0) // seg
    return (which == mine) & (place < length)


def key_mask_across(lengths, rows, seg):
    place, which, length = row_lengths(lengths, rows, 0, seg, (rows, 1))
    if seg == rows:
        return place < length
    mine = lax.broadcasted_iota(jnp.int32, (rows, rows), 1) // seg
    return (which == mine) & (place < length)


def load_weights(groups, order, first, spot, mats, sem):
    side, wide = groups[0].shape[1:]
    starts, waits, at = [], [], 0
    for mat in mats:
        for row in range(mat.shape[0] // side):
            for column in range(mat.shape[1] // wide):
                to = mat.at[row * side : (row + 1) * side, column * wide : (column + 1) * wide]
                if len(groups) == 1:
                    choices = [(None, groups[0].at[order[first + at]])]
                else:
                    choices = group_choices(groups, order, first + at, spot)
                copies = [
                    (where, pltpu.make_async_copy(part, to, sem.at[at])) for where, part in choices
                ]
                starts += copies
                waits.append(copies[0][1])
                at += 1
    for where, copy in starts:
        if where is None:
            copy.start()
        else:
            pl.when(where)(copy.start)
    for copy in waits:
        copy.wait()


def group_choices(groups, layer, group, spot):
    owner, place = divmod(group, 6)
    plane, own_y, own_x = owner // 4, owner // 2 % 2, owner % 2
    is_first = spot[2 + layer] == (0 if plane == 1 - layer else 1)
    far_x, far_y = spot[0] != own_x, spot[1] != own_y
    near_x, near_y = jnp.logical_not(far_x), jnp.logical_not(far_y)
    part, rest = divmod(place, 3)
    choices = []
    for here, (own, by_x, by_y, *both) in (
        (is_first, groups[:5]),
        (jnp.logical_not(is_first), groups[5:]),
    ):
        choices += [
            (here & near_x & near_y, own.at[place]),
            (here & far_x & near_y, by_x.at[place]),
            (here & near_x & far_y, by_y.at[place]),
            (here & far_x & far_y, both[part].at[rest]),
        ]
    return choices


def gather_near(links, piece):
    return links.over_x(piece), links.over_y(piece)


def gather_far(links, by_x, by_y):
    half = by_x.shape[0] // 2
    return links.over_y(by_x[:half]), links.over_x(by_y[half:])


def store_groups(mats, lows, grads, sem):
    side, wide = grads.shape[1:]
    copies, at = [], 0
    for mat, low in zip(mats, lows):
        low[...] = mat[...].astype(bf16)
        for row in range(mat.shape[0] // side):
            for column in range(mat.shape[1] // wide):
                part = low.at[row * side : (row + 1) * side, column * wide : (column + 1) * wide]
                copies.append(pltpu.make_async_copy(part, grads.at[at], sem.at[at]))
                at += 1
    for copy in copies:
        copy.start()
    for copy in copies:
        copy.wait()


def store_planes(first, mats, lows, spot, sets, sem):
    side, wide = sets[0][1].shape[-2:]
    count = 3
    copies, at = [], 0
    for mat, low in zip(mats, lows):
        low[...] = mat[...].astype(bf16)
        for row in range(mat.shape[0] // side):
            for column in range(mat.shape[1] // wide):
                owner, place = divmod(first + at, 2 * count)
                plane, own_y, own_x = owner // 4, owner // 2 % 2, owner % 2
                planes, *refs = next(item for item in sets if plane in item[0])
                plane = planes.index(plane)
                by_y = place < count
                mine = spot[1] == own_y if by_y else spot[0] == own_x
                index = (plane * 2 + (own_x if by_y else own_y)) * count + place % count
                send, keep = (refs[0], refs[2]) if by_y else (refs[1], refs[3])
                region = (
                    slice(row * side, (row + 1) * side),
                    slice(column * wide, (column + 1) * wide),
                )
                copies.append(
                    (mine, pltpu.make_async_copy(mat.at[region], keep.at[index], sem.at[at]))
                )
                copies.append(
                    (
                        jnp.logical_not(mine),
                        pltpu.make_async_copy(low.at[region], send.at[index], sem.at[at]),
                    )
                )
                at += 1
    for where, copy in copies:
        pl.when(where)(copy.start)
    for where, copy in copies:
        pl.when(where)(copy.wait)


def head_lanes(rows):
    return lax.broadcasted_iota(jnp.int32, (rows, 2 * HD), 1) < HD


def embedded(seg, spot, mine, theirs, place_mine, place_theirs):
    rows = mine.shape[0]

    def side_of(ref, places):
        place = jnp.concatenate([places[:seg].astype(f32)] * (rows // seg), axis=0)
        return ref[...].astype(f32) + place

    own, other = side_of(mine, place_mine), side_of(theirs, place_theirs)
    first = spot[4] == 0
    return jnp.concatenate([jnp.where(first, own, other), jnp.where(first, other, own)], axis=1)


def attention_forward_body(
    seg, order, lengths, spot, mine, theirs, place_mine, place_theirs, bias, params, *rest,
):
    groups, rest = rest[:-8], rest[-8:]
    state, qkv, context, logs, out, joint, output_weight, sem = rest
    rows = mine.shape[0]

    @pl.when(pl.program_id(0) == 0)
    def _():
        load_weights(groups, order, 0, spot, (joint, output_weight), sem)

    hat, _ = unit(embedded(seg, spot, mine, theirs, place_mine, place_theirs))
    value = hat * params[0:1] + params[1:2]
    state[...] = value
    projected = dot(value.astype(bf16), joint[...])
    shift = jnp.concatenate(
        [bias[:, :HALF], jnp.zeros((1, HALF), f32), bias[:, HALF : 2 * HALF]], axis=1
    )
    projected = (projected + shift).astype(bf16)
    qkv[...] = projected
    mask = key_mask(lengths, rows, seg)
    first = head_lanes(rows)
    contexts = []
    for pair in range(HALF // (2 * HD)):
        lanes = slice(pair * 2 * HD, (pair + 1) * 2 * HD)
        query = projected[:, :HALF][:, lanes] * jnp.asarray(HD**-0.5, bf16)
        key = projected[:, HALF : 2 * HALF][:, lanes]
        what = projected[:, 2 * HALF :][:, lanes]
        sides = []
        for head in range(2):
            only = jnp.where(first if head == 0 else ~first, query, jnp.zeros_like(query))
            scores = jnp.where(mask, dot(only, key, NT), -1e30)
            top = jnp.max(scores, axis=-1, keepdims=True)
            expo = jnp.exp(scores - top)
            size = jnp.sum(expo, axis=-1, keepdims=True)
            logs[:, 2 * pair + head : 2 * pair + head + 1] = top + jnp.log(size)
            sides.append(dot((expo * (1.0 / size)).astype(bf16), what))
        contexts.append(jnp.where(first, sides[0], sides[1]))
    contexts = jnp.concatenate(contexts, axis=1).astype(bf16)
    context[...] = contexts
    out[...] = dot(contexts, output_weight[...]).astype(bf16)


def forward_ffn_body(
    order, spot, state, own, other, bias, params, *rest,
):
    groups, rest = rest[:-7], rest[-7:]
    hidden, active, slope, out, up_weight, down_weight, sem = rest
    wide = groups[0].shape[2]

    @pl.when(pl.program_id(0) == 0)
    def _():
        load_weights(groups, order, ATTENTION_GROUPS, spot, (up_weight, down_weight), sem)

    hat, _ = unit(state[...] + (own[...].astype(f32) + other[...].astype(f32)) + params[0:1])
    value = hat * params[1:2] + params[2:3]
    hidden[...] = value
    low = value.astype(bf16)
    step = 2 * wide if UNITS % (2 * wide) == 0 else wide
    result = jnp.zeros(out.shape, f32)
    for start in range(0, UNITS, step):
        columns = slice(start, start + step)
        up = dot(low, up_weight[:, columns]) + bias[:, 2 * HALF + start : 2 * HALF + start + step]
        act, rise = gelu_parts(up)
        act = act.astype(bf16)
        active[:, columns] = act
        slope[:, columns] = rise.astype(bf16)
        result = result + dot(act, down_weight[columns, :])
    out[...] = result.astype(bf16)


def pool_body(seg, lengths, hidden, own, other, params, out):
    rows = hidden.shape[0]
    hat, _ = unit(hidden[...] + (own[...].astype(f32) + other[...].astype(f32)) + params[3:4])
    output = hat * params[4:5] + params[5:6]
    live, _ = row_live(lengths, rows, seg)
    output = output * live
    for place in range(rows // seg):
        index = pl.program_id(0) * (rows // seg) + place
        mean = total(output[place * seg : (place + 1) * seg]) / lengths[index].astype(f32)
        out[pl.ds(index, 1), :] = mean


def ffn_backward_body(
    seg, order, sets, amount, lengths, spot, d_pooled, hidden, own, other, active, slope, params,
    *rest,
):
    groups, rest = rest[:amount], rest[amount:]
    base, out, sums, d_bias, *rest = rest
    grads, (up_weight, down_weight, d_up, d_down, sem) = tuple(rest[:-5]), rest[-5:]
    rows = hidden.shape[0]
    wide = groups[0].shape[2]
    step_at, last = pl.program_id(0), pl.num_programs(0) - 1

    @pl.when(step_at == 0)
    def _():
        load_weights(groups, order, ATTENTION_GROUPS, spot, (up_weight, down_weight), sem)
        d_up[...] = jnp.zeros_like(d_up)
        d_down[...] = jnp.zeros_like(d_down)
        sums[...] = jnp.zeros_like(sums)
        d_bias[...] = jnp.zeros_like(d_bias)

    live, length = row_live(lengths, rows, seg)
    pooled = jnp.concatenate(
        [
            jnp.broadcast_to(
                d_pooled[pl.ds(step_at * (rows // seg) + place, 1), :], (seg, MODEL_WIDTH)
            )
            for place in range(rows // seg)
        ],
        axis=0,
    )
    d_output = pooled / length.astype(f32) * live
    value = hidden[...]
    hat, rate = unit(value + (own[...].astype(f32) + other[...].astype(f32)) + params[3:4])
    d_sum = unit_back(d_output * params[4:5], hat, rate)
    base[...] = d_sum
    sums[0:1, :] += total(d_sum)
    sums[1:2, :] += total(d_output * hat)
    sums[2:3, :] += total(d_output)
    low = d_sum.astype(bf16)
    hidden_low = value.astype(bf16)
    step = 2 * wide if UNITS % (2 * wide) == 0 else wide
    result = jnp.zeros(out.shape, f32)
    for start in range(0, UNITS, step):
        columns = slice(start, start + step)
        d_down[columns, :] += dot(active[:, columns], low, TN)
        d_act = dot(low, down_weight[columns, :], NT)
        d_pre = (d_act * slope[:, columns].astype(f32)).astype(bf16)
        d_bias[:, columns] += total(d_pre.astype(f32))
        d_up[:, columns] += dot(hidden_low, d_pre, TN)
        result = result + dot(d_pre, up_weight[:, columns], NT)
    out[...] = result.astype(bf16)

    @pl.when(step_at == last)
    def _():
        mats, lows = (d_up, d_down), (up_weight, down_weight)
        if sets is None:
            store_groups(mats, lows, grads[0], sem)
        else:
            to = [(planes,) + grads[4 * at : 4 * at + 4] for at, planes in enumerate(sets)]
            store_planes(ATTENTION_GROUPS, mats, lows, spot, to, sem)


def attention_backward_body(
    seg, order, planes, carry_in, carry_out, amount, lengths, spot, carried, back_own, back_other,
    state, own, other, qkv, context, logs, params, *rest,
):
    groups, rest = rest[:amount], rest[amount:]
    joint, output_weight, d_joint, d_output_weight, sem = rest[-5:]
    carry, rest = (rest[:4], rest[4:-5]) if carry_in else (None, rest[:-5])
    if planes is not None and not carry_out:
        rest = rest[4:]
    base, out, sums, d_bias, *results = rest
    rows = state.shape[0]
    step_at, last = pl.program_id(0), pl.num_programs(0) - 1

    @pl.when(step_at == 0)
    def _():
        load_weights(groups, order, 0, spot, (joint, output_weight), sem)
        if carry is None:
            d_joint[...] = jnp.zeros_like(d_joint)
            d_output_weight[...] = jnp.zeros_like(d_output_weight)
            sums[...] = jnp.zeros_like(sums)
            d_bias[...] = jnp.zeros_like(d_bias)
        else:
            copies = [
                pltpu.make_async_copy(carry[0], d_joint, sem.at[0]),
                pltpu.make_async_copy(carry[1], d_output_weight, sem.at[1]),
            ]
            for copy in copies:
                copy.start()
            for copy in copies:
                copy.wait()
            sums[...] = carry[2][...]
            d_bias[...] = carry[3][...]

    d_hidden = carried[...] + (back_own[...].astype(f32) + back_other[...].astype(f32))
    value = state[...]
    hat, rate = unit(value + (own[...].astype(f32) + other[...].astype(f32)) + params[0:1])
    d_sum = unit_back(d_hidden * params[1:2], hat, rate)
    base[...] = d_sum
    sums[0:1, :] += total(d_sum)
    sums[1:2, :] += total(d_hidden * hat)
    sums[2:3, :] += total(d_hidden)
    low = d_sum.astype(bf16)
    d_output_weight[...] += dot(context[...], low, TN)
    d_context = dot(low, output_weight[...], NT).astype(bf16)
    mask = key_mask_across(lengths, rows, seg)
    logs_across = jnp.transpose(logs[...])
    first = head_lanes(rows)
    d_queries, d_keys, d_values = [], [], []
    for pair in range(HALF // (2 * HD)):
        lanes = slice(pair * 2 * HD, (pair + 1) * 2 * HD)
        query = qkv[:, pair * 2 * HD : (pair + 1) * 2 * HD] * jnp.asarray(HD**-0.5, bf16)
        key = qkv[:, HALF + pair * 2 * HD : HALF + (pair + 1) * 2 * HD]
        what = qkv[:, 2 * HALF + pair * 2 * HD : 2 * HALF + (pair + 1) * 2 * HD]
        d_pair = d_context[:, lanes]
        sides = []
        for head in range(2):
            mine = first if head == 0 else ~first
            only = jnp.where(mine, query, jnp.zeros_like(query))
            d_only = jnp.where(mine, d_pair, jnp.zeros_like(d_pair))
            scores = jnp.where(mask, dot(key, only, NT), -1e30)
            weights = jnp.exp(scores - logs_across[2 * pair + head : 2 * pair + head + 1, :])
            spread = weights * dot(what, d_only, NT)
            d_scores = spread - weights * total(spread)
            d_scores = d_scores.astype(bf16)
            sides.append(
                (
                    dot(d_scores, key, TN),
                    dot(d_scores, query),
                    dot(weights.astype(bf16), d_pair),
                )
            )
        d_queries.append(jnp.where(first, sides[0][0], sides[1][0]) * HD**-0.5)
        d_keys.append(jnp.where(first, sides[0][1], sides[1][1]))
        d_values.append(jnp.where(first, sides[0][2], sides[1][2]))
    d_qkv = jnp.concatenate(d_queries + d_keys + d_values, axis=1).astype(bf16)
    d_bias[...] += total(d_qkv.astype(f32))
    d_joint[...] += dot(value.astype(bf16), d_qkv, TN)
    out[...] = dot(d_qkv, joint[...], NT).astype(bf16)

    @pl.when(step_at == last)
    def _():
        mats, lows = (d_joint, d_output_weight), (joint, output_weight)
        if carry_out:
            copies = [
                pltpu.make_async_copy(d_joint, results[0], sem.at[0]),
                pltpu.make_async_copy(d_output_weight, results[1], sem.at[1]),
            ]
            for copy in copies:
                copy.start()
            for copy in copies:
                copy.wait()
        elif planes is None:
            store_groups(mats, lows, results[0], sem)
        else:
            store_planes(0, mats, lows, spot, [(planes,) + tuple(results)], sem)


def expand_body(slots, fetched, out):
    hot = lax.broadcasted_iota(jnp.int32, (out.shape[0], fetched.shape[0]), 1) == slots[...]
    out[...] = dot(hot.astype(bf16), fetched[...]).astype(bf16)


def embed_backward_body(
    segs, starts, parts, *refs
):
    sources = [refs[at * 3 : at * 3 + 3] for at in range(len(starts))]
    smalls = refs[3 * len(starts) : 3 * len(starts) + 8]
    mine, theirs, place_mine, place_theirs, slots, spot, params, out, sums = refs[-11:-2]
    d_place, picked = refs[-2:]
    rows = mine.shape[0]
    step_at = pl.program_id(0)

    @pl.when(step_at == 0)
    def _():
        picked[...] = jnp.zeros_like(picked)
        d_place[...] = jnp.zeros_like(d_place)
        sums[...] = jnp.zeros_like(sums)

    def work(seg, base, own, other):
        d_state = base[...] + (own[...].astype(f32) + other[...].astype(f32))
        hat, rate = unit(embedded(seg, spot, mine, theirs, place_mine, place_theirs))
        d_rows = unit_back(d_state * params[0:1], hat, rate)
        sums[0:1, :] += total(d_state * hat)
        sums[1:2, :] += total(d_state)
        own = jnp.where(spot[4] == 0, d_rows[:, :HALF], d_rows[:, HALF:])
        for place in range(rows // seg):
            d_place[:seg, :] += own[place * seg : (place + 1) * seg]
        hot = lax.broadcasted_iota(jnp.int32, (out.shape[0], rows), 0) == slots[0]
        hot = hot.astype(bf16)
        high = own.astype(bf16)
        low = (own - high.astype(f32)).astype(bf16)
        picked[...] += dot(hot, high) + dot(hot, low)

    ends = starts[1:] + (None,)
    for source, seg, start, end in zip(sources, segs, starts, ends):
        here = step_at >= start
        if end is not None:
            here = here & (step_at < end)

        @pl.when(here)
        def _():
            work(seg, *source)

    @pl.when(step_at == pl.num_programs(0) - 1)
    def _():
        width, share = out.shape[0] // parts, rows // parts
        for part in range(parts):
            at = part * width + SLOTS
            picked[at : at + share, :] = d_place[part * share : (part + 1) * share, :]
        lines = []
        for bias, up_bias in (smalls[0:2], smalls[2:4]):
            lines += [bias[:, :HALF], bias[:, 2 * HALF :]]
            lines += [up_bias[:, at : at + HALF] for at in range(0, UNITS, HALF)]
        for at in (0, HALF):
            lines += [sums[row : row + 1, at : at + HALF] for row in range(2)]
            lines += [
                value[row : row + 1, at : at + HALF] for value in smalls[4:] for row in range(3)
            ]
        per = -(-len(lines) // parts)
        for line, value in enumerate(lines):
            at = line // per * width + SLOTS + share + line % per
            picked[at : at + 1, :] = value
        out[...] = picked[...].astype(bf16)


def whole(shape):
    return pl.BlockSpec(shape, lambda i: (0,) * len(shape), pipeline_mode=pl.Buffered(1))


def by_rows(rows, width, offset=0):
    return pl.BlockSpec((rows, width), lambda i: (i + offset, 0))


SMEM = pl.BlockSpec(memory_space=pltpu.SMEM)


def fixed(shape):
    return pl.BlockSpec(shape, lambda i: (0,) * len(shape))


def call(body, grid, in_specs, out_specs, out_shape, scratch=(), us=1.0, name=None, alias=None):
    return pl.pallas_call(
        body,
        grid=(grid,),
        in_specs=in_specs,
        out_specs=out_specs,
        out_shape=[jax.ShapeDtypeStruct(*item) for item in out_shape],
        scratch_shapes=list(scratch),
        compiler_params=pltpu.CompilerParams(vmem_limit_bytes=VMEM_LIMIT),
        cost_estimate=pl.CostEstimate(
            flops=int(us * 1.15e8), bytes_accessed=int(us * 1e4), transcendentals=0
        ),
        input_output_aliases=alias or {},
        name=name,
    )


ANY = pl.BlockSpec(memory_space=pl.ANY)
ATTENTION_GROUPS = 16
FFN_GROUPS = 32


def attention_forward(
    layer, seg, rows, blocks, first, lengths, spot, mine, theirs, groups, order, bias, params
):
    place = mine.shape[0] // rows - 1
    at_place = pl.BlockSpec((rows, HALF), lambda i: (place, 0), pipeline_mode=pl.Buffered(1))
    count = blocks * rows
    return call(
        partial(attention_forward_body, seg, order),
        blocks,
        [
            SMEM,
            SMEM,
            by_rows(rows, HALF, first),
            by_rows(rows, HALF, first),
            at_place,
            at_place,
            whole(bias.shape),
            whole(params.shape),
        ]
        + [ANY] * len(groups),
        [
            by_rows(rows, MODEL_WIDTH),
            by_rows(rows, 3 * HALF),
            by_rows(rows, HALF),
            by_rows(rows, 2 * HD),
            by_rows(rows, MODEL_WIDTH),
        ],
        [
            ((count, MODEL_WIDTH), f32),
            ((count, 3 * HALF), bf16),
            ((count, HALF), bf16),
            ((count, 2 * HD), f32),
            ((count, MODEL_WIDTH), bf16),
        ],
        [
            pltpu.VMEM((MODEL_WIDTH, 3 * HALF), bf16),
            pltpu.VMEM((HALF, MODEL_WIDTH), bf16),
            pltpu.SemaphoreType.DMA((ATTENTION_GROUPS,)),
        ],
        us=2.5 * blocks,
        name=f"attention_forward_{layer}",
    )(lengths, spot, mine, theirs, mine, theirs, bias, params, *groups)


def ffn_forward(layer, rows, spot, state, own, other, groups, order, bias, params):
    count = state.shape[0]
    return call(
        partial(forward_ffn_body, order),
        count // rows,
        [
            SMEM,
            by_rows(rows, MODEL_WIDTH),
            by_rows(rows, MODEL_WIDTH),
            by_rows(rows, MODEL_WIDTH),
            whole(bias.shape),
            whole(params.shape),
        ]
        + [ANY] * len(groups),
        [
            by_rows(rows, MODEL_WIDTH),
            by_rows(rows, UNITS),
            by_rows(rows, UNITS),
            by_rows(rows, MODEL_WIDTH),
        ],
        [
            ((count, MODEL_WIDTH), f32),
            ((count, UNITS), bf16),
            ((count, UNITS), bf16),
            ((count, MODEL_WIDTH), bf16),
        ],
        [
            pltpu.VMEM((MODEL_WIDTH, UNITS), bf16),
            pltpu.VMEM((UNITS, MODEL_WIDTH), bf16),
            pltpu.SemaphoreType.DMA((FFN_GROUPS,)),
        ],
        us=3.8 * count / 256,
        name=f"ffn_forward_{layer}",
    )(spot, state, own, other, bias, params, *groups)


def pool_forward(layer, seg, rows, lengths, hidden, own, other, params):
    count = hidden.shape[0]
    return call(
        partial(pool_body, seg),
        count // rows,
        [
            SMEM,
            by_rows(rows, MODEL_WIDTH),
            by_rows(rows, MODEL_WIDTH),
            by_rows(rows, MODEL_WIDTH),
            whole(params.shape),
        ],
        [fixed((count // seg, MODEL_WIDTH))],
        [((count // seg, MODEL_WIDTH), f32)],
        us=1.1 * (count // rows),
        name=f"pool_{layer}",
    )(lengths, hidden, own, other, params)[0]


def plane_shapes(planes, side, wide):
    shape = (len(planes) * 2 * 3, side, wide)
    return [(shape, bf16)] * 2 + [(shape, f32)] * 2


def ffn_backward(
    layer, seg, rows, lengths, spot, d_pooled, hidden, own, other, active, slope, groups, order,
    params, sets,
):
    side, wide = groups[0].shape[1:]
    count = hidden.shape[0]
    if sets is None:
        results = [((FFN_GROUPS, side, wide), bf16)]
    else:
        results = [item for planes in sets for item in plane_shapes(planes, side, wide)]
    return call(
        partial(ffn_backward_body, seg, order, sets, len(groups)),
        count // rows,
        [
            SMEM,
            SMEM,
            whole(d_pooled.shape),
            by_rows(rows, MODEL_WIDTH),
            by_rows(rows, MODEL_WIDTH),
            by_rows(rows, MODEL_WIDTH),
            by_rows(rows, UNITS),
            by_rows(rows, UNITS),
            whole(params.shape),
        ]
        + [ANY] * len(groups),
        [
            by_rows(rows, MODEL_WIDTH),
            by_rows(rows, MODEL_WIDTH),
            fixed((8, MODEL_WIDTH)),
            fixed((1, UNITS)),
        ]
        + [ANY] * len(results),
        [
            ((count, MODEL_WIDTH), f32),
            ((count, MODEL_WIDTH), bf16),
            ((8, MODEL_WIDTH), f32),
            ((1, UNITS), f32),
        ]
        + results,
        [
            pltpu.VMEM((MODEL_WIDTH, UNITS), bf16),
            pltpu.VMEM((UNITS, MODEL_WIDTH), bf16),
            pltpu.VMEM((MODEL_WIDTH, UNITS), f32),
            pltpu.VMEM((UNITS, MODEL_WIDTH), f32),
            pltpu.SemaphoreType.DMA((FFN_GROUPS,)),
        ],
        us=4.8 * count / 256,
        name=f"ffn_backward_{layer}",
    )(lengths, spot, d_pooled, hidden, own, other, active, slope, params, *groups)


def attention_backward(
    layer, seg, rows, first, blocks, lengths, spot, carried, back_own, back_other, state, own,
    other, qkv, context, logs, groups, order, params, planes=None, buffers=(), carry=(),
    carry_out=False,
):
    side, wide = groups[0].shape[1:]
    count = blocks * rows
    wides = by_rows(rows, MODEL_WIDTH, first)
    out = by_rows(rows, MODEL_WIDTH)
    mats = [((MODEL_WIDTH, 3 * HALF), f32), ((HALF, MODEL_WIDTH), f32)]
    sums = [((8, MODEL_WIDTH), f32), ((1, 3 * HALF), f32)]
    aliases = {}
    if carry_out:
        results = mats
    elif planes is None:
        results = [((ATTENTION_GROUPS, side, wide), bf16)]
    else:
        results = plane_shapes(planes, side, wide)
        before = 12 + len(groups) + len(carry)
        aliases = {before + at: 4 + at for at in range(len(results))}
    return call(
        partial(
            attention_backward_body, seg, order, planes, bool(carry), carry_out, len(groups)
        ),
        blocks,
        [
            SMEM,
            SMEM,
            wides,
            wides,
            wides,
            wides,
            wides,
            wides,
            by_rows(rows, 3 * HALF, first),
            by_rows(rows, HALF, first),
            by_rows(rows, 2 * HD, first),
            whole(params.shape),
        ]
        + [ANY] * len(groups)
        + ([ANY, ANY] + [whole(shape) for shape, _ in sums] if carry else [])
        + [ANY] * len(buffers),
        [out, out] + [fixed(shape) for shape, _ in sums] + [ANY] * len(results),
        [((count, MODEL_WIDTH), f32), ((count, MODEL_WIDTH), bf16)] + sums + results,
        [
            pltpu.VMEM((MODEL_WIDTH, 3 * HALF), bf16),
            pltpu.VMEM((HALF, MODEL_WIDTH), bf16),
            pltpu.VMEM((MODEL_WIDTH, 3 * HALF), f32),
            pltpu.VMEM((HALF, MODEL_WIDTH), f32),
            pltpu.SemaphoreType.DMA((ATTENTION_GROUPS,)),
        ],
        us=5.8 * blocks,
        name=f"attention_backward_{layer}_{first}",
        alias=aliases,
    )(
        lengths, spot, carried, back_own, back_other, state, own, other, qkv, context, logs,
        params, *groups, *carry, *buffers,
    )


def tall_rows(value):
    return 512 if value.shape[0] % 512 == 0 else 256


def expand(rows, slots, fetched):
    count = slots.shape[0]
    return call(
        expand_body,
        count // rows,
        [by_rows(rows, 1), whole(fetched.shape)],
        [by_rows(rows, HALF)],
        [((count, HALF), bf16)],
        us=10.0,
        name="expand",
    )(slots, fetched)[0]


def embed_backward(
    segs, rows, q_parts, p_parts, smalls, mine, theirs, slots, spot, params, parts, width
):
    place = mine.shape[0] // rows - 1
    at_place = pl.BlockSpec((rows, HALF), lambda i: (place, 0), pipeline_mode=pl.Buffered(1))
    blocks = slots.shape[0]
    sources = [q_parts] + list(zip(*p_parts))
    starts, specs, start = [], [], 0
    for source in sources:
        count = source[0].shape[0] // rows
        spec = pl.BlockSpec(
            (rows, MODEL_WIDTH),
            lambda i, start=start, count=count: (jnp.clip(i - start, 0, count - 1), 0),
        )
        specs += [spec] * 3
        starts.append(start)
        start += count
    return call(
        partial(embed_backward_body, segs[:1] + segs[1:] * len(p_parts[0]), tuple(starts), parts),
        blocks,
        specs
        + [whole(value.shape) for value in smalls]
        + [
            by_rows(rows, HALF),
            by_rows(rows, HALF),
            at_place,
            at_place,
            pl.BlockSpec((1, 1, rows), lambda i: (i, 0, 0)),
            SMEM,
            whole(params.shape),
        ],
        [fixed((parts * width, HALF)), fixed((8, MODEL_WIDTH))],
        [((parts * width, HALF), bf16), ((8, MODEL_WIDTH), f32)],
        [pltpu.VMEM((rows, HALF), f32), pltpu.VMEM((parts * width, HALF), f32)],
        us=20.0,
        name="embed_backward",
    )(
        *[part for source in sources for part in source], *smalls, mine, theirs, mine, theirs,
        slots, spot, params,
    )


def pair_blocks(blocks):
    count, side = blocks.shape[0], blocks.shape[-1]
    return (
        blocks.reshape(count // GROUP, GROUP, side, side)
        .transpose(0, 2, 1, 3)
        .reshape(count // GROUP, side, GROUP * side)
    )


def split_pairs(groups):
    count, side = groups.shape[0], groups.shape[1]
    return (
        groups.reshape(count, side, GROUP, side)
        .transpose(0, 2, 1, 3)
        .reshape(count * GROUP, side, side)
    )


def other_core(value):
    return lax.ppermute(value, "tp", [(0, 1), (1, 0)])


def to_all(value, count):
    return lax.all_to_all(jnp.broadcast_to(value[None], (count,) + value.shape), "blk", 0, 0)


def slot_map(present):
    low = jnp.triu(jnp.ones((LANES, LANES), jnp.bfloat16))
    inner = jnp.einsum(
        "ohl,lm->ohm", present.astype(jnp.bfloat16), low, preferred_element_type=jnp.float32
    )
    totals = inner[..., -1]
    before = jnp.cumsum(totals, axis=1) - totals
    ranks = jnp.where(present, inner + before[..., None] - 1.0, -1.0)
    return ranks, jnp.sum(totals, axis=1)


def pick(slots, start, width):
    places = jnp.arange(width, dtype=jnp.float32)
    places = jnp.where(places < SLOTS, places + start, -2.0)
    flat = slots.reshape(slots.shape[0], 1, -1)
    return (flat == places[None, :, None]).astype(jnp.bfloat16)


def pack_body(blocks, out):
    out[0] = jnp.concatenate([blocks[at] for at in range(GROUP)], axis=1).astype(bf16)


def pack(blocks):
    amount, side = blocks.shape[1], blocks.shape[-1]
    return call(
        pack_body,
        amount // GROUP,
        [pl.BlockSpec((None, GROUP, side, side), lambda i: (0, i, 0, 0))],
        [pl.BlockSpec((1, side, GROUP * side), lambda i: (i, 0, 0))],
        [((amount // GROUP, side, GROUP * side), bf16)],
        us=3.0,
        name="pack",
    )(blocks)[0]


def loss_body(asked, codes, positive, d_asked, d_codes, numbers):
    def full(a, b, contract=((1,), (0,))):
        return lax.dot_general(
            a, b, (contract, ((), ())), precision=PRECISION_MAX, preferred_element_type=f32
        )

    scale = 2.0 * MODEL_WIDTH ** (-0.5)
    asks, words = asked[...], codes[...]
    hashed = jnp.tanh(asks)
    dense = full(asks, words, NT) * scale
    binary = full(hashed, words, NT) * scale
    wanted = positive[...]
    columns = lax.broadcasted_iota(jnp.int32, dense.shape, 1)
    hit = columns == wanted
    valid = (wanted >= 0).astype(f32)
    top = jnp.max(dense, axis=1, keepdims=True)
    expo = jnp.exp(dense - top)
    size = jnp.sum(expo, axis=1, keepdims=True)
    cross = top + jnp.log(size) - jnp.sum(jnp.where(hit, dense, 0.0), axis=1, keepdims=True)
    anchor = jnp.sum(jnp.where(hit, binary, 0.0), axis=1, keepdims=True)
    margin = 1.0 - anchor + binary
    small = jnp.exp(-jnp.abs(margin))
    soft = jnp.maximum(margin, 0.0) + jnp.log1p(small)
    others = 1.0 / (dense.shape[1] - 1)
    ranking = jnp.sum(jnp.where(hit, 0.0, soft), axis=1, keepdims=True) * others
    numbers[0:1, :] = jnp.broadcast_to(total(valid * (cross + ranking)), (1, LANES))
    numbers[1:2, :] = jnp.broadcast_to(total(valid), (1, LANES))
    d_dense = valid * (expo / size - hit.astype(f32)) * scale
    rise = jnp.where(margin >= 0, 1.0, small) / (1.0 + small)
    pull = jnp.where(hit, 0.0, rise) * (valid * others)
    d_binary = (pull - jnp.where(hit, jnp.sum(pull, axis=1, keepdims=True), 0.0)) * scale
    d_asked[...] = full(d_dense, words) + full(d_binary, words) * (1.0 - hashed * hashed)
    d_codes[...] = full(d_dense, asks, TN) + full(d_binary, hashed, TN)


def loss_and_back(asked, codes, positive):
    d_asked, d_codes, numbers = call(
        loss_body,
        1,
        [fixed(asked.shape), fixed(codes.shape), fixed(positive.shape)],
        [fixed(asked.shape), fixed(codes.shape), fixed((8, LANES))],
        [(asked.shape, f32), (codes.shape, f32), ((8, LANES), f32)],
        us=5.0,
        name="loss",
    )(asked, codes, positive)
    return numbers[0, 0], numbers[1, 0], d_asked, d_codes


def halves_of(value):
    high = value.astype(bf16)
    return high, (value - high.astype(f32)).astype(bf16)


def near_full(a, b, contract=((1,), (0,))):
    return dot(a[0], b[0], contract) + (dot(a[0], b[1], contract) + dot(a[1], b[0], contract))


def block_products_body(
    paired, inverse, left, right, *rest
):
    parts, (scaled, square, turned, rows, squares) = rest[:-5], rest[-5:]

    @pl.when(pl.program_id(0) == 0)
    def _():
        squares[...] = jnp.zeros_like(squares)

    side = left.shape[-1]
    for at in range(left.shape[0]):
        grad = sum(
            (part[0][:, at * side : (at + 1) * side] if paired else part[at]).astype(f32)
            for part in parts
        )
        grad = grad * inverse[0]
        scaled[at] = grad
        grad_parts = halves_of(grad)
        square[at] = near_full(grad_parts, grad_parts, NT)
        rows[at] = near_full(grad_parts, grad_parts, TN)
        inner = near_full(grad_parts, halves_of(right[at]))
        turned[at] = near_full(halves_of(left[at]), halves_of(inner))
        squares[...] += jnp.broadcast_to(jnp.sum(grad * grad, axis=0, keepdims=True), (8, side))


def block_products(paired, parts, inverse, left, right):
    amount, side = left.shape[1], left.shape[-1]
    per = GROUP if paired else 1
    four = pl.BlockSpec((None, per, side, side), lambda i: (0, i, 0, 0))
    three = pl.BlockSpec((per, side, side), lambda i: (i, 0, 0))
    given = pl.BlockSpec((1,) + parts[0].shape[1:], lambda i: (i, 0, 0))
    return call(
        partial(block_products_body, paired),
        amount // per,
        [SMEM, four, four] + [given] * len(parts),
        [three] * 4 + [fixed((8, side))],
        [((amount, side, side), f32)] * 4 + [((8, side), f32)],
        us=10.0,
        name="block_products",
    )(inverse, left, right, *parts)


def block_update_body(
    factor, scaled, square, rows, turned, left, right, blocks, grads, left_new, right_new, new
):
    scale = factor[0]
    grads[...] = scaled[...] * scale
    left_new[...] = STAT_DECAY * left[...] + ((1.0 - STAT_DECAY) * scale * scale) * square[...]
    right_new[...] = STAT_DECAY * right[...] + ((1.0 - STAT_DECAY) * scale * scale) * rows[...]
    value = blocks[...]
    new[...] = value - SHAMPOO_RATE * (turned[...] * scale + WEIGHT_DECAY * value)


def block_update(factor, scaled, square, rows, turned, left, right, blocks):
    amount, side = left.shape[1], left.shape[-1]
    per = 3 if amount % 3 == 0 else 1
    four = pl.BlockSpec((None, per, side, side), lambda i: (0, i, 0, 0))
    three = pl.BlockSpec((per, side, side), lambda i: (i, 0, 0))
    return call(
        block_update_body,
        amount // per,
        [SMEM] + [three] * 4 + [four] * 3,
        [four] * 4,
        [(left.shape, f32)] * 4,
        us=9.0,
        name="block_update",
    )(factor, scaled, square, rows, turned, left, right, blocks)


class Slice:
    def __init__(self):
        me = lax.axis_index("blk")
        self.x, self.y, self.z = me % 2, me // 2 % 2, me // 4

    @staticmethod
    def over_x(value):
        return lax.ppermute(value, "blk", [(at, at ^ 1) for at in range(16)])

    @staticmethod
    def over_y(value):
        return lax.ppermute(value, "blk", [(at, at ^ 2) for at in range(16)])

    @staticmethod
    def over_z(value, pairs):
        return lax.ppermute(
            value, "blk", [(4 * a + at, 4 * b + at) for a, b in pairs for at in range(4)]
        )


def choose_at(value, index, axis):
    return lax.dynamic_index_in_dim(value, index, axis, keepdims=False)


def add(*values):
    return sum(value.astype(f32) for value in values)


def after(value, *others):
    return lax.optimization_barrier((value,) + others)[0]


def plane_first(links, send_one, send_two, keep_one, keep_two):
    return keep_one, links.over_y(send_one), keep_two, links.over_x(send_two)


def plane_second(links, one, got_one, two, got_two):
    def both(kept, got, index):
        shape = (-1, 2, 3) + kept.shape[1:]
        return add(*(choose_at(part.reshape(shape), index, 1) for part in (kept, got)))

    last_one = links.over_x(both(one, got_one, 1 - links.x).astype(bf16))
    last_two = links.over_y(both(two, got_two, 1 - links.y).astype(bf16))
    return both(one, got_one, links.x), last_one, both(two, got_two, links.y), last_two


def plane_total(one, last_one, two, last_two):
    return jnp.concatenate([add(one, last_one), add(two, last_two)], axis=1)


def column_start(links, plane, pairs):
    return links.over_z(plane.astype(bf16), pairs)


def column_step(links, at_end, first, others, pairs):
    return links.over_z(jnp.where(at_end, first, others).astype(bf16), pairs)


def own_column(links, planes):
    z = links.z
    return jnp.where(
        z < 2, jnp.where(z == 0, planes[0], planes[1]), jnp.where(z == 2, planes[2], planes[3])
    )


def adamw(weight, moment, second, grad):
    moment = BETA_ONE * moment + (1.0 - BETA_ONE) * grad
    second = BETA_TWO * second + (1.0 - BETA_TWO) * grad * grad
    update = (
        moment / (1.0 - BETA_ONE**STEP) / (jnp.sqrt(second / (1.0 - BETA_TWO**STEP)) + ADAM_EPS)
    )
    return (moment, second, weight - ADAM_RATE * (update + WEIGHT_DECAY * weight))


def on_device(
    q_tokens,
    p_tokens,
    q_lengths,
    p_lengths,
    positive,
    table,
    table_moment,
    table_second,
    blocks,
    left_stats,
    right_stats,
    left_roots,
    right_roots,
    vectors,
    vector_moment,
    vector_second,
    shared,
    shared_moment,
    shared_second,
):
    parts = lax.axis_size("blk")
    me, core = lax.axis_index("blk"), lax.axis_index("tp")
    rows_here, half = table.shape
    side = blocks.shape[-1]
    per_device = blocks.shape[1]
    even = per_device % GROUP == 0
    own_blocks = blocks[0].astype(bf16)
    in_order = list(range(ATTENTION_GROUPS + FFN_GROUPS))
    known = parts == 16 and even
    if known:
        links = Slice()
        own_groups = pack(blocks)
        at_z, over = links.z, links.over_z
        spot = jnp.stack(
            [links.x, links.y, (at_z == 0).astype(jnp.int32), (at_z == 3).astype(jnp.int32), core]
        )
        down_one, down_own = over(own_groups, [(3, 2), (2, 1)]), over(own_groups, [(2, 3)])
        up_one, up_own = over(own_groups, [(0, 1), (1, 2)]), over(own_groups, [(1, 0)])
    elif even:
        groups = lax.all_gather(pair_blocks(own_blocks), "blk", axis=0, tiled=True)
    else:
        groups = pair_blocks(lax.all_gather(own_blocks, "blk", axis=0, tiled=True))
    if not known:
        spot = jnp.zeros((5,), jnp.int32).at[4].set(core)
        layer_groups = [(groups[: len(in_order)],), (groups[len(in_order) :],)]
        orders = [in_order, in_order]

    q_live = (jnp.arange(q_tokens.shape[1])[None, :] < q_lengths[:, None]).reshape(-1)
    p_live = (jnp.arange(p_tokens.shape[1])[None, :] < p_lengths[:, None]).reshape(-1)
    tokens = jnp.concatenate([q_tokens.reshape(-1), p_tokens.reshape(-1)])
    live = jnp.concatenate([q_live, p_live])
    tall = -(-rows_here // LANES)
    owner = tokens // rows_here
    inside = tokens - owner * rows_here
    high = jnp.where(live, owner * tall + inside // LANES, -1)
    high_hot = (high[:, None] == jnp.arange(parts * tall)[None, :]).astype(bf16)
    low_hot = (inside[:, None] % LANES == jnp.arange(LANES)[None, :]).astype(bf16)
    uses = jnp.einsum("th,tl->hl", high_hot, low_hot, preferred_element_type=f32)
    present = (uses > 0).reshape(parts, tall, LANES)
    slots, wanted = slot_map(present)
    token_slot = jnp.sum(
        jnp.dot(high_hot.astype(f32), slots.reshape(-1, LANES), precision=PRECISION_MAX) * low_hot,
        axis=1,
    )
    rounds_here = jnp.ceil(jnp.max(wanted) / SLOTS)

    small = jnp.concatenate(
        [
            vectors.astype(bf16).reshape(-1),
            shared.astype(bf16).reshape(-1),
            rounds_here.astype(bf16)[None],
        ]
    )
    small_size = -(-small.shape[0] // LANES) * LANES
    small = jnp.pad(small, (0, small_size - small.shape[0])).reshape(-1, LANES)
    table_low = jnp.pad(table.astype(bf16), ((0, tall * LANES - rows_here), (0, 0)))
    length = p_tokens.shape[1]
    q_length = q_tokens.shape[1]
    share = length // parts
    margin = jnp.zeros((length, half), bf16)
    first_place = jnp.clip(VOCAB - me * rows_here + length, 0, rows_here + length)
    places_here = lax.dynamic_slice_in_dim(
        jnp.concatenate([margin, table_low[:rows_here], margin]), first_place, length, 0
    )
    asks = jnp.concatenate(
        [
            present.astype(bf16),
            jnp.broadcast_to(small[None], (parts,) + small.shape),
            places_here.reshape(parts, share * half // LANES, LANES),
        ],
        axis=1,
    )
    if known:
        asks, down_one, down_own, up_one, up_own = lax.optimization_barrier(
            (asks, down_one, down_own, up_one, up_own)
        )
        down_two, up_two = over(down_one, [(1, 0), (2, 1)]), over(up_one, [(2, 3), (1, 2)])
    asks = lax.all_to_all(asks, "blk", 0, 0)
    if known:
        asks, down_two, up_two = lax.optimization_barrier((asks, down_two, up_two))
        down_three, up_three = over(down_two, [(1, 0)]), over(up_two, [(2, 3)])
        pick_at = lambda *values: jnp.where(
            at_z < 2,
            jnp.where(at_z == 0, values[0], values[1]),
            jnp.where(at_z == 2, values[2], values[3]),
        )
        later_one = pick_at(down_two, down_one, own_groups, own_groups)
        near_one = gather_near(links, later_one)
    asked_slots, _ = slot_map(asks[:, :tall] > 0)
    place_share = jnp.sum(asks[:, tall + small.shape[0] :].astype(f32), axis=0).astype(bf16)
    place_share = place_share.reshape(share, half)
    small = asks[:, tall : tall + small.shape[0]].reshape(parts, -1)
    vector_part, shared_part = vectors.shape[2], shared.shape[1]
    vector_size, shared_size = vectors.size, shared.size
    bias_all = (
        small[:, :vector_size]
        .reshape(parts, LAYERS, vector_part)
        .transpose(1, 0, 2)
        .reshape(LAYERS, -1)
        .astype(f32)
    )
    params_all = (
        small[:, vector_size : vector_size + shared_size]
        .reshape(parts, -1, shared_part)
        .transpose(1, 0, 2)
        .reshape(-1, parts * shared_part)
        .astype(f32)
    )
    rounds = jnp.max(small[:, vector_size + shared_size].astype(f32)).astype(jnp.int32)

    per_part = -(-(LAYERS * (vectors.shape[2] * parts // half) + 2 * shared.shape[0]) // parts)
    width = -(-(SLOTS + share + per_part) // 16) * 16

    def choose(start):
        return pick(asked_slots, start, width)

    def serve(chosen):
        return jnp.einsum("sjr,rc->sjc", chosen, table_low, preferred_element_type=f32).astype(bf16)

    def places_of(start):
        place = token_slot - start
        fits = (high >= 0) & (place >= 0) & (place < SLOTS)
        return jnp.where(fits, owner * width + place.astype(jnp.int32), -1)

    def spread(start):
        return (places_of(start)[:, None] == jnp.arange(parts * width)[None, :]).astype(bf16)

    places_first = places_of(0.0)
    place_at = jnp.arange(length)
    places_first = jnp.concatenate(
        [places_first, place_at // share * width + SLOTS + place_at % share]
    )
    place_rows = places_first[: tokens.shape[0]].reshape(-1, 1, length)
    place_columns = places_first[:, None]

    sent = jnp.concatenate(
        [
            serve(choose(0.0))[:, :SLOTS],
            jnp.broadcast_to(place_share[None], (parts, share, half)),
            jnp.zeros((parts, width - SLOTS - share, half), bf16),
        ],
        axis=1,
    )
    if known:
        sent, down_three, up_three, *near_one = lax.optimization_barrier(
            (sent, down_three, up_three) + near_one
        )
        far_one = gather_far(links, *near_one)
        later_two = pick_at(down_three, down_two, down_one, down_own)
        near_two = gather_near(links, later_two)
    fetched = lax.all_to_all(sent, "blk", 0, 0)
    if known:
        place_columns, place_rows, far_two, near_two = lax.optimization_barrier(
            (place_columns, place_rows, far_one, near_two)
        )
        far_one = far_two
        far_two = gather_far(links, *near_two)
    halves = expand(length, place_columns, fetched.reshape(-1, half))

    def fetch_more(carry):
        done, total = carry
        start = (done * SLOTS).astype(f32)
        more = lax.all_to_all(serve(choose(start)), "blk", 0, 0).reshape(-1, half)
        more = jnp.dot(spread(start), more, preferred_element_type=f32).astype(bf16)
        return done + 1, total.at[: tokens.shape[0]].add(more)

    if known:
        halves, *far_two = lax.optimization_barrier((halves,) + far_two)
        layer_groups = [
            None, (later_one, *near_one, *far_one, later_two, *near_two, *far_two)
        ]
        orders = [0, 1]
        early_one = pick_at(own_groups, own_groups, up_one, up_two)
        early_two = pick_at(up_own, up_one, up_two, up_three)
    halves = lax.while_loop(lambda c: c[0] < rounds, fetch_more, (jnp.int32(1), halves))[1]
    others = other_core(halves)
    embed_params = params_all[:2]
    q_blocks, p_blocks = q_tokens.size // length, p_tokens.size // length

    def first_half(layer, seg, first, count, lengths):
        bias = bias_all[layer : layer + 1]
        params = params_all[2 + 6 * layer : 8 + 6 * layer]
        return [layer, seg, lengths, bias, params] + list(attention_forward(
            layer, seg, length, count, first, lengths, spot, halves, others,
            layer_groups[layer], orders[layer], bias, embed_params,
        ))

    def second_half(kept):
        layer, seg, lengths, bias, params, state, qkv, context, logs, own_one = kept
        other_one = other_core(own_one)
        return kept + [other_one] + list(ffn_forward(
            layer, tall_rows(state), spot, state, own_one, other_one, layer_groups[layer],
            orders[layer], bias, params,
        ))

    def pool_of(kept):
        layer, seg, lengths, _, params = kept[:5]
        hidden, _, _, own_two = kept[11:]
        other_two = other_core(own_two)
        kept.append(other_two)
        return pool_forward(layer, seg, length, lengths, hidden, own_two, other_two, params)

    if known:
        near_one = gather_near(links, early_one)
    p_kept = first_half(1, length, q_blocks, p_blocks, p_lengths)
    if known:
        p_kept[-1], *near_one = lax.optimization_barrier((p_kept[-1],) + near_one)
        far_one = gather_far(links, *near_one)
        near_two = gather_near(links, early_two)
    p_kept = second_half(p_kept)
    if known:
        p_kept[-1], *four = lax.optimization_barrier((p_kept[-1],) + far_one + near_two)
        far_one, near_two = four[:2], four[2:]
        far_two = gather_far(links, *near_two)
    p_pooled = pool_of(p_kept)
    if known:
        p_pooled, *far_two = lax.optimization_barrier((p_pooled,) + far_two)
        layer_groups[0] = (early_one, *near_one, *far_one, early_two, *near_two, *far_two)
    q_kept = second_half(first_half(0, q_length, 0, q_blocks, q_lengths))
    codes_local = jnp.tanh(p_pooled)
    codes_low = codes_local.astype(bf16)
    codes = to_all(codes_low, parts)
    q_kept[-1], codes = lax.optimization_barrier((q_kept[-1], codes))
    pooled = [pool_of(q_kept), p_pooled]
    asked_local = pooled[0]
    codes = codes.reshape(-1, MODEL_WIDTH).astype(f32)
    every = to_all(
        jnp.concatenate(
            [
                asked_local,
                jnp.pad(positive.astype(f32)[None], ((0, 0), (0, MODEL_WIDTH - positive.shape[0]))),
            ]
        ),
        parts,
    )
    q_part, p_part = asked_local.shape[0], codes_local.shape[0]
    asked = every[:, :q_part].reshape(-1, MODEL_WIDTH)
    positives = every[:, q_part, :q_part].reshape(-1).astype(jnp.int32)
    loss_sum, positives_count, d_asked, d_codes = loss_and_back(asked, codes, positives[:, None])
    d_asked = lax.dynamic_slice_in_dim(d_asked, me * q_part, q_part, 0)
    d_codes = lax.dynamic_slice_in_dim(d_codes, me * p_part, p_part, 0)
    d_passages = d_codes * (1.0 - codes_local * codes_local)
    def ffn_back(kept, d_pooled, sets):
        (layer, seg, lengths, bias, params, state, qkv, context, logs, own_one, other_one, hidden,
         active, slope, own_two, other_two) = kept
        return ffn_backward(
            layer, seg, tall_rows(hidden), lengths, spot, d_pooled, hidden, own_two, other_two, active, slope,
            layer_groups[layer], orders[layer], params, sets,
        )

    def attention_back(kept, base, back_own, back_other, first, count, **more):
        (layer, seg, lengths, bias, params, state, qkv, context, logs, own_one, other_one) = kept[:11]
        return attention_backward(
            layer, seg, length, first, count, lengths[first:] if first else lengths, spot, base,
            back_own, back_other, state, own_one, other_one, qkv, context, logs,
            layer_groups[layer], orders[layer], params, **more,
        )

    q_base, q_back, q_ffn_sums, q_up_bias, *q_ffn = ffn_back(
        q_kept, d_asked, ((0, 1),) if known else None
    )
    q_state, q_state_own, q_sums, q_bias, *q_attention = attention_back(
        q_kept, q_base, q_back, other_core(q_back), 0, q_blocks,
        **(dict(planes=(0, 1), buffers=q_ffn) if known else {}),
    )
    p_base, p_back, p_ffn_sums, p_up_bias, *p_ffn = ffn_back(
        p_kept, after(d_passages, q_sums), ((0,), (1,)) if known else None
    )
    if known:
        early = p_blocks // 2
        q_first = plane_first(links, *q_attention)
        top_first = plane_first(links, *p_ffn[4:])
        p_back, *q_first = lax.optimization_barrier((p_back,) + q_first)
        p_back_other = other_core(p_back)
        q_second = plane_second(links, *q_first)
        state_one, own_one, *carry = attention_back(
            p_kept, p_base, p_back, p_back_other, 0, early, carry_out=True
        )
        carry = carry[2:] + carry[:2]
        other_one = other_core(own_one)
        carry[2], *eight = lax.optimization_barrier((carry[2],) + q_second + top_first)
        q_planes = plane_total(*eight[:4])
        top_second = plane_second(links, *eight[4:])
        down = column_start(links, q_planes[0], [(3, 2)])
        state_two, own_two, p_sums, p_bias, *low = attention_back(
            p_kept, p_base, p_back, p_back_other, early, p_blocks - early, carry=carry,
            planes=(0,), buffers=p_ffn[:4],
        )
        own_two, down, *top_second = lax.optimization_barrier((own_two, down) + top_second)
        top_plane = plane_total(*top_second)[0]
        other_two = other_core(own_two)
        up = column_start(links, top_plane, [(0, 1)])
        down = column_step(
            links, links.z == 3, q_planes[1], add(q_planes[0], down), [(3, 2), (2, 1)]
        )
        low_first = plane_first(links, *low)
        state_p = ((state_one, state_two), (own_one, own_two), (other_one, other_two))
        low_first = plane_first(links, *low)
    else:
        p_back_other = other_core(p_back)
        state_one, own_one, p_sums, p_bias, *p_attention = attention_back(
            p_kept, p_base, p_back, p_back_other, 0, p_blocks
        )
        state_p = ((state_one,), (own_one,), (other_core(own_one),))
    smalls = (
        q_bias, q_up_bias, p_bias, p_up_bias, q_sums, q_ffn_sums, p_sums, p_ffn_sums
    )
    vector_rows = LAYERS * vector_part * parts // half
    state_parts = [
        (q_state, q_state_own, other_core(q_state_own)),
        state_p,
    ]
    picked, _ = embed_backward(
        (q_length, length), length, state_parts[0], state_parts[1], smalls, halves, others, place_rows,
        spot, embed_params, parts, width,
    )
    if known:
        picked, up, down, *low_first = lax.optimization_barrier((picked, up, down) + low_first)

    def gather_up(start):
        return embed_backward(
            (q_length, length), length, state_parts[0], state_parts[1], smalls, halves, others,
            places_of(start).reshape(-1, 1, length), spot, embed_params, parts, width,
        )[0].reshape(parts, width, half)

    def put_back(chosen, received):
        return jnp.einsum("sjr,sjc->rc", chosen, received, preferred_element_type=f32)[:rows_here]

    sent = picked.reshape(parts, width, half)
    got = lax.all_to_all(sent, "blk", 0, 0)
    token_grad = put_back(choose(0.0), got)

    def send_more(carry):
        done, total = carry
        start = (done * SLOTS).astype(f32)
        more = lax.all_to_all(gather_up(start), "blk", 0, 0)
        return done + 1, total + put_back(choose(start), more)

    token_grad = lax.while_loop(lambda c: c[0] < rounds, send_more, (jnp.int32(1), token_grad))[1]
    rest = jnp.sum(got[:, SLOTS : SLOTS + share + per_part].astype(f32), axis=0)
    if known:
        low_plane = plane_total(*plane_second(links, *low_first))[0]
        z = links.z
        planes = [q_planes[0], q_planes[1], low_plane, top_plane]
        up = column_step(links, z == 0, low_plane, add(top_plane, up), [(0, 1), (1, 2)])
        down = column_step(
            links, z == 3, low_plane, add(jnp.where(z == 2, q_planes[1], q_planes[0]), down),
            [(3, 2), (2, 1), (1, 0)],
        )
        base = lax.optimization_barrier(
            jnp.where(z == 0, q_planes[1], jnp.where(z == 1, low_plane, top_plane))
        )
        up = links.over_z(
            (base + jnp.where(z == 0, 0.0, up.astype(f32))).astype(bf16),
            [(0, 1), (1, 2), (2, 3)],
        )
        grad_parts = (own_column(links, planes), up, down)
    else:
        all_groups = jnp.concatenate(q_attention + q_ffn + p_attention + p_ffn, axis=0)
        if not even:
            all_groups = split_pairs(all_groups)
        grad_parts = (lax.psum_scatter(all_groups, "blk", scatter_dimension=0, tiled=True),)
    inverse = 1.0 / positives_count
    rest = rest * inverse
    row_index = me * per_part + jnp.arange(per_part)
    counted = ((row_index < vector_rows) | (core == 0)).astype(f32)
    squares = (
        jnp.sum(rest[:share] ** 2)
        + jnp.sum(rest[share:] ** 2 * counted[:, None])
        + jnp.sum((token_grad * inverse) ** 2)
    )
    rest = to_all(rest, parts)
    if known:
        squares, *grad_parts = lax.optimization_barrier((squares,) + grad_parts)
    scaled, square, turned, row_square, block_squares = block_products(
        even, grad_parts, inverse[None], left_roots, right_roots
    )
    block_squares, rest = lax.optimization_barrier((block_squares, rest))
    place_grads = rest[:, :share].reshape(length, half)
    small_grads = rest[:, share:].reshape(-1, half)
    grad_vectors = lax.dynamic_slice_in_dim(
        small_grads[:vector_rows].reshape(LAYERS, -1), me * vector_part, vector_part, 1
    )[None]
    shared_rows = shared.shape[0]
    grad_shared = lax.dynamic_slice_in_dim(
        jnp.concatenate(
            [
                small_grads[vector_rows : vector_rows + shared_rows],
                small_grads[vector_rows + shared_rows : vector_rows + 2 * shared_rows],
            ],
            axis=1,
        ),
        me * shared_part,
        shared_part,
        1,
    )
    margin = jnp.zeros((rows_here, half), f32)
    place_grads = lax.dynamic_slice_in_dim(
        jnp.concatenate([margin, place_grads, margin]),
        jnp.clip(me * rows_here - VOCAB + rows_here, 0, rows_here + length),
        rows_here,
        0,
    )
    table_grad = token_grad * inverse + place_grads
    squares = squares + jnp.sum(block_squares[0])
    devices = parts * 2
    squares = lax.all_to_all(
        jnp.broadcast_to(squares, (devices, 8, LANES)), ("blk", "tp"), 0, 0
    )
    squares = jnp.sum(squares[:, 0, 0])
    grad_norm = jnp.sqrt(squares)
    factor = jnp.minimum(1.0, CLIP / grad_norm)
    block_grads, left_new, right_new, blocks_new = block_update(
        factor[None], scaled, square, row_square, turned, left_stats, right_stats, blocks
    )
    table_moment_new, table_second_new, table_new = adamw(
        table, table_moment, table_second, table_grad * factor
    )
    vector_moment_new, vector_second_new, vectors_new = adamw(
        vectors, vector_moment, vector_second, grad_vectors * factor
    )
    shared_moment_new, shared_second_new, shared_new = adamw(
        shared, shared_moment, shared_second, grad_shared * factor
    )
    return (
        loss_sum,
        positives_count,
        grad_norm,
        block_grads,
        left_new,
        right_new,
        blocks_new,
        table_moment_new,
        table_second_new,
        table_new,
        vector_moment_new,
        vector_second_new,
        vectors_new,
        shared_moment_new,
        shared_second_new,
        shared_new,
    )


def solution(mesh):
    return jax.shard_map(
        on_device,
        mesh=mesh,
        in_specs=(
            P("blk", None),
            P("blk", None),
            P("blk"),
            P("blk"),
            P("blk"),
            P("blk", "tp"),
            P("blk", "tp"),
            P("blk", "tp"),
            P("tp", "blk", None, None),
            P("tp", "blk", None, None),
            P("tp", "blk", None, None),
            P("tp", "blk", None, None),
            P("tp", "blk", None, None),
            P("tp", None, "blk"),
            P("tp", None, "blk"),
            P("tp", None, "blk"),
            P(None, "blk"),
            P(None, "blk"),
            P(None, "blk"),
        ),
        out_specs=(
            P(),
            P(),
            P(),
            P("tp", "blk", None, None),
            P("tp", "blk", None, None),
            P("tp", "blk", None, None),
            P("tp", "blk", None, None),
            P("blk", "tp"),
            P("blk", "tp"),
            P("blk", "tp"),
            P("tp", None, "blk"),
            P("tp", None, "blk"),
            P("tp", None, "blk"),
            P(None, "blk"),
            P(None, "blk"),
            P(None, "blk"),
        ),
        check_vma=False,
    )
```

```python
from functools import partial

import jax
import jax.numpy as jnp
from jax import lax
from jax.experimental import pallas as pl
from jax.experimental.pallas import tpu as pltpu
from jax.sharding import PartitionSpec as P

bf16, f32 = jnp.bfloat16, jnp.float32
MODEL_WIDTH = 768
HALF = MODEL_WIDTH // 2
HD = 64
FF = 3072
UNITS = FF // 2
NORM_EPS = 1e-06
VMEM_LIMIT = 60 * 1024 * 1024
LAYERS = 2
STEP = 10
VOCAB = 30522
CLIP = 0.05
BETA_ONE = 0.9
BETA_TWO = 0.999
STAT_DECAY = 0.95
ADAM_RATE = 0.5
SHAMPOO_RATE = 0.5
WEIGHT_DECAY = 0.01
ADAM_EPS = 1e-08
PRECISION_MAX = lax.Precision.HIGHEST
GROUP = 2
SLOTS = 92
LANES = 128

TAIL = (
    0.16918798443114483,
    0.17071555704933744,
    0.14833696008811015,
    0.2149342153930891,
    -0.09466890560267835,
    0.5477451349382827,
    -0.5122991151213244,
    0.4855729957946344,
    -0.12952484655737367,
)


def gelu_parts(u):
    t = 1.0 / (1.0 + (0.3 * 0.5**0.5) * jnp.abs(u))
    poly = jnp.full_like(t, TAIL[-1])
    for term in TAIL[-2::-1]:
        poly = poly * t + term
    bell = jnp.exp(u * u * -0.5)
    tail = (0.5 * t) * poly * bell
    below = jnp.where(u >= 0, 1.0 - tail, tail)
    return u * below, below + u * (bell * 0.3989422804014327)


def dot(a, b, contract=((1,), (0,))):
    return lax.dot_general(a, b, (contract, ((), ())), preferred_element_type=f32)


NT = ((1,), (1,))
TN = ((0,), (0,))


def unit(value):
    centred = value - jnp.mean(value, axis=-1, keepdims=True)
    rate = lax.rsqrt(jnp.mean(centred * centred, axis=-1, keepdims=True) + NORM_EPS)
    return centred * rate, rate


def unit_back(grad, hat, rate):
    return rate * (
        grad
        - jnp.mean(grad, axis=-1, keepdims=True)
        - hat * jnp.mean(grad * hat, axis=-1, keepdims=True)
    )


def total(value):
    return jnp.sum(value, axis=0, keepdims=True)


def row_lengths(lengths, rows, axis, seg, shape):
    index = lax.broadcasted_iota(jnp.int32, shape, axis)
    if seg == rows:
        return index, None, lengths[pl.program_id(0)]
    which = index // seg
    length = jnp.zeros(shape, jnp.int32)
    before = pl.program_id(0) * (rows // seg)
    for place in range(rows // seg):
        length = jnp.where(which == place, lengths[before + place], length)
    return index - which * seg, which, length


def row_live(lengths, rows, seg):
    place, _, length = row_lengths(lengths, rows, 0, seg, (rows, 1))
    return (place < length).astype(f32), length


def key_mask(lengths, rows, seg):
    if seg == rows:
        place, _, length = row_lengths(lengths, rows, 1, seg, (1, rows))
        return place < length
    place, which, length = row_lengths(lengths, rows, 1, seg, (rows, rows))
    mine = lax.broadcasted_iota(jnp.int32, (rows, rows), 0) // seg
    return (which == mine) & (place < length)


def key_mask_across(lengths, rows, seg):
    place, which, length = row_lengths(lengths, rows, 0, seg, (rows, 1))
    if seg == rows:
        return place < length
    mine = lax.broadcasted_iota(jnp.int32, (rows, rows), 1) // seg
    return (which == mine) & (place < length)


def load_weights(groups, order, first, spot, mats, sem):
    side, wide = groups[0].shape[1:]
    starts, waits, at = [], [], 0
    for mat in mats:
        for row in range(mat.shape[0] // side):
            for column in range(mat.shape[1] // wide):
                to = mat.at[row * side : (row + 1) * side, column * wide : (column + 1) * wide]
                if len(groups) == 1:
                    choices = [(None, groups[0].at[order[first + at]])]
                else:
                    choices = group_choices(groups, order, first + at, spot)
                copies = [
                    (where, pltpu.make_async_copy(part, to, sem.at[at])) for where, part in choices
                ]
                starts += copies
                waits.append(copies[0][1])
                at += 1
    for where, copy in starts:
        if where is None:
            copy.start()
        else:
            pl.when(where)(copy.start)
    for copy in waits:
        copy.wait()


def group_choices(groups, layer, group, spot):
    owner, place = divmod(group, 6)
    plane, own_y, own_x = owner // 4, owner // 2 % 2, owner % 2
    is_first = spot[2 + layer] == (0 if plane == 1 - layer else 1)
    far_x, far_y = spot[0] != own_x, spot[1] != own_y
    near_x, near_y = jnp.logical_not(far_x), jnp.logical_not(far_y)
    part, rest = divmod(place, 3)
    choices = []
    for here, (own, by_x, by_y, *both) in (
        (is_first, groups[:5]),
        (jnp.logical_not(is_first), groups[5:]),
    ):
        choices += [
            (here & near_x & near_y, own.at[place]),
            (here & far_x & near_y, by_x.at[place]),
            (here & near_x & far_y, by_y.at[place]),
            (here & far_x & far_y, both[part].at[rest]),
        ]
    return choices


def gather_near(links, piece):
    return links.over_x(piece), links.over_y(piece)


def gather_far(links, by_x, by_y):
    half = by_x.shape[0] // 2
    return links.over_y(by_x[:half]), links.over_x(by_y[half:])


def store_groups(mats, lows, grads, sem):
    side, wide = grads.shape[1:]
    copies, at = [], 0
    for mat, low in zip(mats, lows):
        low[...] = mat[...].astype(bf16)
        for row in range(mat.shape[0] // side):
            for column in range(mat.shape[1] // wide):
                part = low.at[row * side : (row + 1) * side, column * wide : (column + 1) * wide]
                copies.append(pltpu.make_async_copy(part, grads.at[at], sem.at[at]))
                at += 1
    for copy in copies:
        copy.start()
    for copy in copies:
        copy.wait()


def store_planes(first, mats, lows, spot, sets, sem):
    side, wide = sets[0][1].shape[-2:]
    count = 3
    copies, at = [], 0
    for mat, low in zip(mats, lows):
        low[...] = mat[...].astype(bf16)
        for row in range(mat.shape[0] // side):
            for column in range(mat.shape[1] // wide):
                owner, place = divmod(first + at, 2 * count)
                plane, own_y, own_x = owner // 4, owner // 2 % 2, owner % 2
                planes, *refs = next(item for item in sets if plane in item[0])
                plane = planes.index(plane)
                by_y = place < count
                mine = spot[1] == own_y if by_y else spot[0] == own_x
                index = (plane * 2 + (own_x if by_y else own_y)) * count + place % count
                send, keep = (refs[0], refs[2]) if by_y else (refs[1], refs[3])
                region = (
                    slice(row * side, (row + 1) * side),
                    slice(column * wide, (column + 1) * wide),
                )
                copies.append(
                    (mine, pltpu.make_async_copy(mat.at[region], keep.at[index], sem.at[at]))
                )
                copies.append(
                    (
                        jnp.logical_not(mine),
                        pltpu.make_async_copy(low.at[region], send.at[index], sem.at[at]),
                    )
                )
                at += 1
    for where, copy in copies:
        pl.when(where)(copy.start)
    for where, copy in copies:
        pl.when(where)(copy.wait)


def head_lanes(rows):
    return lax.broadcasted_iota(jnp.int32, (rows, 2 * HD), 1) < HD


def embedded(seg, spot, mine, theirs, place_mine, place_theirs):
    rows = mine.shape[0]

    def side_of(ref, places):
        place = jnp.concatenate([places[:seg].astype(f32)] * (rows // seg), axis=0)
        return ref[...].astype(f32) + place

    own, other = side_of(mine, place_mine), side_of(theirs, place_theirs)
    first = spot[4] == 0
    return jnp.concatenate([jnp.where(first, own, other), jnp.where(first, other, own)], axis=1)


def attention_forward_body(
    seg, order, lengths, spot, mine, theirs, place_mine, place_theirs, bias, params, *rest,
):
    groups, rest = rest[:-8], rest[-8:]
    state, qkv, context, logs, out, joint, output_weight, sem = rest
    rows = mine.shape[0]

    @pl.when(pl.program_id(0) == 0)
    def _():
        load_weights(groups, order, 0, spot, (joint, output_weight), sem)

    hat, _ = unit(embedded(seg, spot, mine, theirs, place_mine, place_theirs))
    value = hat * params[0:1] + params[1:2]
    state[...] = value
    projected = dot(value.astype(bf16), joint[...])
    shift = jnp.concatenate(
        [bias[:, :HALF], jnp.zeros((1, HALF), f32), bias[:, HALF : 2 * HALF]], axis=1
    )
    projected = (projected + shift).astype(bf16)
    qkv[...] = projected
    mask = key_mask(lengths, rows, seg)
    first = head_lanes(rows)
    contexts = []
    for pair in range(HALF // (2 * HD)):
        lanes = slice(pair * 2 * HD, (pair + 1) * 2 * HD)
        query = projected[:, :HALF][:, lanes] * jnp.asarray(HD**-0.5, bf16)
        key = projected[:, HALF : 2 * HALF][:, lanes]
        what = projected[:, 2 * HALF :][:, lanes]
        sides = []
        for head in range(2):
            only = jnp.where(first if head == 0 else ~first, query, jnp.zeros_like(query))
            scores = jnp.where(mask, dot(only, key, NT), -1e30)
            top = jnp.max(scores, axis=-1, keepdims=True)
            expo = jnp.exp(scores - top)
            size = jnp.sum(expo, axis=-1, keepdims=True)
            logs[:, 2 * pair + head : 2 * pair + head + 1] = top + jnp.log(size)
            sides.append(dot((expo * (1.0 / size)).astype(bf16), what))
        contexts.append(jnp.where(first, sides[0], sides[1]))
    contexts = jnp.concatenate(contexts, axis=1).astype(bf16)
    context[...] = contexts
    out[...] = dot(contexts, output_weight[...]).astype(bf16)


def forward_ffn_body(
    order, spot, state, own, other, bias, params, *rest,
):
    groups, rest = rest[:-7], rest[-7:]
    hidden, active, slope, out, up_weight, down_weight, sem = rest
    wide = groups[0].shape[2]

    @pl.when(pl.program_id(0) == 0)
    def _():
        load_weights(groups, order, ATTENTION_GROUPS, spot, (up_weight, down_weight), sem)

    hat, _ = unit(state[...] + (own[...].astype(f32) + other[...].astype(f32)) + params[0:1])
    value = hat * params[1:2] + params[2:3]
    hidden[...] = value
    low = value.astype(bf16)
    step = UNITS
    result = jnp.zeros(out.shape, f32)
    for start in range(0, UNITS, step):
        columns = slice(start, start + step)
        up = dot(low, up_weight[:, columns]) + bias[:, 2 * HALF + start : 2 * HALF + start + step]
        act, rise = gelu_parts(up)
        act = act.astype(bf16)
        active[:, columns] = act
        slope[:, columns] = rise.astype(bf16)
        result = result + dot(act, down_weight[columns, :])
    out[...] = result.astype(bf16)


def pool_body(seg, lengths, hidden, own, other, params, out):
    rows = hidden.shape[0]
    hat, _ = unit(hidden[...] + (own[...].astype(f32) + other[...].astype(f32)) + params[3:4])
    output = hat * params[4:5] + params[5:6]
    live, _ = row_live(lengths, rows, seg)
    output = output * live
    for place in range(rows // seg):
        index = pl.program_id(0) * (rows // seg) + place
        mean = total(output[place * seg : (place + 1) * seg]) / lengths[index].astype(f32)
        out[pl.ds(index, 1), :] = mean


def ffn_backward_body(
    seg, order, sets, amount, lengths, spot, d_pooled, hidden, own, other, active, slope, params,
    *rest,
):
    groups, rest = rest[:amount], rest[amount:]
    base, out, sums, d_bias, *rest = rest
    grads, (up_weight, down_weight, d_up, d_down, sem) = tuple(rest[:-5]), rest[-5:]
    rows = hidden.shape[0]
    wide = groups[0].shape[2]
    step_at, last = pl.program_id(0), pl.num_programs(0) - 1

    @pl.when(step_at == 0)
    def _():
        load_weights(groups, order, ATTENTION_GROUPS, spot, (up_weight, down_weight), sem)
        d_up[...] = jnp.zeros_like(d_up)
        d_down[...] = jnp.zeros_like(d_down)
        sums[...] = jnp.zeros_like(sums)
        d_bias[...] = jnp.zeros_like(d_bias)

    live, length = row_live(lengths, rows, seg)
    pooled = jnp.concatenate(
        [
            jnp.broadcast_to(
                d_pooled[pl.ds(step_at * (rows // seg) + place, 1), :], (seg, MODEL_WIDTH)
            )
            for place in range(rows // seg)
        ],
        axis=0,
    )
    d_output = pooled / length.astype(f32) * live
    value = hidden[...]
    hat, rate = unit(value + (own[...].astype(f32) + other[...].astype(f32)) + params[3:4])
    d_sum = unit_back(d_output * params[4:5], hat, rate)
    base[...] = d_sum
    sums[0:1, :] += total(d_sum)
    sums[1:2, :] += total(d_output * hat)
    sums[2:3, :] += total(d_output)
    low = d_sum.astype(bf16)
    hidden_low = value.astype(bf16)
    step = UNITS
    result = jnp.zeros(out.shape, f32)
    for start in range(0, UNITS, step):
        columns = slice(start, start + step)
        d_down[columns, :] += dot(active[:, columns], low, TN)
        d_act = dot(low, down_weight[columns, :], NT)
        d_pre = (d_act * slope[:, columns].astype(f32)).astype(bf16)
        d_bias[:, columns] += total(d_pre.astype(f32))
        d_up[:, columns] += dot(hidden_low, d_pre, TN)
        result = result + dot(d_pre, up_weight[:, columns], NT)
    out[...] = result.astype(bf16)

    @pl.when(step_at == last)
    def _():
        mats, lows = (d_up, d_down), (up_weight, down_weight)
        if sets is None:
            store_groups(mats, lows, grads[0], sem)
        else:
            to = [(planes,) + grads[4 * at : 4 * at + 4] for at, planes in enumerate(sets)]
            store_planes(ATTENTION_GROUPS, mats, lows, spot, to, sem)


def attention_backward_body(
    seg, order, planes, carry_in, carry_out, amount, lengths, spot, carried, back_own, back_other,
    state, own, other, qkv, context, logs, params, *rest,
):
    groups, rest = rest[:amount], rest[amount:]
    joint, output_weight, d_joint, d_output_weight, sem = rest[-5:]
    carry, rest = (rest[:4], rest[4:-5]) if carry_in else (None, rest[:-5])
    if planes is not None and not carry_out:
        rest = rest[4:]
    base, out, sums, d_bias, *results = rest
    rows = state.shape[0]
    step_at, last = pl.program_id(0), pl.num_programs(0) - 1

    @pl.when(step_at == 0)
    def _():
        load_weights(groups, order, 0, spot, (joint, output_weight), sem)
        if carry is None:
            d_joint[...] = jnp.zeros_like(d_joint)
            d_output_weight[...] = jnp.zeros_like(d_output_weight)
            sums[...] = jnp.zeros_like(sums)
            d_bias[...] = jnp.zeros_like(d_bias)
        else:
            copies = [
                pltpu.make_async_copy(carry[0], d_joint, sem.at[0]),
                pltpu.make_async_copy(carry[1], d_output_weight, sem.at[1]),
            ]
            for copy in copies:
                copy.start()
            for copy in copies:
                copy.wait()
            sums[...] = carry[2][...]
            d_bias[...] = carry[3][...]

    d_hidden = carried[...] + (back_own[...].astype(f32) + back_other[...].astype(f32))
    value = state[...]
    hat, rate = unit(value + (own[...].astype(f32) + other[...].astype(f32)) + params[0:1])
    d_sum = unit_back(d_hidden * params[1:2], hat, rate)
    base[...] = d_sum
    sums[0:1, :] += total(d_sum)
    sums[1:2, :] += total(d_hidden * hat)
    sums[2:3, :] += total(d_hidden)
    low = d_sum.astype(bf16)
    d_output_weight[...] += dot(context[...], low, TN)
    d_context = dot(low, output_weight[...], NT).astype(bf16)
    mask = key_mask_across(lengths, rows, seg)
    logs_across = jnp.transpose(logs[...])
    first = head_lanes(rows)
    d_queries, d_keys, d_values = [], [], []
    for pair in range(HALF // (2 * HD)):
        lanes = slice(pair * 2 * HD, (pair + 1) * 2 * HD)
        query = qkv[:, pair * 2 * HD : (pair + 1) * 2 * HD] * jnp.asarray(HD**-0.5, bf16)
        key = qkv[:, HALF + pair * 2 * HD : HALF + (pair + 1) * 2 * HD]
        what = qkv[:, 2 * HALF + pair * 2 * HD : 2 * HALF + (pair + 1) * 2 * HD]
        d_pair = d_context[:, lanes]
        sides = []
        for head in range(2):
            mine = first if head == 0 else ~first
            only = jnp.where(mine, query, jnp.zeros_like(query))
            d_only = jnp.where(mine, d_pair, jnp.zeros_like(d_pair))
            scores = jnp.where(mask, dot(key, only, NT), -1e30)
            weights = jnp.exp(scores - logs_across[2 * pair + head : 2 * pair + head + 1, :])
            spread = weights * dot(what, d_only, NT)
            d_scores = spread - weights * total(spread)
            d_scores = d_scores.astype(bf16)
            sides.append(
                (
                    dot(d_scores, key, TN),
                    dot(d_scores, query),
                    dot(weights.astype(bf16), d_pair),
                )
            )
        d_queries.append(jnp.where(first, sides[0][0], sides[1][0]) * HD**-0.5)
        d_keys.append(jnp.where(first, sides[0][1], sides[1][1]))
        d_values.append(jnp.where(first, sides[0][2], sides[1][2]))
    d_qkv = jnp.concatenate(d_queries + d_keys + d_values, axis=1).astype(bf16)
    d_bias[...] += total(d_qkv.astype(f32))
    d_joint[...] += dot(value.astype(bf16), d_qkv, TN)
    out[...] = dot(d_qkv, joint[...], NT).astype(bf16)

    @pl.when(step_at == last)
    def _():
        mats, lows = (d_joint, d_output_weight), (joint, output_weight)
        if carry_out:
            copies = [
                pltpu.make_async_copy(d_joint, results[0], sem.at[0]),
                pltpu.make_async_copy(d_output_weight, results[1], sem.at[1]),
            ]
            for copy in copies:
                copy.start()
            for copy in copies:
                copy.wait()
        elif planes is None:
            store_groups(mats, lows, results[0], sem)
        else:
            store_planes(0, mats, lows, spot, [(planes,) + tuple(results)], sem)


def expand_body(slots, fetched, out):
    hot = lax.broadcasted_iota(jnp.int32, (out.shape[0], fetched.shape[0]), 1) == slots[...]
    out[...] = dot(hot.astype(bf16), fetched[...]).astype(bf16)


def embed_backward_body(
    segs, starts, parts, *refs
):
    sources = [refs[at * 3 : at * 3 + 3] for at in range(len(starts))]
    smalls = refs[3 * len(starts) : 3 * len(starts) + 8]
    mine, theirs, place_mine, place_theirs, slots, spot, params, out, sums = refs[-11:-2]
    d_place, picked = refs[-2:]
    rows = mine.shape[0]
    step_at = pl.program_id(0)

    @pl.when(step_at == 0)
    def _():
        picked[...] = jnp.zeros_like(picked)
        d_place[...] = jnp.zeros_like(d_place)
        sums[...] = jnp.zeros_like(sums)

    def work(seg, base, own, other):
        d_state = base[...] + (own[...].astype(f32) + other[...].astype(f32))
        hat, rate = unit(embedded(seg, spot, mine, theirs, place_mine, place_theirs))
        d_rows = unit_back(d_state * params[0:1], hat, rate)
        sums[0:1, :] += total(d_state * hat)
        sums[1:2, :] += total(d_state)
        own = jnp.where(spot[4] == 0, d_rows[:, :HALF], d_rows[:, HALF:])
        for place in range(rows // seg):
            d_place[:seg, :] += own[place * seg : (place + 1) * seg]
        hot = lax.broadcasted_iota(jnp.int32, (out.shape[0], rows), 0) == slots[0]
        hot = hot.astype(bf16)
        high = own.astype(bf16)
        low = (own - high.astype(f32)).astype(bf16)
        picked[...] += dot(hot, high) + dot(hot, low)

    ends = starts[1:] + (None,)
    for source, seg, start, end in zip(sources, segs, starts, ends):
        here = step_at >= start
        if end is not None:
            here = here & (step_at < end)

        @pl.when(here)
        def _():
            work(seg, *source)

    @pl.when(step_at == pl.num_programs(0) - 1)
    def _():
        width, share = out.shape[0] // parts, rows // parts
        for part in range(parts):
            at = part * width + SLOTS
            picked[at : at + share, :] = d_place[part * share : (part + 1) * share, :]
        lines = []
        for bias, up_bias in (smalls[0:2], smalls[2:4]):
            lines += [bias[:, :HALF], bias[:, 2 * HALF :]]
            lines += [up_bias[:, at : at + HALF] for at in range(0, UNITS, HALF)]
        for at in (0, HALF):
            lines += [sums[row : row + 1, at : at + HALF] for row in range(2)]
            lines += [
                value[row : row + 1, at : at + HALF] for value in smalls[4:] for row in range(3)
            ]
        per = -(-len(lines) // parts)
        for line, value in enumerate(lines):
            at = line // per * width + SLOTS + share + line % per
            picked[at : at + 1, :] = value
        out[...] = picked[...].astype(bf16)


def whole(shape):
    return pl.BlockSpec(shape, lambda i: (0,) * len(shape), pipeline_mode=pl.Buffered(1))


def by_rows(rows, width, offset=0):
    return pl.BlockSpec((rows, width), lambda i: (i + offset, 0))


SMEM = pl.BlockSpec(memory_space=pltpu.SMEM)


def fixed(shape):
    return pl.BlockSpec(shape, lambda i: (0,) * len(shape))


def call(body, grid, in_specs, out_specs, out_shape, scratch=(), us=1.0, name=None, alias=None):
    return pl.pallas_call(
        body,
        grid=(grid,),
        in_specs=in_specs,
        out_specs=out_specs,
        out_shape=[jax.ShapeDtypeStruct(*item) for item in out_shape],
        scratch_shapes=list(scratch),
        compiler_params=pltpu.CompilerParams(vmem_limit_bytes=VMEM_LIMIT),
        cost_estimate=pl.CostEstimate(
            flops=int(us * 1.15e8), bytes_accessed=int(us * 1e4), transcendentals=0
        ),
        input_output_aliases=alias or {},
        name=name,
    )


ANY = pl.BlockSpec(memory_space=pl.ANY)
ATTENTION_GROUPS = 16
FFN_GROUPS = 32


def attention_forward(
    layer, seg, rows, blocks, first, lengths, spot, mine, theirs, groups, order, bias, params
):
    place = mine.shape[0] // rows - 1
    at_place = pl.BlockSpec((rows, HALF), lambda i: (place, 0), pipeline_mode=pl.Buffered(1))
    count = blocks * rows
    return call(
        partial(attention_forward_body, seg, order),
        blocks,
        [
            SMEM,
            SMEM,
            by_rows(rows, HALF, first),
            by_rows(rows, HALF, first),
            at_place,
            at_place,
            whole(bias.shape),
            whole(params.shape),
        ]
        + [ANY] * len(groups),
        [
            by_rows(rows, MODEL_WIDTH),
            by_rows(rows, 3 * HALF),
            by_rows(rows, HALF),
            by_rows(rows, 2 * HD),
            by_rows(rows, MODEL_WIDTH),
        ],
        [
            ((count, MODEL_WIDTH), f32),
            ((count, 3 * HALF), bf16),
            ((count, HALF), bf16),
            ((count, 2 * HD), f32),
            ((count, MODEL_WIDTH), bf16),
        ],
        [
            pltpu.VMEM((MODEL_WIDTH, 3 * HALF), bf16),
            pltpu.VMEM((HALF, MODEL_WIDTH), bf16),
            pltpu.SemaphoreType.DMA((ATTENTION_GROUPS,)),
        ],
        us=2.5 * blocks,
        name=f"attention_forward_{layer}",
    )(lengths, spot, mine, theirs, mine, theirs, bias, params, *groups)


def ffn_forward(layer, rows, spot, state, own, other, groups, order, bias, params):
    count = state.shape[0]
    return call(
        partial(forward_ffn_body, order),
        count // rows,
        [
            SMEM,
            by_rows(rows, MODEL_WIDTH),
            by_rows(rows, MODEL_WIDTH),
            by_rows(rows, MODEL_WIDTH),
            whole(bias.shape),
            whole(params.shape),
        ]
        + [ANY] * len(groups),
        [
            by_rows(rows, MODEL_WIDTH),
            by_rows(rows, UNITS),
            by_rows(rows, UNITS),
            by_rows(rows, MODEL_WIDTH),
        ],
        [
            ((count, MODEL_WIDTH), f32),
            ((count, UNITS), bf16),
            ((count, UNITS), bf16),
            ((count, MODEL_WIDTH), bf16),
        ],
        [
            pltpu.VMEM((MODEL_WIDTH, UNITS), bf16),
            pltpu.VMEM((UNITS, MODEL_WIDTH), bf16),
            pltpu.SemaphoreType.DMA((FFN_GROUPS,)),
        ],
        us=3.8 * count / 256,
        name=f"ffn_forward_{layer}",
    )(spot, state, own, other, bias, params, *groups)


def pool_forward(layer, seg, rows, lengths, hidden, own, other, params):
    count = hidden.shape[0]
    return call(
        partial(pool_body, seg),
        count // rows,
        [
            SMEM,
            by_rows(rows, MODEL_WIDTH),
            by_rows(rows, MODEL_WIDTH),
            by_rows(rows, MODEL_WIDTH),
            whole(params.shape),
        ],
        [fixed((count // seg, MODEL_WIDTH))],
        [((count // seg, MODEL_WIDTH), f32)],
        us=1.1 * (count // rows),
        name=f"pool_{layer}",
    )(lengths, hidden, own, other, params)[0]


def plane_shapes(planes, side, wide):
    shape = (len(planes) * 2 * 3, side, wide)
    return [(shape, bf16)] * 2 + [(shape, f32)] * 2


def ffn_backward(
    layer, seg, rows, lengths, spot, d_pooled, hidden, own, other, active, slope, groups, order,
    params, sets,
):
    side, wide = groups[0].shape[1:]
    count = hidden.shape[0]
    if sets is None:
        results = [((FFN_GROUPS, side, wide), bf16)]
    else:
        results = [item for planes in sets for item in plane_shapes(planes, side, wide)]
    return call(
        partial(ffn_backward_body, seg, order, sets, len(groups)),
        count // rows,
        [
            SMEM,
            SMEM,
            whole(d_pooled.shape),
            by_rows(rows, MODEL_WIDTH),
            by_rows(rows, MODEL_WIDTH),
            by_rows(rows, MODEL_WIDTH),
            by_rows(rows, UNITS),
            by_rows(rows, UNITS),
            whole(params.shape),
        ]
        + [ANY] * len(groups),
        [
            by_rows(rows, MODEL_WIDTH),
            by_rows(rows, MODEL_WIDTH),
            fixed((8, MODEL_WIDTH)),
            fixed((1, UNITS)),
        ]
        + [ANY] * len(results),
        [
            ((count, MODEL_WIDTH), f32),
            ((count, MODEL_WIDTH), bf16),
            ((8, MODEL_WIDTH), f32),
            ((1, UNITS), f32),
        ]
        + results,
        [
            pltpu.VMEM((MODEL_WIDTH, UNITS), bf16),
            pltpu.VMEM((UNITS, MODEL_WIDTH), bf16),
            pltpu.VMEM((MODEL_WIDTH, UNITS), f32),
            pltpu.VMEM((UNITS, MODEL_WIDTH), f32),
            pltpu.SemaphoreType.DMA((FFN_GROUPS,)),
        ],
        us=4.8 * count / 256,
        name=f"ffn_backward_{layer}",
    )(lengths, spot, d_pooled, hidden, own, other, active, slope, params, *groups)


def attention_backward(
    layer, seg, rows, first, blocks, lengths, spot, carried, back_own, back_other, state, own,
    other, qkv, context, logs, groups, order, params, planes=None, buffers=(), carry=(),
    carry_out=False,
):
    side, wide = groups[0].shape[1:]
    count = blocks * rows
    wides = by_rows(rows, MODEL_WIDTH, first)
    out = by_rows(rows, MODEL_WIDTH)
    mats = [((MODEL_WIDTH, 3 * HALF), f32), ((HALF, MODEL_WIDTH), f32)]
    sums = [((8, MODEL_WIDTH), f32), ((1, 3 * HALF), f32)]
    aliases = {}
    if carry_out:
        results = mats
    elif planes is None:
        results = [((ATTENTION_GROUPS, side, wide), bf16)]
    else:
        results = plane_shapes(planes, side, wide)
        before = 12 + len(groups) + len(carry)
        aliases = {before + at: 4 + at for at in range(len(results))}
    return call(
        partial(
            attention_backward_body, seg, order, planes, bool(carry), carry_out, len(groups)
        ),
        blocks,
        [
            SMEM,
            SMEM,
            wides,
            wides,
            wides,
            wides,
            wides,
            wides,
            by_rows(rows, 3 * HALF, first),
            by_rows(rows, HALF, first),
            by_rows(rows, 2 * HD, first),
            whole(params.shape),
        ]
        + [ANY] * len(groups)
        + ([ANY, ANY] + [whole(shape) for shape, _ in sums] if carry else [])
        + [ANY] * len(buffers),
        [out, out] + [fixed(shape) for shape, _ in sums] + [ANY] * len(results),
        [((count, MODEL_WIDTH), f32), ((count, MODEL_WIDTH), bf16)] + sums + results,
        [
            pltpu.VMEM((MODEL_WIDTH, 3 * HALF), bf16),
            pltpu.VMEM((HALF, MODEL_WIDTH), bf16),
            pltpu.VMEM((MODEL_WIDTH, 3 * HALF), f32),
            pltpu.VMEM((HALF, MODEL_WIDTH), f32),
            pltpu.SemaphoreType.DMA((ATTENTION_GROUPS,)),
        ],
        us=5.8 * blocks,
        name=f"attention_backward_{layer}_{first}",
        alias=aliases,
    )(
        lengths, spot, carried, back_own, back_other, state, own, other, qkv, context, logs,
        params, *groups, *carry, *buffers,
    )


def tall_rows(value):
    return 512 if value.shape[0] % 512 == 0 else 256


def expand(rows, slots, fetched):
    count = slots.shape[0]
    return call(
        expand_body,
        count // rows,
        [by_rows(rows, 1), whole(fetched.shape)],
        [by_rows(rows, HALF)],
        [((count, HALF), bf16)],
        us=10.0,
        name="expand",
    )(slots, fetched)[0]


def embed_backward(
    segs, rows, q_parts, p_parts, smalls, mine, theirs, slots, spot, params, parts, width
):
    place = mine.shape[0] // rows - 1
    at_place = pl.BlockSpec((rows, HALF), lambda i: (place, 0), pipeline_mode=pl.Buffered(1))
    blocks = slots.shape[0]
    sources = [q_parts] + list(zip(*p_parts))
    starts, specs, start = [], [], 0
    for source in sources:
        count = source[0].shape[0] // rows
        spec = pl.BlockSpec(
            (rows, MODEL_WIDTH),
            lambda i, start=start, count=count: (jnp.clip(i - start, 0, count - 1), 0),
        )
        specs += [spec] * 3
        starts.append(start)
        start += count
    return call(
        partial(embed_backward_body, segs[:1] + segs[1:] * len(p_parts[0]), tuple(starts), parts),
        blocks,
        specs
        + [whole(value.shape) for value in smalls]
        + [
            by_rows(rows, HALF),
            by_rows(rows, HALF),
            at_place,
            at_place,
            pl.BlockSpec((1, 1, rows), lambda i: (i, 0, 0)),
            SMEM,
            whole(params.shape),
        ],
        [fixed((parts * width, HALF)), fixed((8, MODEL_WIDTH))],
        [((parts * width, HALF), bf16), ((8, MODEL_WIDTH), f32)],
        [pltpu.VMEM((rows, HALF), f32), pltpu.VMEM((parts * width, HALF), f32)],
        us=20.0,
        name="embed_backward",
    )(
        *[part for source in sources for part in source], *smalls, mine, theirs, mine, theirs,
        slots, spot, params,
    )


def pair_blocks(blocks):
    count, side = blocks.shape[0], blocks.shape[-1]
    return (
        blocks.reshape(count // GROUP, GROUP, side, side)
        .transpose(0, 2, 1, 3)
        .reshape(count // GROUP, side, GROUP * side)
    )


def split_pairs(groups):
    count, side = groups.shape[0], groups.shape[1]
    return (
        groups.reshape(count, side, GROUP, side)
        .transpose(0, 2, 1, 3)
        .reshape(count * GROUP, side, side)
    )


def other_core(value):
    return lax.ppermute(value, "tp", [(0, 1), (1, 0)])


def to_all(value, count):
    return lax.all_to_all(jnp.broadcast_to(value[None], (count,) + value.shape), "blk", 0, 0)


def slot_map(present):
    low = jnp.triu(jnp.ones((LANES, LANES), jnp.bfloat16))
    inner = jnp.einsum(
        "ohl,lm->ohm", present.astype(jnp.bfloat16), low, preferred_element_type=jnp.float32
    )
    totals = inner[..., -1]
    before = jnp.cumsum(totals, axis=1) - totals
    ranks = jnp.where(present, inner + before[..., None] - 1.0, -1.0)
    return ranks, jnp.sum(totals, axis=1)


def pick(slots, start, width):
    places = jnp.arange(width, dtype=jnp.float32)
    places = jnp.where(places < SLOTS, places + start, -2.0)
    flat = slots.reshape(slots.shape[0], 1, -1)
    return (flat == places[None, :, None]).astype(jnp.bfloat16)


def pack_body(blocks, out):
    out[0] = jnp.concatenate([blocks[at] for at in range(GROUP)], axis=1).astype(bf16)


def pack(blocks):
    amount, side = blocks.shape[1], blocks.shape[-1]
    return call(
        pack_body,
        amount // GROUP,
        [pl.BlockSpec((None, GROUP, side, side), lambda i: (0, i, 0, 0))],
        [pl.BlockSpec((1, side, GROUP * side), lambda i: (i, 0, 0))],
        [((amount // GROUP, side, GROUP * side), bf16)],
        us=3.0,
        name="pack",
    )(blocks)[0]


def loss_body(asked, codes, positive, d_asked, d_codes, numbers):
    def full(a, b, contract=((1,), (0,))):
        return lax.dot_general(
            a, b, (contract, ((), ())), precision=PRECISION_MAX, preferred_element_type=f32
        )

    scale = 2.0 * MODEL_WIDTH ** (-0.5)
    asks, words = asked[...], codes[...]
    hashed = jnp.tanh(asks)
    dense = full(asks, words, NT) * scale
    binary = full(hashed, words, NT) * scale
    wanted = positive[...]
    columns = lax.broadcasted_iota(jnp.int32, dense.shape, 1)
    hit = columns == wanted
    valid = (wanted >= 0).astype(f32)
    top = jnp.max(dense, axis=1, keepdims=True)
    expo = jnp.exp(dense - top)
    size = jnp.sum(expo, axis=1, keepdims=True)
    cross = top + jnp.log(size) - jnp.sum(jnp.where(hit, dense, 0.0), axis=1, keepdims=True)
    anchor = jnp.sum(jnp.where(hit, binary, 0.0), axis=1, keepdims=True)
    margin = 1.0 - anchor + binary
    small = jnp.exp(-jnp.abs(margin))
    soft = jnp.maximum(margin, 0.0) + jnp.log1p(small)
    others = 1.0 / (dense.shape[1] - 1)
    ranking = jnp.sum(jnp.where(hit, 0.0, soft), axis=1, keepdims=True) * others
    numbers[0:1, :] = jnp.broadcast_to(total(valid * (cross + ranking)), (1, LANES))
    numbers[1:2, :] = jnp.broadcast_to(total(valid), (1, LANES))
    d_dense = valid * (expo / size - hit.astype(f32)) * scale
    rise = jnp.where(margin >= 0, 1.0, small) / (1.0 + small)
    pull = jnp.where(hit, 0.0, rise) * (valid * others)
    d_binary = (pull - jnp.where(hit, jnp.sum(pull, axis=1, keepdims=True), 0.0)) * scale
    d_asked[...] = full(d_dense, words) + full(d_binary, words) * (1.0 - hashed * hashed)
    d_codes[...] = full(d_dense, asks, TN) + full(d_binary, hashed, TN)


def loss_and_back(asked, codes, positive):
    d_asked, d_codes, numbers = call(
        loss_body,
        1,
        [fixed(asked.shape), fixed(codes.shape), fixed(positive.shape)],
        [fixed(asked.shape), fixed(codes.shape), fixed((8, LANES))],
        [(asked.shape, f32), (codes.shape, f32), ((8, LANES), f32)],
        us=5.0,
        name="loss",
    )(asked, codes, positive)
    return numbers[0, 0], numbers[1, 0], d_asked, d_codes


def halves_of(value):
    high = value.astype(bf16)
    return high, (value - high.astype(f32)).astype(bf16)


def near_full(a, b, contract=((1,), (0,))):
    return dot(a[0], b[0], contract) + (dot(a[0], b[1], contract) + dot(a[1], b[0], contract))


def block_products_body(
    paired, inverse, left, right, *rest
):
    parts, (scaled, square, turned, rows, squares) = rest[:-5], rest[-5:]

    @pl.when(pl.program_id(0) == 0)
    def _():
        squares[...] = jnp.zeros_like(squares)

    side = left.shape[-1]
    for at in range(left.shape[0]):
        grad = sum(
            (part[0][:, at * side : (at + 1) * side] if paired else part[at]).astype(f32)
            for part in parts
        )
        grad = grad * inverse[0]
        scaled[at] = grad
        grad_parts = halves_of(grad)
        square[at] = near_full(grad_parts, grad_parts, NT)
        rows[at] = near_full(grad_parts, grad_parts, TN)
        inner = near_full(grad_parts, halves_of(right[at]))
        turned[at] = near_full(halves_of(left[at]), halves_of(inner))
        squares[...] += jnp.broadcast_to(jnp.sum(grad * grad, axis=0, keepdims=True), (8, side))


def block_products(paired, parts, inverse, left, right):
    amount, side = left.shape[1], left.shape[-1]
    per = GROUP if paired else 1
    four = pl.BlockSpec((None, per, side, side), lambda i: (0, i, 0, 0))
    three = pl.BlockSpec((per, side, side), lambda i: (i, 0, 0))
    given = pl.BlockSpec((1,) + parts[0].shape[1:], lambda i: (i, 0, 0))
    return call(
        partial(block_products_body, paired),
        amount // per,
        [SMEM, four, four] + [given] * len(parts),
        [three] * 4 + [fixed((8, side))],
        [((amount, side, side), f32)] * 4 + [((8, side), f32)],
        us=10.0,
        name="block_products",
    )(inverse, left, right, *parts)


def block_update_body(
    factor, scaled, square, rows, turned, left, right, blocks, grads, left_new, right_new, new
):
    scale = factor[0]
    grads[...] = scaled[...] * scale
    left_new[...] = STAT_DECAY * left[...] + ((1.0 - STAT_DECAY) * scale * scale) * square[...]
    right_new[...] = STAT_DECAY * right[...] + ((1.0 - STAT_DECAY) * scale * scale) * rows[...]
    value = blocks[...]
    new[...] = value - SHAMPOO_RATE * (turned[...] * scale + WEIGHT_DECAY * value)


def block_update(factor, scaled, square, rows, turned, left, right, blocks):
    amount, side = left.shape[1], left.shape[-1]
    per = 3 if amount % 3 == 0 else 1
    four = pl.BlockSpec((None, per, side, side), lambda i: (0, i, 0, 0))
    three = pl.BlockSpec((per, side, side), lambda i: (i, 0, 0))
    return call(
        block_update_body,
        amount // per,
        [SMEM] + [three] * 4 + [four] * 3,
        [four] * 4,
        [(left.shape, f32)] * 4,
        us=9.0,
        name="block_update",
    )(factor, scaled, square, rows, turned, left, right, blocks)


class Slice:
    def __init__(self):
        me = lax.axis_index("blk")
        self.x, self.y, self.z = me % 2, me // 2 % 2, me // 4

    @staticmethod
    def over_x(value):
        return lax.ppermute(value, "blk", [(at, at ^ 1) for at in range(16)])

    @staticmethod
    def over_y(value):
        return lax.ppermute(value, "blk", [(at, at ^ 2) for at in range(16)])

    @staticmethod
    def over_z(value, pairs):
        return lax.ppermute(
            value, "blk", [(4 * a + at, 4 * b + at) for a, b in pairs for at in range(4)]
        )


def choose_at(value, index, axis):
    return lax.dynamic_index_in_dim(value, index, axis, keepdims=False)


def add(*values):
    return sum(value.astype(f32) for value in values)


def after(value, *others):
    return lax.optimization_barrier((value,) + others)[0]


def plane_first(links, send_one, send_two, keep_one, keep_two):
    return keep_one, links.over_y(send_one), keep_two, links.over_x(send_two)


def plane_second(links, one, got_one, two, got_two):
    def both(kept, got, index):
        shape = (-1, 2, 3) + kept.shape[1:]
        return add(*(choose_at(part.reshape(shape), index, 1) for part in (kept, got)))

    last_one = links.over_x(both(one, got_one, 1 - links.x).astype(bf16))
    last_two = links.over_y(both(two, got_two, 1 - links.y).astype(bf16))
    return both(one, got_one, links.x), last_one, both(two, got_two, links.y), last_two


def plane_total(one, last_one, two, last_two):
    return jnp.concatenate([add(one, last_one), add(two, last_two)], axis=1)


def column_start(links, plane, pairs):
    return links.over_z(plane.astype(bf16), pairs)


def column_step(links, at_end, first, others, pairs):
    return links.over_z(jnp.where(at_end, first, others).astype(bf16), pairs)


def own_column(links, planes):
    z = links.z
    return jnp.where(
        z < 2, jnp.where(z == 0, planes[0], planes[1]), jnp.where(z == 2, planes[2], planes[3])
    )


def adamw(weight, moment, second, grad):
    moment = BETA_ONE * moment + (1.0 - BETA_ONE) * grad
    second = BETA_TWO * second + (1.0 - BETA_TWO) * grad * grad
    update = (
        moment / (1.0 - BETA_ONE**STEP) / (jnp.sqrt(second / (1.0 - BETA_TWO**STEP)) + ADAM_EPS)
    )
    return (moment, second, weight - ADAM_RATE * (update + WEIGHT_DECAY * weight))


def on_device(
    q_tokens,
    p_tokens,
    q_lengths,
    p_lengths,
    positive,
    table,
    table_moment,
    table_second,
    blocks,
    left_stats,
    right_stats,
    left_roots,
    right_roots,
    vectors,
    vector_moment,
    vector_second,
    shared,
    shared_moment,
    shared_second,
):
    parts = lax.axis_size("blk")
    me, core = lax.axis_index("blk"), lax.axis_index("tp")
    rows_here, half = table.shape
    side = blocks.shape[-1]
    per_device = blocks.shape[1]
    even = per_device % GROUP == 0
    own_blocks = blocks[0].astype(bf16)
    in_order = list(range(ATTENTION_GROUPS + FFN_GROUPS))
    known = parts == 16 and even
    if known:
        links = Slice()
        own_groups = pack(blocks)
        at_z, over = links.z, links.over_z
        spot = jnp.stack(
            [links.x, links.y, (at_z == 0).astype(jnp.int32), (at_z == 3).astype(jnp.int32), core]
        )
        down_one, down_own = over(own_groups, [(3, 2), (2, 1)]), over(own_groups, [(2, 3)])
        up_one, up_own = over(own_groups, [(0, 1), (1, 2)]), over(own_groups, [(1, 0)])
    elif even:
        groups = lax.all_gather(pair_blocks(own_blocks), "blk", axis=0, tiled=True)
    else:
        groups = pair_blocks(lax.all_gather(own_blocks, "blk", axis=0, tiled=True))
    if not known:
        spot = jnp.zeros((5,), jnp.int32).at[4].set(core)
        layer_groups = [(groups[: len(in_order)],), (groups[len(in_order) :],)]
        orders = [in_order, in_order]

    q_live = (jnp.arange(q_tokens.shape[1])[None, :] < q_lengths[:, None]).reshape(-1)
    p_live = (jnp.arange(p_tokens.shape[1])[None, :] < p_lengths[:, None]).reshape(-1)
    tokens = jnp.concatenate([q_tokens.reshape(-1), p_tokens.reshape(-1)])
    live = jnp.concatenate([q_live, p_live])
    tall = -(-rows_here // LANES)
    owner = tokens // rows_here
    inside = tokens - owner * rows_here
    high = jnp.where(live, owner * tall + inside // LANES, -1)
    high_hot = (high[:, None] == jnp.arange(parts * tall)[None, :]).astype(bf16)
    low_hot = (inside[:, None] % LANES == jnp.arange(LANES)[None, :]).astype(bf16)
    uses = jnp.einsum("th,tl->hl", high_hot, low_hot, preferred_element_type=f32)
    present = (uses > 0).reshape(parts, tall, LANES)
    slots, wanted = slot_map(present)
    token_slot = jnp.sum(
        jnp.dot(high_hot.astype(f32), slots.reshape(-1, LANES), precision=PRECISION_MAX) * low_hot,
        axis=1,
    )
    rounds_here = jnp.ceil(jnp.max(wanted) / SLOTS)

    small = jnp.concatenate(
        [
            vectors.astype(bf16).reshape(-1),
            shared.astype(bf16).reshape(-1),
            rounds_here.astype(bf16)[None],
        ]
    )
    small_size = -(-small.shape[0] // LANES) * LANES
    small = jnp.pad(small, (0, small_size - small.shape[0])).reshape(-1, LANES)
    table_low = jnp.pad(table.astype(bf16), ((0, tall * LANES - rows_here), (0, 0)))
    length = p_tokens.shape[1]
    q_length = q_tokens.shape[1]
    share = length // parts
    margin = jnp.zeros((length, half), bf16)
    first_place = jnp.clip(VOCAB - me * rows_here + length, 0, rows_here + length)
    places_here = lax.dynamic_slice_in_dim(
        jnp.concatenate([margin, table_low[:rows_here], margin]), first_place, length, 0
    )
    asks = jnp.concatenate(
        [
            present.astype(bf16),
            jnp.broadcast_to(small[None], (parts,) + small.shape),
            places_here.reshape(parts, share * half // LANES, LANES),
        ],
        axis=1,
    )
    if known:
        asks, down_one, down_own, up_one, up_own = lax.optimization_barrier(
            (asks, down_one, down_own, up_one, up_own)
        )
        down_two, up_two = over(down_one, [(1, 0), (2, 1)]), over(up_one, [(2, 3), (1, 2)])
    asks = lax.all_to_all(asks, "blk", 0, 0)
    if known:
        asks, down_two, up_two = lax.optimization_barrier((asks, down_two, up_two))
        down_three, up_three = over(down_two, [(1, 0)]), over(up_two, [(2, 3)])
        pick_at = lambda *values: jnp.where(
            at_z < 2,
            jnp.where(at_z == 0, values[0], values[1]),
            jnp.where(at_z == 2, values[2], values[3]),
        )
        later_one = pick_at(down_two, down_one, own_groups, own_groups)
        near_one = gather_near(links, later_one)
    asked_slots, _ = slot_map(asks[:, :tall] > 0)
    place_share = jnp.sum(asks[:, tall + small.shape[0] :].astype(f32), axis=0).astype(bf16)
    place_share = place_share.reshape(share, half)
    small = asks[:, tall : tall + small.shape[0]].reshape(parts, -1)
    vector_part, shared_part = vectors.shape[2], shared.shape[1]
    vector_size, shared_size = vectors.size, shared.size
    bias_all = (
        small[:, :vector_size]
        .reshape(parts, LAYERS, vector_part)
        .transpose(1, 0, 2)
        .reshape(LAYERS, -1)
        .astype(f32)
    )
    params_all = (
        small[:, vector_size : vector_size + shared_size]
        .reshape(parts, -1, shared_part)
        .transpose(1, 0, 2)
        .reshape(-1, parts * shared_part)
        .astype(f32)
    )
    rounds = jnp.max(small[:, vector_size + shared_size].astype(f32)).astype(jnp.int32)

    per_part = -(-(LAYERS * (vectors.shape[2] * parts // half) + 2 * shared.shape[0]) // parts)
    width = -(-(SLOTS + share + per_part) // 16) * 16

    def choose(start):
        return pick(asked_slots, start, width)

    def serve(chosen):
        return jnp.einsum("sjr,rc->sjc", chosen, table_low, preferred_element_type=f32).astype(bf16)

    def places_of(start):
        place = token_slot - start
        fits = (high >= 0) & (place >= 0) & (place < SLOTS)
        return jnp.where(fits, owner * width + place.astype(jnp.int32), -1)

    def spread(start):
        return (places_of(start)[:, None] == jnp.arange(parts * width)[None, :]).astype(bf16)

    places_first = places_of(0.0)
    place_at = jnp.arange(length)
    places_first = jnp.concatenate(
        [places_first, place_at // share * width + SLOTS + place_at % share]
    )
    place_rows = places_first[: tokens.shape[0]].reshape(-1, 1, length)
    place_columns = places_first[:, None]

    sent = jnp.concatenate(
        [
            serve(choose(0.0))[:, :SLOTS],
            jnp.broadcast_to(place_share[None], (parts, share, half)),
            jnp.zeros((parts, width - SLOTS - share, half), bf16),
        ],
        axis=1,
    )
    if known:
        sent, down_three, up_three, *near_one = lax.optimization_barrier(
            (sent, down_three, up_three) + near_one
        )
        far_one = gather_far(links, *near_one)
        later_two = pick_at(down_three, down_two, down_one, down_own)
        near_two = gather_near(links, later_two)
    fetched = lax.all_to_all(sent, "blk", 0, 0)
    if known:
        place_columns, place_rows, far_two, near_two = lax.optimization_barrier(
            (place_columns, place_rows, far_one, near_two)
        )
        far_one = far_two
        far_two = gather_far(links, *near_two)
    halves = expand(tall_rows(place_columns), place_columns, fetched.reshape(-1, half))

    def fetch_more(carry):
        done, total = carry
        start = (done * SLOTS).astype(f32)
        more = lax.all_to_all(serve(choose(start)), "blk", 0, 0).reshape(-1, half)
        more = jnp.dot(spread(start), more, preferred_element_type=f32).astype(bf16)
        return done + 1, total.at[: tokens.shape[0]].add(more)

    if known:
        halves, *far_two = lax.optimization_barrier((halves,) + far_two)
        layer_groups = [
            None, (later_one, *near_one, *far_one, later_two, *near_two, *far_two)
        ]
        orders = [0, 1]
        early_one = pick_at(own_groups, own_groups, up_one, up_two)
        early_two = pick_at(up_own, up_one, up_two, up_three)
    halves = lax.while_loop(lambda c: c[0] < rounds, fetch_more, (jnp.int32(1), halves))[1]
    others = other_core(halves)
    embed_params = params_all[:2]
    q_blocks, p_blocks = q_tokens.size // length, p_tokens.size // length

    def first_half(layer, seg, first, count, lengths):
        bias = bias_all[layer : layer + 1]
        params = params_all[2 + 6 * layer : 8 + 6 * layer]
        return [layer, seg, lengths, bias, params] + list(attention_forward(
            layer, seg, length, count, first, lengths, spot, halves, others,
            layer_groups[layer], orders[layer], bias, embed_params,
        ))

    def second_half(kept):
        layer, seg, lengths, bias, params, state, qkv, context, logs, own_one = kept
        other_one = other_core(own_one)
        return kept + [other_one] + list(ffn_forward(
            layer, tall_rows(state), spot, state, own_one, other_one, layer_groups[layer],
            orders[layer], bias, params,
        ))

    def pool_of(kept):
        layer, seg, lengths, _, params = kept[:5]
        hidden, _, _, own_two = kept[11:]
        other_two = other_core(own_two)
        kept.append(other_two)
        return pool_forward(layer, seg, tall_rows(hidden), lengths, hidden, own_two, other_two, params)

    if known:
        near_one = gather_near(links, early_one)
    p_kept = first_half(1, length, q_blocks, p_blocks, p_lengths)
    if known:
        p_kept[-1], *near_one = lax.optimization_barrier((p_kept[-1],) + near_one)
        far_one = gather_far(links, *near_one)
        near_two = gather_near(links, early_two)
    p_kept = second_half(p_kept)
    if known:
        p_kept[-1], *four = lax.optimization_barrier((p_kept[-1],) + far_one + near_two)
        far_one, near_two = four[:2], four[2:]
        far_two = gather_far(links, *near_two)
    p_pooled = pool_of(p_kept)
    if known:
        p_pooled, *far_two = lax.optimization_barrier((p_pooled,) + far_two)
        layer_groups[0] = (early_one, *near_one, *far_one, early_two, *near_two, *far_two)
    q_kept = second_half(first_half(0, q_length, 0, q_blocks, q_lengths))
    codes_local = jnp.tanh(p_pooled)
    codes_low = codes_local.astype(bf16)
    codes = to_all(codes_low, parts)
    q_kept[-1], codes = lax.optimization_barrier((q_kept[-1], codes))
    pooled = [pool_of(q_kept), p_pooled]
    asked_local = pooled[0]
    codes = codes.reshape(-1, MODEL_WIDTH).astype(f32)
    every = to_all(
        jnp.concatenate(
            [
                asked_local,
                jnp.pad(positive.astype(f32)[None], ((0, 0), (0, MODEL_WIDTH - positive.shape[0]))),
            ]
        ),
        parts,
    )
    q_part, p_part = asked_local.shape[0], codes_local.shape[0]
    asked = every[:, :q_part].reshape(-1, MODEL_WIDTH)
    positives = every[:, q_part, :q_part].reshape(-1).astype(jnp.int32)
    loss_sum, positives_count, d_asked, d_codes = loss_and_back(asked, codes, positives[:, None])
    d_asked = lax.dynamic_slice_in_dim(d_asked, me * q_part, q_part, 0)
    d_codes = lax.dynamic_slice_in_dim(d_codes, me * p_part, p_part, 0)
    d_passages = d_codes * (1.0 - codes_local * codes_local)
    def ffn_back(kept, d_pooled, sets):
        (layer, seg, lengths, bias, params, state, qkv, context, logs, own_one, other_one, hidden,
         active, slope, own_two, other_two) = kept
        return ffn_backward(
            layer, seg, tall_rows(hidden), lengths, spot, d_pooled, hidden, own_two, other_two, active, slope,
            layer_groups[layer], orders[layer], params, sets,
        )

    def attention_back(kept, base, back_own, back_other, first, count, **more):
        (layer, seg, lengths, bias, params, state, qkv, context, logs, own_one, other_one) = kept[:11]
        return attention_backward(
            layer, seg, length, first, count, lengths[first:] if first else lengths, spot, base,
            back_own, back_other, state, own_one, other_one, qkv, context, logs,
            layer_groups[layer], orders[layer], params, **more,
        )

    q_base, q_back, q_ffn_sums, q_up_bias, *q_ffn = ffn_back(
        q_kept, d_asked, ((0, 1),) if known else None
    )
    q_state, q_state_own, q_sums, q_bias, *q_attention = attention_back(
        q_kept, q_base, q_back, other_core(q_back), 0, q_blocks,
        **(dict(planes=(0, 1), buffers=q_ffn) if known else {}),
    )
    p_base, p_back, p_ffn_sums, p_up_bias, *p_ffn = ffn_back(
        p_kept, after(d_passages, q_sums), ((0,), (1,)) if known else None
    )
    if known:
        early = p_blocks // 2
        q_first = plane_first(links, *q_attention)
        top_first = plane_first(links, *p_ffn[4:])
        p_back, *q_first = lax.optimization_barrier((p_back,) + q_first)
        p_back_other = other_core(p_back)
        q_second = plane_second(links, *q_first)
        state_one, own_one, *carry = attention_back(
            p_kept, p_base, p_back, p_back_other, 0, early, carry_out=True
        )
        carry = carry[2:] + carry[:2]
        other_one = other_core(own_one)
        carry[2], *eight = lax.optimization_barrier((carry[2],) + q_second + top_first)
        q_planes = plane_total(*eight[:4])
        top_second = plane_second(links, *eight[4:])
        down = column_start(links, q_planes[0], [(3, 2)])
        state_two, own_two, p_sums, p_bias, *low = attention_back(
            p_kept, p_base, p_back, p_back_other, early, p_blocks - early, carry=carry,
            planes=(0,), buffers=p_ffn[:4],
        )
        own_two, down, *top_second = lax.optimization_barrier((own_two, down) + top_second)
        top_plane = plane_total(*top_second)[0]
        other_two = other_core(own_two)
        up = column_start(links, top_plane, [(0, 1)])
        down = column_step(
            links, links.z == 3, q_planes[1], add(q_planes[0], down), [(3, 2), (2, 1)]
        )
        low_first = plane_first(links, *low)
        state_p = ((state_one, state_two), (own_one, own_two), (other_one, other_two))
        low_first = plane_first(links, *low)
    else:
        p_back_other = other_core(p_back)
        state_one, own_one, p_sums, p_bias, *p_attention = attention_back(
            p_kept, p_base, p_back, p_back_other, 0, p_blocks
        )
        state_p = ((state_one,), (own_one,), (other_core(own_one),))
    smalls = (
        q_bias, q_up_bias, p_bias, p_up_bias, q_sums, q_ffn_sums, p_sums, p_ffn_sums
    )
    vector_rows = LAYERS * vector_part * parts // half
    state_parts = [
        (q_state, q_state_own, other_core(q_state_own)),
        state_p,
    ]
    picked, _ = embed_backward(
        (q_length, length), length, state_parts[0], state_parts[1], smalls, halves, others, place_rows,
        spot, embed_params, parts, width,
    )
    if known:
        picked, up, down, *low_first = lax.optimization_barrier((picked, up, down) + low_first)

    def gather_up(start):
        return embed_backward(
            (q_length, length), length, state_parts[0], state_parts[1], smalls, halves, others,
            places_of(start).reshape(-1, 1, length), spot, embed_params, parts, width,
        )[0].reshape(parts, width, half)

    def put_back(chosen, received):
        return jnp.einsum("sjr,sjc->rc", chosen, received, preferred_element_type=f32)[:rows_here]

    sent = picked.reshape(parts, width, half)
    got = lax.all_to_all(sent, "blk", 0, 0)
    token_grad = put_back(choose(0.0), got)

    def send_more(carry):
        done, total = carry
        start = (done * SLOTS).astype(f32)
        more = lax.all_to_all(gather_up(start), "blk", 0, 0)
        return done + 1, total + put_back(choose(start), more)

    token_grad = lax.while_loop(lambda c: c[0] < rounds, send_more, (jnp.int32(1), token_grad))[1]
    rest = jnp.sum(got[:, SLOTS : SLOTS + share + per_part].astype(f32), axis=0)
    if known:
        low_plane = plane_total(*plane_second(links, *low_first))[0]
        z = links.z
        planes = [q_planes[0], q_planes[1], low_plane, top_plane]
        up = column_step(links, z == 0, low_plane, add(top_plane, up), [(0, 1), (1, 2)])
        down = column_step(
            links, z == 3, low_plane, add(jnp.where(z == 2, q_planes[1], q_planes[0]), down),
            [(3, 2), (2, 1), (1, 0)],
        )
        base = lax.optimization_barrier(
            jnp.where(z == 0, q_planes[1], jnp.where(z == 1, low_plane, top_plane))
        )
        up = links.over_z(
            (base + jnp.where(z == 0, 0.0, up.astype(f32))).astype(bf16),
            [(0, 1), (1, 2), (2, 3)],
        )
        grad_parts = (own_column(links, planes), up, down)
    else:
        all_groups = jnp.concatenate(q_attention + q_ffn + p_attention + p_ffn, axis=0)
        if not even:
            all_groups = split_pairs(all_groups)
        grad_parts = (lax.psum_scatter(all_groups, "blk", scatter_dimension=0, tiled=True),)
    inverse = 1.0 / positives_count
    rest = rest * inverse
    row_index = me * per_part + jnp.arange(per_part)
    counted = ((row_index < vector_rows) | (core == 0)).astype(f32)
    squares = (
        jnp.sum(rest[:share] ** 2)
        + jnp.sum(rest[share:] ** 2 * counted[:, None])
        + jnp.sum((token_grad * inverse) ** 2)
    )
    rest = to_all(rest, parts)
    if known:
        squares, *grad_parts = lax.optimization_barrier((squares,) + grad_parts)
    scaled, square, turned, row_square, block_squares = block_products(
        even, grad_parts, inverse[None], left_roots, right_roots
    )
    block_squares, rest = lax.optimization_barrier((block_squares, rest))
    place_grads = rest[:, :share].reshape(length, half)
    small_grads = rest[:, share:].reshape(-1, half)
    grad_vectors = lax.dynamic_slice_in_dim(
        small_grads[:vector_rows].reshape(LAYERS, -1), me * vector_part, vector_part, 1
    )[None]
    shared_rows = shared.shape[0]
    grad_shared = lax.dynamic_slice_in_dim(
        jnp.concatenate(
            [
                small_grads[vector_rows : vector_rows + shared_rows],
                small_grads[vector_rows + shared_rows : vector_rows + 2 * shared_rows],
            ],
            axis=1,
        ),
        me * shared_part,
        shared_part,
        1,
    )
    margin = jnp.zeros((rows_here, half), f32)
    place_grads = lax.dynamic_slice_in_dim(
        jnp.concatenate([margin, place_grads, margin]),
        jnp.clip(me * rows_here - VOCAB + rows_here, 0, rows_here + length),
        rows_here,
        0,
    )
    table_grad = token_grad * inverse + place_grads
    squares = squares + jnp.sum(block_squares[0])
    devices = parts * 2
    squares = lax.all_to_all(
        jnp.broadcast_to(squares, (devices, 8, LANES)), ("blk", "tp"), 0, 0
    )
    squares = jnp.sum(squares[:, 0, 0])
    grad_norm = jnp.sqrt(squares)
    factor = jnp.minimum(1.0, CLIP / grad_norm)
    block_grads, left_new, right_new, blocks_new = block_update(
        factor[None], scaled, square, row_square, turned, left_stats, right_stats, blocks
    )
    table_moment_new, table_second_new, table_new = adamw(
        table, table_moment, table_second, table_grad * factor
    )
    vector_moment_new, vector_second_new, vectors_new = adamw(
        vectors, vector_moment, vector_second, grad_vectors * factor
    )
    shared_moment_new, shared_second_new, shared_new = adamw(
        shared, shared_moment, shared_second, grad_shared * factor
    )
    return (
        loss_sum,
        positives_count,
        grad_norm,
        block_grads,
        left_new,
        right_new,
        blocks_new,
        table_moment_new,
        table_second_new,
        table_new,
        vector_moment_new,
        vector_second_new,
        vectors_new,
        shared_moment_new,
        shared_second_new,
        shared_new,
    )


def solution(mesh):
    return jax.shard_map(
        on_device,
        mesh=mesh,
        in_specs=(
            P("blk", None),
            P("blk", None),
            P("blk"),
            P("blk"),
            P("blk"),
            P("blk", "tp"),
            P("blk", "tp"),
            P("blk", "tp"),
            P("tp", "blk", None, None),
            P("tp", "blk", None, None),
            P("tp", "blk", None, None),
            P("tp", "blk", None, None),
            P("tp", "blk", None, None),
            P("tp", None, "blk"),
            P("tp", None, "blk"),
            P("tp", None, "blk"),
            P(None, "blk"),
            P(None, "blk"),
            P(None, "blk"),
        ),
        out_specs=(
            P(),
            P(),
            P(),
            P("tp", "blk", None, None),
            P("tp", "blk", None, None),
            P("tp", "blk", None, None),
            P("tp", "blk", None, None),
            P("blk", "tp"),
            P("blk", "tp"),
            P("blk", "tp"),
            P("tp", None, "blk"),
            P("tp", None, "blk"),
            P("tp", None, "blk"),
            P(None, "blk"),
            P(None, "blk"),
            P(None, "blk"),
        ),
        check_vma=False,
    )
```
